32 devices in a mesh: dp: 8 (over y, x, core), fsdp: 4 (over z).
Axes of the slice: x: 2, y: 2, z: 4, core: 2. Of those that a mesh axis runs over, the one named last changes fastest.
Arguments:
- tokens: bfloat16 [8192, 800], P(('dp', 'fsdp')), may hold values from -6 to 6
- cotangent: bfloat16 [8192, 800], P(('dp', 'fsdp')), may hold values from -6 to 6
- lengths: int32 [32, 8], P(('dp', 'fsdp')), may hold values from 1 to 192, 256 in all within a row
- dilation: int32 [2], replicated, may hold values from 1 to 8, as said below
- proj_in: float32 [2, 800, 400], P(None, 'fsdp'), may hold values from -0.21875 to 0.21875
- conv_weight: float32 [400, 3200], P('fsdp'), may hold values from -0.15625 to 0.15625
- proj_out: float32 [2, 400, 800], P(None, 'fsdp'), may hold values from -0.3125 to 0.3125
- vec_wide: float32 [2, 3, 800], P(None, None, 'fsdp'), may hold values from -1.2 to 1.6
- vec_narrow: float32 [2, 6, 400], P(None, None, 'fsdp'), may hold values from -1.2 to 1.6
- mom_in: float32 [2, 800, 400], P(None, 'fsdp'), may hold values from -160 to 160
- mom_conv: float32 [400, 3200], P('fsdp'), may hold values from -160 to 160
- mom_out: float32 [2, 400, 800], P(None, 'fsdp'), may hold values from -160 to 160
- mom_wide: float32 [2, 3, 800], P(None, None, 'fsdp'), may hold values from -160 to 160
- mom_narrow: float32 [2, 6, 400], P(None, None, 'fsdp'), may hold values from -160 to 160
Outputs:
- out_tokens: bfloat16 [8192, 800], P(('dp', 'fsdp'))
- grad_tokens: float32 [8192, 800], P(('dp', 'fsdp'))
- new_mom_in: float32 [2, 800, 400], P(None, 'fsdp')
- new_mom_conv: float32 [400, 3200], P('fsdp')
- new_mom_out: float32 [2, 400, 800], P(None, 'fsdp')
- new_mom_wide: float32 [2, 3, 800], P(None, None, 'fsdp')
- new_mom_narrow: float32 [2, 6, 400], P(None, None, 'fsdp')
- new_proj_in: float32 [2, 800, 400], P(None, 'fsdp')
- new_conv: float32 [400, 3200], P('fsdp')
- new_proj_out: float32 [2, 400, 800], P(None, 'fsdp')
- new_vec_wide: float32 [2, 3, 800], P(None, None, 'fsdp')
- new_vec_narrow: float32 [2, 6, 400], P(None, None, 'fsdp')
- low_proj_in: bfloat16 [2, 800, 400], P(None, 'fsdp')
- low_conv: bfloat16 [400, 3200], P('fsdp')
- low_proj_out: bfloat16 [2, 400, 800], P(None, 'fsdp')
The draws below stay inside these ranges and needn't reach their ends.
Inputs may be any that keep to these rules, and one draw needn't show every extreme that they name: `lengths`: row r holds the sentences of the r-th device in order and sums to 256; each row has one sentence of exactly 192 characters. `dilation`: one of the two rates is exactly 8.
All inputs are finite; a program needn't handle non-finite values.
Results may differ from the reference program's by a relative error of at most 0.017.
Values may be sent and summed in bfloat16 or wider, within the bound.
A program may use at most 192 MiB of HBM per device.

```python
import math
import jax
import jax.numpy as jnp
import numpy as np
from jax import lax

D = 800
H = 400
K_ENC = 5
K_DEC = 3
MAX_DILATION = 8
NS_STEPS = 5
SEQ_DEV = 8
TOK_DEV = 256
TOKEN_TOTAL = 8192
N_DP = 8
N_FSDP = 4


def mixed_vectors(key, full_shape, gain_rows):
    gain_key, shift_key = jax.random.split(key)
    gains = jnp.exp(jax.random.uniform(gain_key, full_shape, jnp.float32, math.log(0.6), math.log(1.6)))
    shifts = 0.3 * jnp.clip(jax.random.normal(shift_key, full_shape, jnp.float32), -4.0, 4.0)
    row_ids = jnp.arange(full_shape[1])
    is_gain = row_ids < 0
    for gain_row in gain_rows:
        is_gain = is_gain | (row_ids == gain_row)
    return jnp.where(is_gain[None, :, None], gains, shifts).astype(jnp.float32)


def draw_vec_wide(key, part):
    key = jax.random.fold_in(key, 11)
    return mixed_vectors(key, (2, 3, D), [0])


def draw_vec_narrow(key, part):
    key = jax.random.fold_in(key, 13)
    return mixed_vectors(key, (2, 6, H), [1, 4])


def draw_dilation(key, part):
    key = jax.random.fold_in(key, 7)
    dilation_key, order_key = jax.random.split(key)
    reduced_rate = jax.random.randint(dilation_key, (), 1, MAX_DILATION)
    order_bit = jax.random.randint(order_key, (), 0, 2)
    highest_rate = jnp.int32(MAX_DILATION)
    return jnp.where(order_bit == 1, jnp.stack([highest_rate, reduced_rate]), jnp.stack([reduced_rate, highest_rate])).astype(jnp.int32)


def steps_of(stream_key, extent, cuts, low, largest):
    gain, own = 1.0, jax.random.fold_in(stream_key, 6)
    for axis_at, parts in cuts:
        heights = jnp.exp(jax.random.uniform(jax.random.fold_in(own, axis_at), (parts,), jnp.float32, low / len(cuts), largest / len(cuts)))
        gain = gain * jnp.repeat(heights, extent[axis_at] // parts).reshape([-1 if axis == axis_at else 1 for axis in range(len(extent))])
    return gain


def profile(amount, total, reach, slope):
    loads = [(1 << 20) // math.isqrt(grade ** slope) + 1 for grade in range(2, amount + 1)]
    rest, counts = total - reach - (amount - 1), [1] * (amount - 1)
    while rest > 0:
        free = [i for i in range(amount - 1) if counts[i] < reach]
        mass, remaining = sum([loads[i] for i in free]), rest
        for i in free:
            addition = min(reach - counts[i], max(1, remaining * loads[i] // mass), rest)
            counts[i] = counts[i] + addition
            rest = rest - addition
    return np.array([reach] + counts)


def uneven(own_key, number_of, total, limit, lean):
    if number_of == 2:
        one = jax.random.randint(own_key, (), max(1, total - limit), min(limit, total - 1) + 1)
        return jnp.stack([one, total - one])
    sizes = jnp.asarray(profile(number_of, total, limit, lean), jnp.int32)
    twos = (number_of - 1) // 2
    donor, sink = sizes[1:1 + 2 * twos:2], sizes[2:2 + 2 * twos:2]
    slack = jnp.minimum(donor - 1, limit - sink)
    passed = jax.random.randint(jax.random.fold_in(own_key, 1), (twos,), 0, 1 << 20) % (slack + 1)
    sizes = sizes.at[1:1 + 2 * twos:2].set(donor - passed).at[2:2 + 2 * twos:2].set(sink + passed)
    return sizes[jax.random.permutation(jax.random.fold_in(own_key, 2), number_of)]


def gaussian(stream_key, shape, scale, most, cuts=(), kind=jnp.bfloat16):
    values = scale * jax.random.normal(stream_key, shape, jnp.float32)
    if cuts:
        values = values * steps_of(stream_key, shape, cuts, -0.22, 0.18)
    return jnp.clip(values, -most, most).astype(kind)


def setup_inputs(seed: int = 0) -> dict:
    key_of = jax.random.split(jax.random.key(seed), 15)
    tokens = gaussian(key_of[0], (TOKEN_TOTAL, D), 1.0, 6.0, ((0, 32),))
    cotangent = gaussian(key_of[1], (TOKEN_TOTAL, D), 1.0, 6.0, ((0, 32),))
    lengths = jax.vmap(lambda own: uneven(own, SEQ_DEV, TOK_DEV, TOK_DEV - 8 * SEQ_DEV, 2))(jax.random.split(key_of[2], (N_DP * N_FSDP))).reshape((N_DP * N_FSDP, SEQ_DEV)).astype(jnp.int32)
    dilation = draw_dilation(jax.random.fold_in(key_of[14], 71), 0)
    proj_in = gaussian(key_of[4], (2, D, H), D ** -0.5, 0.21875, ((1, 4),), jnp.float32)
    conv_weight = gaussian(key_of[5], (H, (K_ENC + K_DEC) * H), (4 * H) ** -0.5, 0.15625, ((0, 4),), jnp.float32)
    proj_out = gaussian(key_of[6], (2, H, D), H ** -0.5, 0.3125, ((1, 4),), jnp.float32)
    vec_wide = draw_vec_wide(jax.random.fold_in(key_of[14], 71), 0)
    vec_narrow = draw_vec_narrow(jax.random.fold_in(key_of[14], 71), 0)
    mom_in = gaussian(key_of[9], (2, D, H), (0.3 * (TOK_DEV * N_DP * N_FSDP) ** 0.5), 160.0, ((1, 4),), jnp.float32)
    mom_conv = gaussian(key_of[10], (H, (K_ENC + K_DEC) * H), (0.3 * (TOK_DEV * N_DP * N_FSDP) ** 0.5), 160.0, ((0, 4),), jnp.float32)
    mom_out = gaussian(key_of[11], (2, H, D), (0.3 * (TOK_DEV * N_DP * N_FSDP) ** 0.5), 160.0, ((1, 4),), jnp.float32)
    mom_wide = gaussian(key_of[12], (2, 3, D), (0.3 * (TOK_DEV * N_DP * N_FSDP) ** 0.5), 160.0, ((2, 4),), jnp.float32)
    mom_narrow = gaussian(key_of[13], (2, 6, H), (0.3 * (TOK_DEV * N_DP * N_FSDP) ** 0.5), 160.0, ((2, 4),), jnp.float32)
    return dict(tokens=tokens, cotangent=cotangent, lengths=lengths, dilation=dilation, proj_in=proj_in, conv_weight=conv_weight, proj_out=proj_out, vec_wide=vec_wide, vec_narrow=vec_narrow, mom_in=mom_in, mom_conv=mom_conv, mom_out=mom_out, mom_wide=mom_wide, mom_narrow=mom_narrow)


@jax.custom_vjp
def low(v):
    return lax.optimization_barrier(v.astype(jnp.bfloat16)).astype(jnp.float32)

@jax.custom_vjp
def low_back(v):
    return v

def low_keep(v):
    return (low(v), None)

def low_pass(kept, grad):
    return (grad,)

def back_keep(v):
    return (v, None)

def back_low(kept, grad):
    return (low(grad),)
low.defvjp(low_keep, low_pass)
low_back.defvjp(back_keep, back_low)
EPSILON = 1e-05
NORM_FLOOR = 1e-07
COEF_A = 3.4445
COEF_B = -4.775
COEF_C = 2.0315
MOMENT_DECAY = 0.5
MATRIX_RATE = 0.5
VECTOR_RATE = 0.1
PRECISE = lax.Precision.HIGHEST

def layer_norm(values, gain_row, offset):
    center = values - lax.optimization_barrier(jnp.mean(values, axis=-1, keepdims=True))
    spread = lax.optimization_barrier(jnp.mean(center * center, axis=-1, keepdims=True))
    return center * lax.rsqrt(spread + EPSILON) * gain_row + offset

def norm_gelu(values, gain_row, offset):
    return jax.nn.gelu(layer_norm(values, gain_row, offset), approximate=True)

def segment_ids(lengths_row, count_rows):
    seq_ends = jnp.cumsum(lengths_row).astype(jnp.int32)
    places = jnp.arange(count_rows, dtype=jnp.int32)
    return lax.optimization_barrier(jnp.sum((places[:, None] >= seq_ends[None, :]).astype(jnp.int32), axis=1))

def shifted(values, segment, offset, receptive_rows):
    count_rows = values.shape[0]
    padded = jnp.pad(values, ((receptive_rows, receptive_rows), (0, 0)))
    padded_seg = jnp.pad(segment, (receptive_rows, receptive_rows), constant_values=-1)
    first_index = (offset + receptive_rows).astype(jnp.int32)
    moved = lax.dynamic_slice_in_dim(padded, first_index, count_rows, 0)
    moved_seg = lax.dynamic_slice_in_dim(padded_seg, first_index, count_rows, 0)
    return jnp.where((moved_seg == segment)[:, None], moved, jnp.zeros((), values.dtype))

def orthogonalize(matrix):
    flipped = matrix.shape[0] > matrix.shape[1]
    current = matrix.T if flipped else matrix
    current = current / (jnp.sqrt(jnp.sum(current * current)) + NORM_FLOOR)
    for unused in range(NS_STEPS):
        gram_matrix = jnp.dot(current, current.T, precision=PRECISE)
        polynomial = COEF_B * gram_matrix + COEF_C * jnp.dot(gram_matrix, gram_matrix, precision=PRECISE)
        current = COEF_A * current + jnp.dot(polynomial, current, precision=PRECISE)
    return current.T if flipped else current

def step_scale(row_count, col_count, fan_count):
    return math.sqrt(max(row_count, col_count) / fan_count)

def conv_block(inputs, w_in, w_conv, w_out, wide_vec, narrow_vec, segment, offsets, receptive_rows):
    first_act = low(norm_gelu(inputs, wide_vec[0], wide_vec[1]))
    hidden = low_back(jnp.dot(first_act, w_in, precision=PRECISE)) + narrow_vec[0]
    second_act = low(norm_gelu(hidden, narrow_vec[1], narrow_vec[2]))
    tap_products = jnp.dot(second_act, w_conv, precision=PRECISE)
    inner_width = w_in.shape[1]
    conv_sum = shifted(tap_products[:, :inner_width], segment, offsets[0], receptive_rows)
    for j in range(1, len(offsets)):
        conv_sum = conv_sum + shifted(tap_products[:, j * inner_width:(j + 1) * inner_width], segment, offsets[j], receptive_rows)
    conv_sum = low_back(conv_sum) + narrow_vec[3]
    third_act = low(norm_gelu(conv_sum, narrow_vec[4], narrow_vec[5]))
    return inputs + low_back(jnp.dot(third_act, w_out, precision=PRECISE)) + wide_vec[2]

def reference(tokens, cotangent, lengths, dilation, proj_in, conv_weight, proj_out, vec_wide, vec_narrow, mom_in, mom_conv, mom_out, mom_wide, mom_narrow):
    masters = (proj_in, conv_weight, proj_out, vec_wide, vec_narrow)
    params = tuple((p.astype(jnp.bfloat16).astype(jnp.float32) for p in masters))
    row_total = N_DP * N_FSDP
    token_rows = tokens.reshape(row_total, TOK_DEV, D)
    cot_rows = cotangent.reshape(row_total, TOK_DEV, D)
    receptive_rows = 2 * MAX_DILATION
    split_col = K_ENC * H
    enc_offsets = [(j - K_ENC // 2) * dilation[0] for j in range(K_ENC)]
    dec_offsets = [-j * dilation[1] for j in range(K_DEC)]

    def forward(inputs, weights, segment):
        w_in, w_conv, w_out, wide_all, narrow_all = weights
        hidden = conv_block(inputs, w_in[0], w_conv[:, :split_col], w_out[0], wide_all[0], narrow_all[0], segment, enc_offsets, receptive_rows)
        return conv_block(hidden, w_in[1], w_conv[:, split_col:], w_out[1], wide_all[1], narrow_all[1], segment, dec_offsets, receptive_rows)

    def one_row(totals, item):
        token_row, cot_row, lengths_row = item
        segment = segment_ids(lengths_row, TOK_DEV)
        result, pullback = jax.vjp(lambda inputs, weights: forward(inputs, weights, segment), token_row.astype(jnp.float32), params)
        grad_row, grad_weights = pullback(cot_row.astype(jnp.float32))
        totals = tuple((a + g for a, g in zip(totals, grad_weights)))
        return (totals, (result.astype(jnp.bfloat16), grad_row))
    initial = tuple((jnp.zeros_like(p) for p in params))
    grads, (out_rows, grad_rows) = lax.scan(one_row, initial, (token_rows, cot_rows, lengths))
    olds = (mom_in, mom_conv, mom_out, mom_wide, mom_narrow)
    new_mom_in, new_mom_conv, new_mom_out, new_mom_wide, new_mom_narrow = tuple((MOMENT_DECAY * old_state + grad_sum for old_state, grad_sum in zip(olds, grads)))
    step_in = jnp.stack([orthogonalize(new_mom_in[b]) * step_scale(D, H, D) for b in range(2)])
    step_conv = jnp.concatenate([orthogonalize(new_mom_conv[:, :split_col]) * step_scale(H, K_ENC * H, K_ENC * H), orthogonalize(new_mom_conv[:, split_col:]) * step_scale(H, K_DEC * H, K_DEC * H)], axis=1)
    step_out = jnp.stack([orthogonalize(new_mom_out[b]) * step_scale(H, D, H) for b in range(2)])
    new_proj_in = proj_in - MATRIX_RATE * step_in
    new_conv = conv_weight - MATRIX_RATE * step_conv
    new_proj_out = proj_out - MATRIX_RATE * step_out
    vector_step = VECTOR_RATE / math.sqrt(row_total * TOK_DEV)
    new_vec_wide = vec_wide - vector_step * new_mom_wide
    new_vec_narrow = vec_narrow - vector_step * new_mom_narrow
    return (out_rows.reshape(row_total * TOK_DEV, D), grad_rows.reshape(row_total * TOK_DEV, D), new_mom_in, new_mom_conv, new_mom_out, new_mom_wide, new_mom_narrow, new_proj_in, new_conv, new_proj_out, new_vec_wide, new_vec_narrow, new_proj_in.astype(jnp.bfloat16), new_conv.astype(jnp.bfloat16), new_proj_out.astype(jnp.bfloat16))
```

```python
import functools
import math

import jax
import jax.numpy as jnp
from jax import lax
from jax.experimental import pallas as pl
from jax.experimental.pallas import tpu as pltpu
from jax.sharding import PartitionSpec as P

D = 800
H = 400
K_ENC = 5
K_DEC = 3
NS_STEPS = 5
EPSILON = 1e-05
NORM_FLOOR = 1e-07
COEF_A = 3.4445
COEF_B = -4.775
COEF_C = 2.0315
MOMENT_DECAY = 0.5
MATRIX_RATE = 0.5
VECTOR_RATE = 0.1

F32 = jnp.float32
BF16 = jnp.bfloat16
MESH = pl.DeviceIdType.MESH

OWNERS = 4
PIECES = 8
SHARD = 100
ROWS = 112
PIECE = 896
COLS = PIECES * PIECE
WO_AT = (0, 896)
CONV_AT = 1792
WI_AT = ((4992, 5504), (6016, 6528))
VEC_AT = 7040
SPLIT = K_ENC * H
TOK = 256
GROUPED = OWNERS * ROWS

GELU_K = math.sqrt(2.0 / math.pi)
GELU_C = 0.044715


def vmem(shape, dtype):
    return pltpu.VMEM(shape, dtype)


def dot(a, b):
    return lax.dot_general(a, b, (((1,), (0,)), ((), ())), preferred_element_type=F32)


def dot_nt(a, b):
    return lax.dot_general(a, b, (((1,), (1,)), ((), ())), preferred_element_type=F32)


def dot_tn(a, b):
    return lax.dot_general(a, b, (((0,), (0,)), ((), ())), preferred_element_type=F32)


def one_hot(mask):
    return jnp.where(mask, 1.0, 0.0).astype(BF16)


def pack(slab, conv, w_in, w_out, wide, narrow):
    slab[...] = jnp.zeros((ROWS, COLS), BF16)
    slab[:SHARD, CONV_AT : CONV_AT + 3200] = conv[...].astype(BF16)
    for b in range(2):
        slab[:SHARD, WO_AT[b] : WO_AT[b] + D] = w_out[b].astype(BF16)
        for h in range(2):
            at = WI_AT[b][h]
            slab[:SHARD, at : at + H] = w_in[b, h * SHARD : (h + 1) * SHARD, :].astype(BF16)
    for b in range(2):
        for k in range(6):
            m = 6 * b + k
            slab[m : m + 1, VEC_AT : VEC_AT + SHARD] = narrow[b, k : k + 1, :].astype(BF16)
        for k in range(3):
            for h in range(2):
                m = 16 + 16 * h + 3 * b + k
                part = wide[b, k : k + 1, h * SHARD : (h + 1) * SHARD]
                slab[m : m + 1, VEC_AT : VEC_AT + SHARD] = part.astype(BF16)


def place():
    at = lax.axis_index("dp")
    piece = at % PIECES
    return at - piece, piece, lax.axis_index("fsdp")


def flip(value, bit):
    return value + bit - 2 * bit * ((value // bit) % 2)


def other_owner(own, step):
    if step == 3:
        return 3 - own
    return flip(own, step)


def columns(piece):
    return pl.ds(pl.multiple_of(piece * PIECE, PIECE), PIECE)


def remote(src, dst, send, recv, device):
    return pltpu.make_async_remote_copy(
        src_ref=src,
        dst_ref=dst,
        send_sem=send,
        recv_sem=recv,
        device_id=device,
        device_id_type=MESH,
    )


def greet(devices):
    barrier = pltpu.get_barrier_semaphore()
    for device in devices:
        pl.semaphore_signal(barrier, inc=1, device_id=device, device_id_type=MESH)
    return barrier


class Gather:
    SEMS = 10

    def __init__(self, view, send, recv, at):
        base, piece, own = place()
        self.view, self.send, self.recv, self.at = view, send, recv, at
        self.piece = piece
        self.near = {bit: (base + flip(piece, bit), own) for bit in (1, 2, 4)}
        self.started = []

    def copy(self, bit, q, part, k):
        ref = self.view(q, part)
        sems = (self.send.at[self.at + k], self.recv.at[self.at + k])
        return remote(ref, ref, sems[0], sems[1], self.near[bit])

    def start(self, bit, q, part, k):
        copy = self.copy(bit, q, part, k)
        copy.start()
        self.started.append(copy)

    def first(self):
        p = self.piece
        self.start(4, p, 0, 0)
        self.start(2, p, 1, 1)

    def second(self):
        p = self.piece
        for k in (0, 1):
            self.started[k].wait_recv()
        self.start(2, p, 0, 2)
        self.start(2, flip(p, 4), 0, 3)
        self.start(4, p, 1, 4)
        self.start(4, flip(p, 2), 1, 5)
        self.start(1, p, None, 6)

    def third(self):
        p = self.piece
        for k in (2, 3, 4, 5):
            self.started[k].wait_recv()
        self.start(1, flip(p, 2), None, 7)
        self.start(1, flip(p, 4), None, 8)
        self.start(1, flip(flip(p, 2), 4), None, 9)

    def last(self):
        for k in (6, 7, 8, 9):
            self.started[k].wait_recv()

    def finish(self):
        for copy in self.started:
            copy.wait_send()


def part_rows(part):
    if part is None:
        return pl.ds(0, ROWS)
    return pl.ds(0, 64) if part == 0 else pl.ds(64, 48)


def gather_kernel(conv, w_in, w_out, wide, narrow, full, z_send, z_recv, send, recv):
    base, piece, own = place()
    me = base + piece
    near = [(base + flip(piece, bit), own) for bit in (1, 2, 4)]
    column = [(me, other_owner(own, step)) for step in (1, 2, 3)]
    barrier = greet(near + column)
    pack(full.at[own], conv, w_in, w_out, wide, narrow)
    pl.semaphore_wait(barrier, 6)
    mine = full.at[own, :, columns(piece)]
    crossing = []
    for step in (1, 2, 3):
        copy = remote(mine, mine, z_send.at[step - 1], z_recv.at[step - 1], column[step - 1])
        copy.start()
        crossing.append(copy)
    gathers = []
    for step in (1, 2, 3):
        there = other_owner(own, step)

        def view(q, part, there=there):
            return full.at[there, part_rows(part), columns(q)]

        gathers.append(Gather(view, send, recv, (step - 1) * Gather.SEMS))
    for step in (1, 2, 3):
        crossing[step - 1].wait_recv()
        gathers[step - 1].first()
    for one in gathers:
        one.second()
    for one in gathers:
        one.third()
    for one in gathers:
        one.last()
    for one in gathers:
        one.finish()
    for copy in crossing:
        copy.wait_send()


def gather_weights(conv, w_in, w_out, wide, narrow):
    in_vmem = pl.BlockSpec(memory_space=pltpu.VMEM)
    count = 3 * Gather.SEMS
    return pl.pallas_call(
        gather_kernel,
        out_shape=jax.ShapeDtypeStruct((OWNERS, ROWS, COLS), BF16),
        in_specs=[in_vmem] * 5,
        out_specs=in_vmem,
        scratch_shapes=[
            pltpu.SemaphoreType.DMA((3,)),
            pltpu.SemaphoreType.DMA((3,)),
            pltpu.SemaphoreType.DMA((count,)),
            pltpu.SemaphoreType.DMA((count,)),
        ],
        compiler_params=pltpu.CompilerParams(
            collective_id=0, has_side_effects=True, vmem_limit_bytes=40 << 20
        ),
        name="gather_weights",
    )(conv, w_in, w_out, wide, narrow)


def norm_forward(src, width, chunk, gain, shift, act, unit, slope, spread):
    def body(k, carry):
        rows = pl.ds(pl.multiple_of(k * chunk, chunk), chunk)
        x = src[rows, :width].astype(F32)
        center = x - jnp.mean(x, axis=1, keepdims=True)
        scale = lax.rsqrt(jnp.mean(center * center, axis=1, keepdims=True) + EPSILON)
        xhat = center * scale
        a = xhat * gain + shift
        square = a * a
        half = 0.5 + 0.5 * jnp.tanh(a * (GELU_K + (GELU_K * GELU_C) * square))
        act[rows, :width] = (a * half).astype(BF16)
        unit[rows, :width] = xhat
        inner = GELU_K + (3.0 * GELU_K * GELU_C) * square
        slope[rows, :width] = half + (2.0 * a * inner) * (half * (1.0 - half))
        spread[rows, :] = jnp.broadcast_to(scale, (chunk, 128))
        return carry

    lax.fori_loop(0, TOK // chunk, body, 0)


def fold_rows(values):
    total = values[0:8]
    for k in range(1, values.shape[0] // 8):
        total = total + values[8 * k : 8 * k + 8]
    return total


def norm_backward(grad, width, chunk, gain, unit, slope, spread, finish):
    def body(k, sums):
        rows = pl.ds(pl.multiple_of(k * chunk, chunk), chunk)
        da = grad[rows, :width] * slope[rows, :width]
        xhat = unit[rows, :width]
        product = da * xhat
        dxhat = da * gain
        mean_one = jnp.mean(dxhat, axis=1, keepdims=True)
        mean_two = jnp.mean(dxhat * xhat, axis=1, keepdims=True)
        dx = spread[rows, 0:1] * (dxhat - mean_one - xhat * mean_two)
        finish(rows, dx)
        return (sums[0] + fold_rows(product), sums[1] + fold_rows(da), sums[2] + fold_rows(dx))

    zero = jnp.zeros((8, width), F32)
    sums = lax.fori_loop(0, TOK // chunk, body, (zero, zero, zero))
    return tuple(jnp.sum(s, axis=0, keepdims=True) for s in sums)


def iota(shape, dim):
    return lax.broadcasted_iota(jnp.int32, shape, dim)


def compute_kernel(
    dilation, lengths, tokens, cotangent, full, mom_conv, mom_in, mom_out, mom_wide, mom_narrow,
    out, grad_tokens, grads,
    far, perm_h, vec_w, vec_n, w_in, x_one, wide_grad, tall,
    act_d, act_h, act_g, hid, conv_in, spare, e_all,
    unit_d, slope_d, spread_d, unit_h, slope_h, spread_h,
):
    own = lax.axis_index("fsdp")
    row, col = iota((TOK, TOK), 0), iota((TOK, TOK), 1)
    seg_row, seg_col = jnp.zeros((TOK, TOK), jnp.int32), jnp.zeros((TOK, TOK), jnp.int32)
    end = jnp.int32(0)
    for k in range(8):
        end = end + lengths[0, k]
        seg_row = seg_row + jnp.where(row >= end, 1, 0)
        seg_col = seg_col + jnp.where(col >= end, 1, 0)
    far[...] = jnp.where(seg_row == seg_col, col - row, 4 * TOK)

    def mover(offset):
        return one_hot(far[...] == offset)

    row, col = iota((H, GROUPED), 0), iota((H, GROUPED), 1)
    group = jnp.where(col >= ROWS, 1, 0) + jnp.where(col >= 2 * ROWS, 1, 0) + jnp.where(col >= 3 * ROWS, 1, 0)
    used = col - ROWS * group < SHARD
    perm_h[...] = one_hot((row == col - (ROWS - SHARD) * group) & used)

    row_n, col_n = iota((128, H), 0), iota((128, H), 1)
    row_w, col_w = iota((128, D), 0), iota((128, D), 1)
    total_n, total_w = jnp.zeros((16, H), F32), jnp.zeros((16, D), F32)
    put_n, put_w = [], []
    for i in range(OWNERS):
        lanes = slice(VEC_AT, VEC_AT + 128)
        put_n.append(one_hot((col_n == row_n + SHARD * i) & (row_n < SHARD)))
        total_n = total_n + dot(full[i, 0:16, lanes], put_n[i])
        for h in range(2):
            put_w.append(one_hot((col_w == row_w + SHARD * (2 * i + h)) & (row_w < SHARD)))
            total_w = total_w + dot(full[i, 16 + 16 * h : 32 + 16 * h, lanes], put_w[2 * i + h])
    vec_n[...] = total_n
    vec_w[...] = total_w

    def narrow(b, k):
        return vec_n[6 * b + k : 6 * b + k + 1, :]

    def wide(b, k):
        return vec_w[3 * b + k : 3 * b + k + 1, :]

    def weight_out(b):
        return full[:, :, WO_AT[b] : WO_AT[b] + D].reshape(GROUPED, D)

    for b in range(2):
        for i in range(OWNERS):
            for h in range(2):
                at = SHARD * (2 * i + h)
                lanes = slice(WI_AT[b][h], WI_AT[b][h] + H)
                w_in[b, at : at + SHARD, :] = full[i, 0:SHARD, lanes].astype(F32)

    def taps(b):
        if b == 0:
            return [(H * j, (j - K_ENC // 2) * dilation[0]) for j in range(K_ENC)]
        return [(SPLIT + H * j, -j * dilation[1]) for j in range(K_DEC)]

    def window(at):
        return at - at % 128

    x_one[...] = tokens[...].astype(F32)
    for b in range(2):
        src = tokens if b == 0 else x_one
        norm_forward(src, D, 16, wide(b, 0), wide(b, 1), act_d.at[b], unit_d.at[b], slope_d.at[b], spread_d.at[b])
        hid[:, :] = dot(act_d[b], w_in[b].astype(BF16)) + narrow(b, 0)
        norm_forward(hid, H, 32, narrow(b, 1), narrow(b, 2), act_h.at[0], unit_h.at[b, 0], slope_h.at[b, 0], spread_h.at[b, 0])
        act_g[b, 0] = dot(act_h[0], perm_h[...]).astype(BF16)
        for j, (at, offset) in enumerate(taps(b)):
            moved = dot(mover(offset), act_g[b, 0]).astype(BF16)
            low = CONV_AT + window(at)
            product = dot(moved, full[:, :, low : low + 512].reshape(GROUPED, 512))
            if at % 128:
                product = pltpu.roll(product, 512 - at % 128, 1)
            if j == 0:
                conv_in[...] = product
            else:
                conv_in[...] += product
        conv_in[:, :H] += narrow(b, 3)
        norm_forward(conv_in, H, 32, narrow(b, 4), narrow(b, 5), act_h.at[1], unit_h.at[b, 1], slope_h.at[b, 1], spread_h.at[b, 1])
        act_g[b, 1] = dot(act_h[1], perm_h[...]).astype(BF16)
        result = (x_one[...] + dot(act_g[b, 1], weight_out(b))) + wide(b, 2)
        if b == 0:
            x_one[...] = result
        else:
            out[...] = result.astype(BF16)

    grads[:, :, VEC_AT : VEC_AT + 128] = jnp.zeros((OWNERS, ROWS, 128), BF16)
    upstream = cotangent
    rows_w, rows_n = [None] * 6, [None] * 12
    for b in (1, 0):
        if b == 1:
            e3 = cotangent[...]
            rows_w[3 * b + 2] = jnp.sum(cotangent[...].astype(F32), axis=0, keepdims=True)
        else:
            e3 = wide_grad[...].astype(BF16)
        grads[:, :, WO_AT[b] : WO_AT[b] + D] = dot_tn(act_g[b, 1], e3).astype(BF16).reshape(OWNERS, ROWS, D)
        grads[:, :, WO_AT[b] + D : WO_AT[b] + PIECE] = jnp.zeros((OWNERS, ROWS, PIECE - D), BF16)
        back = dot_nt(e3, weight_out(b)).astype(BF16)
        spare[...] = dot_nt(back, perm_h[...])

        def keep_low(rows, dx):
            act_h[0, rows, :] = dx.astype(BF16)

        sums = norm_backward(spare, H, 32, narrow(b, 4), unit_h.at[b, 1], slope_h.at[b, 1], spread_h.at[b, 1], keep_low)
        rows_n[6 * b + 4], rows_n[6 * b + 5], rows_n[6 * b + 3] = sums
        low_at, high_at = (1920, 3200) if b == 1 else (0, 2048)
        span = high_at - low_at
        e_all[:, :span] = jnp.zeros((TOK, span), BF16)
        for at, offset in taps(b):
            moved = dot(mover(-offset), act_h[0])
            moved = jnp.concatenate([moved, jnp.zeros((TOK, 512 - H), F32)], axis=1)
            if at % 128:
                moved = pltpu.roll(moved, at % 128, 1)
            low = window(at) - low_at
            e_all[:, low : low + 512] += moved.astype(BF16)
        piece = dot_tn(act_g[b, 0], e_all[:, :span]).astype(BF16).reshape(OWNERS, ROWS, span)
        low, high = CONV_AT + low_at, CONV_AT + high_at
        if b == 1:
            grads[:, :, low:high] = piece
        else:
            grads[:, :, low : high - 128] = piece[:, :, : span - 128]
            grads[:, :, high - 128 : high] += piece[:, :, span - 128 :]
        back = dot_nt(e_all[:, :span], full[:, :, low:high].reshape(GROUPED, span)).astype(BF16)
        spare[...] = dot_nt(back, perm_h[...])
        sums = norm_backward(spare, H, 32, narrow(b, 1), unit_h.at[b, 0], slope_h.at[b, 0], spread_h.at[b, 0], keep_low)
        rows_n[6 * b + 1], rows_n[6 * b + 2], rows_n[6 * b + 0] = sums
        tall[:, :] = dot_tn(act_d[b], act_h[0])
        for i in range(OWNERS):
            for h in range(2):
                at = SHARD * (2 * i + h)
                low = WI_AT[b][h]
                grads[i, 0:SHARD, low : low + H] = tall[at : at + SHARD, :].astype(BF16)
                grads[i, SHARD:ROWS, low : low + H] = jnp.zeros((ROWS - SHARD, H), BF16)
                grads[i, :, low + H : low + 512] = jnp.zeros((ROWS, 512 - H), BF16)
        wide_back = dot_nt(act_h[0], w_in[b].astype(BF16))
        x_one[...] = wide_back

        def add_up(rows, dx, b=b):
            if b == 1:
                wide_grad[rows, :] = cotangent[rows, :].astype(F32) + dx
            else:
                grad_tokens[rows, :] = wide_grad[rows, :] + dx

        sums = norm_backward(x_one, D, 16, wide(b, 0), unit_d.at[b], slope_d.at[b], spread_d.at[b], add_up)
        rows_w[3 * b + 0], rows_w[3 * b + 1] = sums[0], sums[1]
        if b == 1:
            rows_w[2] = jnp.sum(wide_grad[...], axis=0, keepdims=True)
    for m in range(12):
        vec_n[m : m + 1, :] = rows_n[m]
    for m in range(6):
        vec_w[m : m + 1, :] = rows_w[m]
    low_n, low_w = vec_n[...].astype(BF16), vec_w[...].astype(BF16)
    lanes = slice(VEC_AT, VEC_AT + 128)
    for i in range(OWNERS):
        grads[i, 0:16, lanes] = dot_nt(low_n, put_n[i]).astype(BF16)
        for h in range(2):
            grads[i, 16 + 16 * h : 32 + 16 * h, lanes] = dot_nt(low_w, put_w[2 * i + h]).astype(BF16)

    @pl.when(lax.axis_index("dp") == 0)
    def _():
        slab = grads.at[own]

        def add(rows, lanes, value):
            slab[rows, lanes] = (slab[rows, lanes].astype(F32) + MOMENT_DECAY * value).astype(BF16)

        full_rows = slice(0, SHARD)
        add(full_rows, slice(CONV_AT, CONV_AT + 3200), mom_conv[...])
        for b in range(2):
            add(full_rows, slice(WO_AT[b], WO_AT[b] + D), mom_out[b])
            for h in range(2):
                at = WI_AT[b][h]
                add(full_rows, slice(at, at + H), mom_in[b, h * SHARD : (h + 1) * SHARD, :])
            for k in range(6):
                m = 6 * b + k
                add(slice(m, m + 1), slice(VEC_AT, VEC_AT + SHARD), mom_narrow[b, k : k + 1, :])
            for k in range(3):
                for h in range(2):
                    m = 16 + 16 * h + 3 * b + k
                    part = mom_wide[b, k : k + 1, h * SHARD : (h + 1) * SHARD]
                    add(slice(m, m + 1), slice(VEC_AT, VEC_AT + SHARD), part)


def compute(dilation, lengths, tokens, cotangent, full, moments):
    in_vmem = pl.BlockSpec(memory_space=pltpu.VMEM)
    in_smem = pl.BlockSpec(memory_space=pltpu.SMEM)
    return pl.pallas_call(
        compute_kernel,
        out_shape=(
            jax.ShapeDtypeStruct((TOK, D), BF16),
            jax.ShapeDtypeStruct((TOK, D), F32),
            jax.ShapeDtypeStruct((OWNERS, ROWS, COLS), BF16),
        ),
        in_specs=[in_smem] * 2 + [in_vmem] * 8,
        out_specs=(in_vmem,) * 3,
        scratch_shapes=[
            vmem((TOK, TOK), jnp.int32),
            vmem((H, GROUPED), BF16),
            vmem((16, D), F32),
            vmem((16, H), F32),
            vmem((2, D, H), F32),
            vmem((TOK, D), F32),
            vmem((TOK, D), F32),
            vmem((D, H), F32),
            vmem((2, TOK, D), BF16),
            vmem((2, TOK, H), BF16),
            vmem((2, 2, TOK, GROUPED), BF16),
            vmem((TOK, H), F32),
            vmem((TOK, 512), F32),
            vmem((TOK, H), F32),
            vmem((TOK, 2048), BF16),
            vmem((2, TOK, D), F32),
            vmem((2, TOK, D), F32),
            vmem((2, TOK, 128), F32),
            vmem((2, 2, TOK, H), F32),
            vmem((2, 2, TOK, H), F32),
            vmem((2, 2, TOK, 128), F32),
        ],
        compiler_params=pltpu.CompilerParams(vmem_limit_bytes=58 << 20),
        name="blocks",
    )(dilation, lengths, tokens, cotangent, full, *moments)


MATRICES = (
    dict(kind="out", pieces=(0,), piece=0, own=2, lanes=(0, D), scale=math.sqrt(D / H)),
    dict(kind="out", pieces=(1,), piece=1, own=1, lanes=(0, D), scale=math.sqrt(D / H)),
    dict(kind="conv", pieces=(2, 3, 4), piece=3, own=1, lanes=(0, 2000), scale=1.0),
    dict(kind="conv", pieces=(4, 5), piece=4, own=2, lanes=(208, 1408), scale=1.0),
    dict(kind="in", pieces=(5, 6), piece=6, own=2, lanes=(512, 1536), scale=1.0),
    dict(kind="in", pieces=(6, 7), piece=7, own=1, lanes=(640, 1664), scale=1.0),
)
WINDOW = 3 * PIECE
ROUTES = tuple((k, s, q) for k, m in enumerate(MATRICES) for s, q in enumerate(m["pieces"]))


def is_at(piece, own, matrix):
    return (piece == matrix["piece"]) & (own == matrix["own"])


def not_at(piece, own, matrix):
    return (piece != matrix["piece"]) | (own != matrix["own"])


def window_lanes(s):
    return pl.ds(s * PIECE, PIECE)


def greet_owners(barrier, base, piece, own):
    for k, s, q in ROUTES:
        matrix = MATRICES[k]
        there = (base + matrix["piece"], matrix["own"])

        @pl.when((piece == q) & not_at(piece, own, matrix))
        def _(there=there):
            pl.semaphore_signal(barrier, inc=1, device_id=there, device_id_type=MESH)

    for k, s, q in ROUTES:
        matrix = MATRICES[k]

        @pl.when(is_at(piece, own, matrix))
        def _(matrix=matrix, q=q):
            for i in range(OWNERS):
                if q != matrix["piece"] or i != matrix["own"]:
                    pl.semaphore_signal(barrier, inc=1, device_id=(base + q, i), device_id_type=MESH)


def owner_greetings(piece, own):
    count = jnp.int32(0)
    for k, s, q in ROUTES:
        matrix = MATRICES[k]
        holds = (piece == q) & not_at(piece, own, matrix)
        count = count + jnp.where(holds, 1, 0)
        count = count + jnp.where(is_at(piece, own, matrix), OWNERS - (1 if q == matrix["piece"] else 0), 0)
    return count


def reduce_kernel(
    extra, grads, moment, matrix_window,
    from_core, sums, from_x, from_y, last_x, last_y, from_z, from_far,
    core_send, core_recv, plane_send, plane_recv, z_send, z_recv, far_send, far_recv,
    gather_send, gather_recv, own_send, own_recv,
):
    base, piece, own = place()
    me = base + piece
    core, near_x, near_y = [(base + flip(piece, bit), own) for bit in (1, 2, 4)]
    column = [(me, other_owner(own, step)) for step in (1, 2, 3)]
    far = [(flip(me, bit), own) for bit in extra]
    barrier = greet([core, near_x, near_y] + column + far)
    greet_owners(barrier, base, piece, own)
    pl.semaphore_wait(barrier, 6 + len(extra) + owner_greetings(piece, own))

    parity = piece % 2
    at = piece // 2
    at_x, at_y, at_xy = flip(at, 1), flip(at, 2), 3 - at
    order = (at_xy, at_x, at_y, at)
    started = []

    def send(src, dst, sems, k, device):
        copy = remote(src, dst, sems[0].at[k], sems[1].at[k], device)
        copy.start()
        started.append(copy)
        return copy

    crossing = []
    for k, m in enumerate(order):
        theirs = grads.at[:, :, columns(2 * m + 1 - parity)]
        crossing.append(send(theirs, from_core.at[k], (core_send, core_recv), k, core))

    def merge(k, m):
        crossing[k].wait_recv()
        mine = grads[:, :, columns(2 * m + parity)].astype(F32)
        sums[k] = (mine + from_core[k].astype(F32)).astype(BF16)

    plane = (plane_send, plane_recv)
    low, high = pl.ds(0, 2), pl.ds(2, 2)
    merge(0, at_xy)
    one_x = send(sums.at[0, low], from_x.at[0], plane, 0, near_x)
    one_y = send(sums.at[0, high], from_y.at[0], plane, 1, near_y)
    merge(1, at_x)
    two_x = send(sums.at[1, low], from_x.at[1], plane, 2, near_x)
    merge(2, at_y)
    two_y = send(sums.at[2, high], from_y.at[1], plane, 3, near_y)
    merge(3, at)
    one_x.wait_recv()
    sums[2, 0:2] = (sums[2, 0:2].astype(F32) + from_x[0].astype(F32)).astype(BF16)
    three_y = send(sums.at[2, low], last_y, plane, 4, near_y)
    one_y.wait_recv()
    sums[1, 2:4] = (sums[1, 2:4].astype(F32) + from_y[0].astype(F32)).astype(BF16)
    three_x = send(sums.at[1, high], last_x, plane, 5, near_x)
    two_x.wait_recv()
    two_y.wait_recv()
    three_y.wait_recv()
    three_x.wait_recv()
    low_sum = sums[3, 0:2].astype(F32) + from_x[1].astype(F32) + last_y[...].astype(F32)
    high_sum = sums[3, 2:4].astype(F32) + from_y[1].astype(F32) + last_x[...].astype(F32)
    sums[3, 0:2] = low_sum.astype(BF16)
    sums[3, 2:4] = high_sum.astype(BF16)
    for k, device in enumerate(far):
        copy = remote(sums.at[3], from_far.at[k], far_send.at[k], far_recv.at[k], device)
        copy.start()
        copy.wait()
        sums[3] = (sums[3].astype(F32) + from_far[k].astype(F32)).astype(BF16)
    crossing = []
    for step in (1, 2, 3):
        there = other_owner(own, step)
        crossing.append(
            send(sums.at[3, there], from_z.at[step - 1], (z_send, z_recv), step - 1, column[step - 1])
        )
    total = sums[3, own].astype(F32)
    for step in (1, 2, 3):
        crossing[step - 1].wait_recv()
        total = total + from_z[step - 1].astype(F32)
    moment[:, columns(piece)] = total.astype(BF16)

    def view(q, part):
        return moment.at[part_rows(part), columns(q)]

    gather = Gather(view, gather_send, gather_recv, 0)
    gather.first()

    def to_owner(k, s, q):
        matrix = MATRICES[k]
        there = (base + matrix["piece"], matrix["own"])
        src = moment.at[:, columns(piece)]
        dst = matrix_window.at[own, :, window_lanes(s)]
        return remote(src, dst, own_send.at[k], own_recv.at[OWNERS * s + own], there)

    for k, s, q in ROUTES:
        matrix = MATRICES[k]

        @pl.when((piece == q) & not_at(piece, own, matrix))
        def _(k=k, s=s, q=q):
            to_owner(k, s, q).start()

        @pl.when((piece == q) & is_at(piece, own, matrix))
        def _(s=s):
            matrix_window[own, :, window_lanes(s)] = moment[:, columns(piece)]

    gather.second()
    gather.third()
    gather.last()
    for k, s, q in ROUTES:
        matrix = MATRICES[k]

        @pl.when((piece == q) & not_at(piece, own, matrix))
        def _(k=k, s=s, q=q):
            to_owner(k, s, q).wait_send()

        @pl.when(is_at(piece, own, matrix))
        def _(matrix=matrix, s=s, q=q):
            for i in range(OWNERS):
                if q != matrix["piece"] or i != matrix["own"]:
                    dst = matrix_window.at[i, :, window_lanes(s)]
                    src = moment.at[:, columns(piece)]
                    sems = (own_send.at[0], own_recv.at[OWNERS * s + i])
                    remote(src, dst, sems[0], sems[1], (base + q, i)).wait_recv()

    gather.finish()
    for copy in started:
        copy.wait_send()


def reduce_grads(grads, extra):
    in_vmem = pl.BlockSpec(memory_space=pltpu.VMEM)

    def dma(n):
        return pltpu.SemaphoreType.DMA((max(n, 1),))

    part = (OWNERS, ROWS, PIECE)
    half = (2, ROWS, PIECE)
    return pl.pallas_call(
        functools.partial(reduce_kernel, extra),
        out_shape=(
            jax.ShapeDtypeStruct((ROWS, COLS), BF16),
            jax.ShapeDtypeStruct((OWNERS, ROWS, WINDOW), BF16),
        ),
        in_specs=[in_vmem],
        out_specs=(in_vmem,) * 2,
        scratch_shapes=[
            vmem((4,) + part, BF16),
            vmem((4,) + part, BF16),
            vmem((2,) + half, BF16),
            vmem((2,) + half, BF16),
            vmem(half, BF16),
            vmem(half, BF16),
            vmem((3, ROWS, PIECE), BF16),
            vmem((max(len(extra), 1),) + part, BF16),
            dma(4), dma(4), dma(6), dma(6), dma(3), dma(3), dma(len(extra)), dma(len(extra)),
            dma(Gather.SEMS), dma(Gather.SEMS), dma(6), dma(12),
        ],
        compiler_params=pltpu.CompilerParams(
            collective_id=1, has_side_effects=True, vmem_limit_bytes=48 << 20
        ),
        name="reduce_grads",
    )(grads)


def split(a):
    high = a.astype(BF16)
    return high, (a - high.astype(F32)).astype(BF16)


def dot_fine(a, b):
    a_high, a_low = split(a)
    b_high, b_low = split(b)
    return dot(a_high, b_high) + (dot(a_high, b_low) + dot(a_low, b_high))


def dot_low(a, b):
    return dot(a.astype(BF16), b.astype(BF16))


def polynomial_of(gram, size):
    eye = iota((size, size), 0) == iota((size, size), 1)
    unit = jnp.where(eye, 1.0, 0.0)
    power = jnp.sum(jnp.sum(jnp.where(eye, gram, 0.0), axis=1, keepdims=True), axis=0, keepdims=True)
    inverse = 1.0 / (jnp.sqrt(power) + NORM_FLOOR)
    current = gram * inverse * inverse
    result = None
    for step in range(NS_STEPS):
        square = dot_fine if step > 2 else dot_low
        poly = COEF_A * unit + COEF_B * current + COEF_C * square(current, current)
        result = poly if result is None else dot_low(poly, result)
        if step < NS_STEPS - 1:
            first = dot_fine if step < 2 else dot_low
            second = dot_fine if step < 1 else dot_low
            current = second(first(poly, current), poly)
    return result, inverse


def ortho_kernel(window, update):
    piece, own = lax.axis_index("dp") % PIECES, lax.axis_index("fsdp")
    for matrix in MATRICES:

        @pl.when(is_at(piece, own, matrix))
        def _(matrix=matrix):
            low, high = matrix["lanes"]
            factor = MATRIX_RATE * matrix["scale"]
            if matrix["kind"] == "in":
                halves = [
                    window[:, :, low + 512 * h : low + 512 * (h + 1)].reshape(GROUPED, 512) for h in range(2)
                ]
                gram = dot_tn(halves[0], halves[0]) + dot_tn(halves[1], halves[1])
                poly, inverse = polynomial_of(gram, 512)
                poly = (poly * (inverse * factor)).astype(BF16)
                update[...] = jnp.zeros(update.shape, BF16)
                for h in range(2):
                    step = dot(halves[h], poly).astype(BF16).reshape(OWNERS, ROWS, 512)
                    update[:, :, low + 512 * h : low + 512 * (h + 1)] = step
            else:
                start = low - low % 128
                stop = -(-high // 128) * 128
                values = window[:, :, start:stop].reshape(GROUPED, stop - start)
                lane = iota((GROUPED, stop - start), 1) + start
                values = jnp.where((lane >= low) & (lane < high), values, jnp.zeros((), BF16))
                poly, inverse = polynomial_of(dot_nt(values, values), GROUPED)
                poly = (poly * (inverse * factor)).astype(BF16)
                step = dot(poly, values).astype(BF16).reshape(OWNERS, ROWS, stop - start)
                update[...] = jnp.zeros(update.shape, BF16)
                update[:, :, start:stop] = step


def orthogonalize(window):
    in_vmem = pl.BlockSpec(memory_space=pltpu.VMEM)
    return pl.pallas_call(
        ortho_kernel,
        out_shape=jax.ShapeDtypeStruct(window.shape, BF16),
        in_specs=[in_vmem],
        out_specs=in_vmem,
        compiler_params=pltpu.CompilerParams(vmem_limit_bytes=48 << 20),
        name="orthogonalize",
    )(window)


def slot_of(k, q):
    return sum(1 for j, s, other in ROUTES if other == q and j < k)


def spread_kernel(window, update, parts, send, recv, gather_send, gather_recv):
    base, piece, own = place()
    barrier = greet([(base + flip(piece, bit), own) for bit in (1, 2, 4)])
    greet_owners(barrier, base, piece, own)
    pl.semaphore_wait(barrier, 3 + owner_greetings(piece, own))

    def outgoing(s, q, slot, i):
        src = window.at[i, :, window_lanes(s)]
        return remote(src, parts.at[slot], send.at[OWNERS * s + i], recv.at[slot], (base + q, i))

    for k, s, q in ROUTES:
        matrix = MATRICES[k]
        slot = slot_of(k, q)

        @pl.when(is_at(piece, own, matrix))
        def _(matrix=matrix, s=s, q=q, slot=slot):
            for i in range(OWNERS):
                if q != matrix["piece"] or i != matrix["own"]:
                    outgoing(s, q, slot, i).start()
                else:
                    parts[slot] = window[i, :, window_lanes(s)]

    for k, s, q in ROUTES:
        matrix = MATRICES[k]
        slot = slot_of(k, q)

        @pl.when((piece == q) & not_at(piece, own, matrix))
        def _(matrix=matrix, slot=slot):
            there = (base + matrix["piece"], matrix["own"])
            remote(window.at[0, :, window_lanes(0)], parts.at[slot], send.at[0], recv.at[slot], there).wait_recv()

    shared = [q for q in range(PIECES) if sum(1 for r in ROUTES if r[2] == q) == 2]
    update[:, columns(piece)] = parts[0]
    for q in shared:

        @pl.when(piece == q)
        def _():
            update[:, columns(piece)] = parts[0] + parts[1]

    def view(q, part):
        return update.at[part_rows(part), columns(q)]

    gather = Gather(view, gather_send, gather_recv, 0)
    gather.first()
    gather.second()
    gather.third()
    gather.last()
    gather.finish()
    for k, s, q in ROUTES:
        matrix = MATRICES[k]

        @pl.when(is_at(piece, own, matrix))
        def _(matrix=matrix, s=s, q=q):
            for i in range(OWNERS):
                if q != matrix["piece"] or i != matrix["own"]:
                    outgoing(s, q, 0, i).wait_send()


def spread_steps(window):
    in_vmem = pl.BlockSpec(memory_space=pltpu.VMEM)

    def dma(n):
        return pltpu.SemaphoreType.DMA((n,))

    return pl.pallas_call(
        spread_kernel,
        out_shape=jax.ShapeDtypeStruct((ROWS, COLS), BF16),
        in_specs=[in_vmem],
        out_specs=in_vmem,
        scratch_shapes=[
            vmem((2, ROWS, PIECE), BF16),
            dma(12), dma(2), dma(Gather.SEMS), dma(Gather.SEMS),
        ],
        compiler_params=pltpu.CompilerParams(
            collective_id=2, has_side_effects=True, vmem_limit_bytes=40 << 20
        ),
        name="spread_steps",
    )(window)


def finish_kernel(
    vector_step, moment, update, conv, w_in, w_out, wide, narrow,
    mom_in, mom_conv, mom_out, mom_wide, mom_narrow,
    new_in, new_conv, new_out, new_wide, new_narrow, low_in, low_conv, low_out,
):
    lanes = slice(CONV_AT, CONV_AT + 3200)
    mom_conv[...] = moment[:SHARD, lanes].astype(F32)
    value = conv[...] - update[:SHARD, lanes].astype(F32)
    new_conv[...] = value
    low_conv[...] = value.astype(BF16)
    for b in range(2):
        lanes = slice(WO_AT[b], WO_AT[b] + D)
        mom_out[b] = moment[:SHARD, lanes].astype(F32)
        value = w_out[b] - update[:SHARD, lanes].astype(F32)
        new_out[b] = value
        low_out[b] = value.astype(BF16)
        for h in range(2):
            lanes = slice(WI_AT[b][h], WI_AT[b][h] + H)
            rows = slice(h * SHARD, (h + 1) * SHARD)
            mom_in[b, rows, :] = moment[:SHARD, lanes].astype(F32)
            value = w_in[b, rows, :] - update[:SHARD, lanes].astype(F32)
            new_in[b, rows, :] = value
            low_in[b, rows, :] = value.astype(BF16)
        lanes = slice(VEC_AT, VEC_AT + SHARD)
        vectors = moment[:, VEC_AT : VEC_AT + 128].astype(F32)
        for k in range(6):
            m = 6 * b + k
            value = vectors[m : m + 1, :SHARD]
            mom_narrow[b, k : k + 1, :] = value
            new_narrow[b, k : k + 1, :] = narrow[b, k : k + 1, :] - vector_step * value
        for k in range(3):
            for h in range(2):
                m = 16 + 16 * h + 3 * b + k
                lanes = slice(h * SHARD, (h + 1) * SHARD)
                value = vectors[m : m + 1, :SHARD]
                mom_wide[b, k : k + 1, lanes] = value
                new_wide[b, k : k + 1, lanes] = wide[b, k : k + 1, lanes] - vector_step * value


def finish(vector_step, moment, update, conv, w_in, w_out, wide, narrow):
    in_vmem = pl.BlockSpec(memory_space=pltpu.VMEM)
    shapes = [w_in.shape, conv.shape, w_out.shape, wide.shape, narrow.shape]
    outs = [jax.ShapeDtypeStruct(s, F32) for s in shapes + shapes]
    outs += [jax.ShapeDtypeStruct(s, BF16) for s in shapes[:3]]
    return pl.pallas_call(
        functools.partial(finish_kernel, vector_step),
        out_shape=tuple(outs),
        in_specs=[in_vmem] * 7,
        out_specs=(in_vmem,) * len(outs),
        compiler_params=pltpu.CompilerParams(vmem_limit_bytes=40 << 20),
        name="finish",
    )(moment, update, conv, w_in, w_out, wide, narrow)


def shards(
    extra, vector_step, tokens, cotangent, lengths, dilation, proj_in, conv_weight, proj_out, vec_wide, vec_narrow,
    mom_in, mom_conv, mom_out, mom_wide, mom_narrow,
):
    full = gather_weights(conv_weight, proj_in, proj_out, vec_wide, vec_narrow)
    moments = (mom_conv, mom_in, mom_out, mom_wide, mom_narrow)
    out, grad_tokens, grads = compute(dilation, lengths, tokens, cotangent, full, moments)
    moment, window = reduce_grads(grads, extra)
    update = spread_steps(orthogonalize(window))
    rest = finish(vector_step, moment, update, conv_weight, proj_in, proj_out, vec_wide, vec_narrow)
    return (out, grad_tokens) + tuple(rest)


def solution(mesh):
    groups, owners = mesh.shape["dp"], mesh.shape["fsdp"]
    assert owners == OWNERS and groups % PIECES == 0
    extra, bit = [], PIECES
    while bit < groups:
        extra.append(bit)
        bit *= 2
    assert bit == groups
    vector_step = VECTOR_RATE / math.sqrt(TOK * groups * owners)
    tok, rep = P(("dp", "fsdp"), None), P()
    mid, first, final = P(None, "fsdp", None), P("fsdp", None), P(None, None, "fsdp")
    params = (mid, first, mid, final, final)
    return jax.shard_map(
        functools.partial(shards, tuple(extra), vector_step),
        mesh=mesh,
        in_specs=(tok, tok, tok, rep) + params + params,
        out_specs=(tok, tok) + params + params + (mid, first, mid),
        check_vma=False,
    )
```

```python
import functools
import math

import jax
import jax.numpy as jnp
from jax import lax
from jax.experimental import pallas as pl
from jax.experimental.pallas import tpu as pltpu
from jax.sharding import PartitionSpec as P

D = 800
H = 400
K_ENC = 5
K_DEC = 3
NS_STEPS = 5
EPSILON = 1e-05
NORM_FLOOR = 1e-07
COEF_A = 3.4445
COEF_B = -4.775
COEF_C = 2.0315
MOMENT_DECAY = 0.5
MATRIX_RATE = 0.5
VECTOR_RATE = 0.1

F32 = jnp.float32
BF16 = jnp.bfloat16
MESH = pl.DeviceIdType.MESH

OWNERS = 4
PIECES = 8
SHARD = 100
ROWS = 112
PIECE = 896
COLS = PIECES * PIECE
WO_AT = (0, 896)
CONV_AT = 1792
WI_AT = ((4992, 5504), (6016, 6528))
VEC_AT = 7040
SPLIT = K_ENC * H
TOK = 256
GROUPED = OWNERS * ROWS

GELU_K = math.sqrt(2.0 / math.pi)
GELU_C = 0.044715


def vmem(shape, dtype):
    return pltpu.VMEM(shape, dtype)


def dot(a, b):
    return lax.dot_general(a, b, (((1,), (0,)), ((), ())), preferred_element_type=F32)


def dot_nt(a, b):
    return lax.dot_general(a, b, (((1,), (1,)), ((), ())), preferred_element_type=F32)


def dot_tn(a, b):
    return lax.dot_general(a, b, (((0,), (0,)), ((), ())), preferred_element_type=F32)


def one_hot(mask):
    return jnp.where(mask, 1.0, 0.0).astype(BF16)


def pack(slab, conv, w_in, w_out, wide, narrow):
    slab[...] = jnp.zeros((ROWS, COLS), BF16)
    slab[:SHARD, CONV_AT : CONV_AT + 3200] = conv[...].astype(BF16)
    for b in range(2):
        slab[:SHARD, WO_AT[b] : WO_AT[b] + D] = w_out[:, b, :].astype(BF16)
        for h in range(2):
            at = WI_AT[b][h]
            slab[:SHARD, at : at + H] = w_in[b, h * SHARD : (h + 1) * SHARD, :].astype(BF16)
    for b in range(2):
        for k in range(6):
            m = 6 * b + k
            slab[m : m + 1, VEC_AT : VEC_AT + SHARD] = narrow[k, b : b + 1, :].astype(BF16)
        for k in range(3):
            for h in range(2):
                m = 16 + 16 * h + 3 * b + k
                part = wide[k, b : b + 1, h * SHARD : (h + 1) * SHARD]
                slab[m : m + 1, VEC_AT : VEC_AT + SHARD] = part.astype(BF16)


def place():
    at = lax.axis_index("dp")
    piece = at % PIECES
    return at - piece, piece, lax.axis_index("fsdp")


def flip(value, bit):
    return value + bit - 2 * bit * ((value // bit) % 2)


def other_owner(own, step):
    if step == 3:
        return 3 - own
    return flip(own, step)


def columns(piece):
    return pl.ds(pl.multiple_of(piece * PIECE, PIECE), PIECE)


def remote(src, dst, send, recv, device):
    return pltpu.make_async_remote_copy(
        src_ref=src,
        dst_ref=dst,
        send_sem=send,
        recv_sem=recv,
        device_id=device,
        device_id_type=MESH,
    )


def greet(devices):
    barrier = pltpu.get_barrier_semaphore()
    for device in devices:
        pl.semaphore_signal(barrier, inc=1, device_id=device, device_id_type=MESH)
    return barrier


class Gather:
    SEMS = 10

    def __init__(self, view, send, recv, at):
        base, piece, own = place()
        self.view, self.send, self.recv, self.at = view, send, recv, at
        self.piece = piece
        self.near = {bit: (base + flip(piece, bit), own) for bit in (1, 2, 4)}
        self.started = []

    def copy(self, bit, q, part, k):
        ref = self.view(q, part)
        sems = (self.send.at[self.at + k], self.recv.at[self.at + k])
        return remote(ref, ref, sems[0], sems[1], self.near[bit])

    def start(self, bit, q, part, k):
        copy = self.copy(bit, q, part, k)
        copy.start()
        self.started.append(copy)

    def first(self):
        p = self.piece
        self.start(4, p, 0, 0)
        self.start(2, p, 1, 1)

    def second(self):
        p = self.piece
        for k in (0, 1):
            self.started[k].wait_recv()
        self.start(2, p, 0, 2)
        self.start(2, flip(p, 4), 0, 3)
        self.start(4, p, 1, 4)
        self.start(4, flip(p, 2), 1, 5)
        self.start(1, p, None, 6)

    def third(self):
        p = self.piece
        for k in (2, 3, 4, 5):
            self.started[k].wait_recv()
        self.start(1, flip(p, 2), None, 7)
        self.start(1, flip(p, 4), None, 8)
        self.start(1, flip(flip(p, 2), 4), None, 9)

    def last(self):
        for k in (6, 7, 8, 9):
            self.started[k].wait_recv()

    def finish(self):
        for copy in self.started:
            copy.wait_send()


def part_rows(part):
    if part is None:
        return pl.ds(0, ROWS)
    return pl.ds(0, 64) if part == 0 else pl.ds(64, 48)


def gather_kernel(conv, w_in, w_out, wide, narrow, full, z_send, z_recv, send, recv):
    base, piece, own = place()
    me = base + piece
    near = [(base + flip(piece, bit), own) for bit in (1, 2, 4)]
    column = [(me, other_owner(own, step)) for step in (1, 2, 3)]
    barrier = greet(near + column)
    pack(full.at[own], conv, w_in, w_out, wide, narrow)
    pl.semaphore_wait(barrier, 6)
    mine = full.at[own, :, columns(piece)]
    crossing = []
    for step in (1, 2, 3):
        copy = remote(mine, mine, z_send.at[step - 1], z_recv.at[step - 1], column[step - 1])
        copy.start()
        crossing.append(copy)
    gathers = []
    for step in (1, 2, 3):
        there = other_owner(own, step)

        def view(q, part, there=there):
            return full.at[there, part_rows(part), columns(q)]

        gathers.append(Gather(view, send, recv, (step - 1) * Gather.SEMS))
    for step in (1, 2, 3):
        crossing[step - 1].wait_recv()
        gathers[step - 1].first()
    for one in gathers:
        one.second()
    for one in gathers:
        one.third()
    for one in gathers:
        one.last()
    for one in gathers:
        one.finish()
    for copy in crossing:
        copy.wait_send()


def gather_weights(conv, w_in, w_out, wide, narrow):
    in_vmem = pl.BlockSpec(memory_space=pltpu.VMEM)
    count = 3 * Gather.SEMS
    return pl.pallas_call(
        gather_kernel,
        out_shape=jax.ShapeDtypeStruct((OWNERS, ROWS, COLS), BF16),
        in_specs=[in_vmem] * 5,
        out_specs=in_vmem,
        scratch_shapes=[
            pltpu.SemaphoreType.DMA((3,)),
            pltpu.SemaphoreType.DMA((3,)),
            pltpu.SemaphoreType.DMA((count,)),
            pltpu.SemaphoreType.DMA((count,)),
        ],
        compiler_params=pltpu.CompilerParams(
            collective_id=0, has_side_effects=True, vmem_limit_bytes=40 << 20
        ),
        name="gather_weights",
    )(conv, w_in, w_out, wide, narrow)


def norm_forward(src, width, chunk, gain, shift, act, unit, slope, spread):
    def body(k, carry):
        rows = pl.ds(pl.multiple_of(k * chunk, chunk), chunk)
        x = src[rows, :width].astype(F32)
        center = x - jnp.mean(x, axis=1, keepdims=True)
        scale = lax.rsqrt(jnp.mean(center * center, axis=1, keepdims=True) + EPSILON)
        xhat = center * scale
        a = xhat * gain + shift
        square = a * a
        half = 0.5 + 0.5 * jnp.tanh(a * (GELU_K + (GELU_K * GELU_C) * square))
        act[rows, :width] = (a * half).astype(BF16)
        unit[rows, :width] = xhat
        inner = GELU_K + (3.0 * GELU_K * GELU_C) * square
        slope[rows, :width] = half + (2.0 * a * inner) * (half * (1.0 - half))
        spread[rows, :] = jnp.broadcast_to(scale, (chunk, 128))
        return carry

    lax.fori_loop(0, TOK // chunk, body, 0)


def fold_rows(values):
    total = values[0:8]
    for k in range(1, values.shape[0] // 8):
        total = total + values[8 * k : 8 * k + 8]
    return total


def norm_backward(grad, width, chunk, gain, unit, slope, spread, finish):
    def body(k, sums):
        rows = pl.ds(pl.multiple_of(k * chunk, chunk), chunk)
        da = grad[rows, :width] * slope[rows, :width]
        xhat = unit[rows, :width]
        product = da * xhat
        dxhat = da * gain
        mean_one = jnp.mean(dxhat, axis=1, keepdims=True)
        mean_two = jnp.mean(dxhat * xhat, axis=1, keepdims=True)
        dx = spread[rows, 0:1] * (dxhat - mean_one - xhat * mean_two)
        finish(rows, dx)
        return (sums[0] + fold_rows(product), sums[1] + fold_rows(da), sums[2] + fold_rows(dx))

    zero = jnp.zeros((8, width), F32)
    sums = lax.fori_loop(0, TOK // chunk, body, (zero, zero, zero))
    return tuple(jnp.sum(s, axis=0, keepdims=True) for s in sums)


def iota(shape, dim):
    return lax.broadcasted_iota(jnp.int32, shape, dim)


def compute_kernel(
    dilation, lengths, tokens, cotangent, full, mom_conv, mom_in, mom_out, mom_wide, mom_narrow,
    out, grad_tokens, grads,
    far, perm_h, vec_w, vec_n, w_in, x_one, wide_grad, tall,
    act_d, act_h, act_g, hid, conv_in, spare, e_all,
    unit_d, slope_d, spread_d, unit_h, slope_h, spread_h,
):
    own = lax.axis_index("fsdp")
    row, col = iota((TOK, TOK), 0), iota((TOK, TOK), 1)
    seg_row, seg_col = jnp.zeros((TOK, TOK), jnp.int32), jnp.zeros((TOK, TOK), jnp.int32)
    end = jnp.int32(0)
    for k in range(8):
        end = end + lengths[0, k]
        seg_row = seg_row + jnp.where(row >= end, 1, 0)
        seg_col = seg_col + jnp.where(col >= end, 1, 0)
    far[...] = jnp.where(seg_row == seg_col, col - row, 4 * TOK)

    def mover(offset):
        return one_hot(far[...] == offset)

    row, col = iota((H, GROUPED), 0), iota((H, GROUPED), 1)
    group = jnp.where(col >= ROWS, 1, 0) + jnp.where(col >= 2 * ROWS, 1, 0) + jnp.where(col >= 3 * ROWS, 1, 0)
    used = col - ROWS * group < SHARD
    perm_h[...] = one_hot((row == col - (ROWS - SHARD) * group) & used)

    row_n, col_n = iota((128, H), 0), iota((128, H), 1)
    row_w, col_w = iota((128, D), 0), iota((128, D), 1)
    total_n, total_w = jnp.zeros((16, H), F32), jnp.zeros((16, D), F32)
    put_n, put_w = [], []
    for i in range(OWNERS):
        lanes = slice(VEC_AT, VEC_AT + 128)
        put_n.append(one_hot((col_n == row_n + SHARD * i) & (row_n < SHARD)))
        total_n = total_n + dot(full[i, 0:16, lanes], put_n[i])
        for h in range(2):
            put_w.append(one_hot((col_w == row_w + SHARD * (2 * i + h)) & (row_w < SHARD)))
            total_w = total_w + dot(full[i, 16 + 16 * h : 32 + 16 * h, lanes], put_w[2 * i + h])
    vec_n[...] = total_n
    vec_w[...] = total_w

    def narrow(b, k):
        return vec_n[6 * b + k : 6 * b + k + 1, :]

    def wide(b, k):
        return vec_w[3 * b + k : 3 * b + k + 1, :]

    def weight_out(b):
        return full[:, :, WO_AT[b] : WO_AT[b] + D].reshape(GROUPED, D)

    for b in range(2):
        for i in range(OWNERS):
            for h in range(2):
                at = SHARD * (2 * i + h)
                lanes = slice(WI_AT[b][h], WI_AT[b][h] + H)
                w_in[b, at : at + SHARD, :] = full[i, 0:SHARD, lanes].astype(F32)

    def taps(b):
        if b == 0:
            return [(H * j, (j - K_ENC // 2) * dilation[0]) for j in range(K_ENC)]
        return [(SPLIT + H * j, -j * dilation[1]) for j in range(K_DEC)]

    def window(at):
        return at - at % 128

    x_one[...] = tokens[...].astype(F32).T
    for b in range(2):
        norm_forward(x_one, D, 128, wide(b, 0), wide(b, 1), act_d.at[b], unit_d.at[b], slope_d.at[b], spread_d.at[b])
        hid[:, :] = dot(act_d[b], w_in[b].astype(BF16)) + narrow(b, 0)
        norm_forward(hid, H, 128, narrow(b, 1), narrow(b, 2), act_h.at[0], unit_h.at[b, 0], slope_h.at[b, 0], spread_h.at[b, 0])
        act_g[b, 0] = dot(act_h[0], perm_h[...]).astype(BF16)
        for j, (at, offset) in enumerate(taps(b)):
            moved = dot(mover(offset), act_g[b, 0]).astype(BF16)
            low = CONV_AT + window(at)
            product = dot(moved, full[:, :, low : low + 512].reshape(GROUPED, 512))
            if at % 128:
                product = pltpu.roll(product, 512 - at % 128, 1)
            if j == 0:
                conv_in[...] = product
            else:
                conv_in[...] += product
        conv_in[:, :H] += narrow(b, 3)
        norm_forward(conv_in, H, 128, narrow(b, 4), narrow(b, 5), act_h.at[1], unit_h.at[b, 1], slope_h.at[b, 1], spread_h.at[b, 1])
        act_g[b, 1] = dot(act_h[1], perm_h[...]).astype(BF16)
        result = (x_one[...] + dot(act_g[b, 1], weight_out(b))) + wide(b, 2)
        if b == 0:
            x_one[...] = result
        else:
            out[...] = result.T.astype(BF16)

    grads[:, :, VEC_AT : VEC_AT + 128] = jnp.zeros((OWNERS, ROWS, 128), BF16)
    rows_w, rows_n = [None] * 6, [None] * 12
    for b in (1, 0):
        if b == 1:
            wide_grad[...] = cotangent[...].astype(F32).T
        rows_w[3 * b + 2] = jnp.sum(wide_grad[...], axis=0, keepdims=True)
        e3 = wide_grad[...].astype(BF16)
        grads[:, :, WO_AT[b] : WO_AT[b] + D] = dot_tn(act_g[b, 1], e3).astype(BF16).reshape(OWNERS, ROWS, D)
        grads[:, :, WO_AT[b] + D : WO_AT[b] + PIECE] = jnp.zeros((OWNERS, ROWS, PIECE - D), BF16)
        back = dot_nt(e3, weight_out(b)).astype(BF16)
        spare[...] = dot_nt(back, perm_h[...])

        def keep_low(rows, dx):
            act_h[0, rows, :] = dx.astype(BF16)

        sums = norm_backward(spare, H, 128, narrow(b, 4), unit_h.at[b, 1], slope_h.at[b, 1], spread_h.at[b, 1], keep_low)
        rows_n[6 * b + 4], rows_n[6 * b + 5], rows_n[6 * b + 3] = sums
        low_at, high_at = (1920, 3200) if b == 1 else (0, 2048)
        span = high_at - low_at
        e_all[:, :span] = jnp.zeros((TOK, span), BF16)
        for at, offset in taps(b):
            moved = dot(mover(-offset), act_h[0])
            moved = jnp.concatenate([moved, jnp.zeros((TOK, 512 - H), F32)], axis=1)
            if at % 128:
                moved = pltpu.roll(moved, at % 128, 1)
            low = window(at) - low_at
            e_all[:, low : low + 512] += moved.astype(BF16)
        piece = dot_tn(act_g[b, 0], e_all[:, :span]).astype(BF16).reshape(OWNERS, ROWS, span)
        low, high = CONV_AT + low_at, CONV_AT + high_at
        if b == 1:
            grads[:, :, low:high] = piece
        else:
            grads[:, :, low : high - 128] = piece[:, :, : span - 128]
            grads[:, :, high - 128 : high] += piece[:, :, span - 128 :]
        back = dot_nt(e_all[:, :span], full[:, :, low:high].reshape(GROUPED, span)).astype(BF16)
        spare[...] = dot_nt(back, perm_h[...])
        sums = norm_backward(spare, H, 128, narrow(b, 1), unit_h.at[b, 0], slope_h.at[b, 0], spread_h.at[b, 0], keep_low)
        rows_n[6 * b + 1], rows_n[6 * b + 2], rows_n[6 * b + 0] = sums
        tall[:, :] = dot_tn(act_d[b], act_h[0])
        for i in range(OWNERS):
            for h in range(2):
                at = SHARD * (2 * i + h)
                low = WI_AT[b][h]
                grads[i, 0:SHARD, low : low + H] = tall[at : at + SHARD, :].astype(BF16)
                grads[i, SHARD:ROWS, low : low + H] = jnp.zeros((ROWS - SHARD, H), BF16)
                grads[i, :, low + H : low + 512] = jnp.zeros((ROWS, 512 - H), BF16)
        wide_back = dot_nt(act_h[0], w_in[b].astype(BF16))
        x_one[...] = wide_back

        def add_up(rows, dx):
            wide_grad[rows, :] += dx

        sums = norm_backward(x_one, D, 128, wide(b, 0), unit_d.at[b], slope_d.at[b], spread_d.at[b], add_up)
        rows_w[3 * b + 0], rows_w[3 * b + 1] = sums[0], sums[1]
    grad_tokens[...] = wide_grad[...].T
    for m in range(12):
        vec_n[m : m + 1, :] = rows_n[m]
    for m in range(6):
        vec_w[m : m + 1, :] = rows_w[m]
    low_n, low_w = vec_n[...].astype(BF16), vec_w[...].astype(BF16)
    lanes = slice(VEC_AT, VEC_AT + 128)
    for i in range(OWNERS):
        grads[i, 0:16, lanes] = dot_nt(low_n, put_n[i]).astype(BF16)
        for h in range(2):
            grads[i, 16 + 16 * h : 32 + 16 * h, lanes] = dot_nt(low_w, put_w[2 * i + h]).astype(BF16)

    @pl.when(lax.axis_index("dp") == 0)
    def _():
        slab = grads.at[own]

        def add(rows, lanes, value):
            slab[rows, lanes] = (slab[rows, lanes].astype(F32) + MOMENT_DECAY * value).astype(BF16)

        full_rows = slice(0, SHARD)
        add(full_rows, slice(CONV_AT, CONV_AT + 3200), mom_conv[...])
        for b in range(2):
            add(full_rows, slice(WO_AT[b], WO_AT[b] + D), mom_out[:, b, :])
            for h in range(2):
                at = WI_AT[b][h]
                add(full_rows, slice(at, at + H), mom_in[b, h * SHARD : (h + 1) * SHARD, :])
            for k in range(6):
                m = 6 * b + k
                add(slice(m, m + 1), slice(VEC_AT, VEC_AT + SHARD), mom_narrow[k, b : b + 1, :])
            for k in range(3):
                for h in range(2):
                    m = 16 + 16 * h + 3 * b + k
                    part = mom_wide[k, b : b + 1, h * SHARD : (h + 1) * SHARD]
                    add(slice(m, m + 1), slice(VEC_AT, VEC_AT + SHARD), part)


def compute(dilation, lengths, tokens, cotangent, full, moments):
    in_vmem = pl.BlockSpec(memory_space=pltpu.VMEM)
    in_smem = pl.BlockSpec(memory_space=pltpu.SMEM)
    return pl.pallas_call(
        compute_kernel,
        out_shape=(
            jax.ShapeDtypeStruct((D, TOK), BF16),
            jax.ShapeDtypeStruct((D, TOK), F32),
            jax.ShapeDtypeStruct((OWNERS, ROWS, COLS), BF16),
        ),
        in_specs=[in_smem] * 2 + [in_vmem] * 8,
        out_specs=(in_vmem,) * 3,
        scratch_shapes=[
            vmem((TOK, TOK), jnp.int32),
            vmem((H, GROUPED), BF16),
            vmem((16, D), F32),
            vmem((16, H), F32),
            vmem((2, D, H), F32),
            vmem((TOK, D), F32),
            vmem((TOK, D), F32),
            vmem((D, H), F32),
            vmem((2, TOK, D), BF16),
            vmem((2, TOK, H), BF16),
            vmem((2, 2, TOK, GROUPED), BF16),
            vmem((TOK, H), F32),
            vmem((TOK, 512), F32),
            vmem((TOK, H), F32),
            vmem((TOK, 2048), BF16),
            vmem((2, TOK, D), F32),
            vmem((2, TOK, D), F32),
            vmem((2, TOK, 128), F32),
            vmem((2, 2, TOK, H), F32),
            vmem((2, 2, TOK, H), F32),
            vmem((2, 2, TOK, 128), F32),
        ],
        compiler_params=pltpu.CompilerParams(vmem_limit_bytes=58 << 20),
        name="blocks",
    )(dilation, lengths, tokens, cotangent, full, *moments)


MATRICES = (
    dict(kind="out", pieces=(0,), piece=0, own=2, lanes=(0, D), scale=math.sqrt(D / H)),
    dict(kind="out", pieces=(1,), piece=1, own=1, lanes=(0, D), scale=math.sqrt(D / H)),
    dict(kind="conv", pieces=(2, 3, 4), piece=3, own=1, lanes=(0, 2000), scale=1.0),
    dict(kind="conv", pieces=(4, 5), piece=4, own=2, lanes=(208, 1408), scale=1.0),
    dict(kind="in", pieces=(5, 6), piece=6, own=2, lanes=(512, 1536), scale=1.0),
    dict(kind="in", pieces=(6, 7), piece=7, own=1, lanes=(640, 1664), scale=1.0),
)
WINDOW = 3 * PIECE
ROUTES = tuple((k, s, q) for k, m in enumerate(MATRICES) for s, q in enumerate(m["pieces"]))


def is_at(piece, own, matrix):
    return (piece == matrix["piece"]) & (own == matrix["own"])


def not_at(piece, own, matrix):
    return (piece != matrix["piece"]) | (own != matrix["own"])


def window_lanes(s):
    return pl.ds(s * PIECE, PIECE)


def greet_owners(barrier, base, piece, own):
    for k, s, q in ROUTES:
        matrix = MATRICES[k]
        there = (base + matrix["piece"], matrix["own"])

        @pl.when((piece == q) & not_at(piece, own, matrix))
        def _(there=there):
            pl.semaphore_signal(barrier, inc=1, device_id=there, device_id_type=MESH)

    for k, s, q in ROUTES:
        matrix = MATRICES[k]

        @pl.when(is_at(piece, own, matrix))
        def _(matrix=matrix, q=q):
            for i in range(OWNERS):
                if q != matrix["piece"] or i != matrix["own"]:
                    pl.semaphore_signal(barrier, inc=1, device_id=(base + q, i), device_id_type=MESH)


def owner_greetings(piece, own):
    count = jnp.int32(0)
    for k, s, q in ROUTES:
        matrix = MATRICES[k]
        holds = (piece == q) & not_at(piece, own, matrix)
        count = count + jnp.where(holds, 1, 0)
        count = count + jnp.where(is_at(piece, own, matrix), OWNERS - (1 if q == matrix["piece"] else 0), 0)
    return count


def reduce_kernel(
    extra, grads, moment, matrix_window,
    from_core, sums, from_x, from_y, last_x, last_y, from_z, from_far,
    core_send, core_recv, plane_send, plane_recv, z_send, z_recv, far_send, far_recv,
    gather_send, gather_recv, own_send, own_recv,
):
    base, piece, own = place()
    me = base + piece
    core, near_x, near_y = [(base + flip(piece, bit), own) for bit in (1, 2, 4)]
    column = [(me, other_owner(own, step)) for step in (1, 2, 3)]
    far = [(flip(me, bit), own) for bit in extra]
    barrier = greet([core, near_x, near_y] + column + far)
    greet_owners(barrier, base, piece, own)
    pl.semaphore_wait(barrier, 6 + len(extra) + owner_greetings(piece, own))

    parity = piece % 2
    at = piece // 2
    at_x, at_y, at_xy = flip(at, 1), flip(at, 2), 3 - at
    order = (at_xy, at_x, at_y, at)
    started = []

    def send(src, dst, sems, k, device):
        copy = remote(src, dst, sems[0].at[k], sems[1].at[k], device)
        copy.start()
        started.append(copy)
        return copy

    crossing = []
    for k, m in enumerate(order):
        theirs = grads.at[:, :, columns(2 * m + 1 - parity)]
        crossing.append(send(theirs, from_core.at[k], (core_send, core_recv), k, core))

    def merge(k, m):
        crossing[k].wait_recv()
        mine = grads[:, :, columns(2 * m + parity)].astype(F32)
        sums[k] = (mine + from_core[k].astype(F32)).astype(BF16)

    plane = (plane_send, plane_recv)
    low, high = pl.ds(0, 2), pl.ds(2, 2)
    merge(0, at_xy)
    one_x = send(sums.at[0, low], from_x.at[0], plane, 0, near_x)
    one_y = send(sums.at[0, high], from_y.at[0], plane, 1, near_y)
    merge(1, at_x)
    two_x = send(sums.at[1, low], from_x.at[1], plane, 2, near_x)
    merge(2, at_y)
    two_y = send(sums.at[2, high], from_y.at[1], plane, 3, near_y)
    merge(3, at)
    one_x.wait_recv()
    sums[2, 0:2] = (sums[2, 0:2].astype(F32) + from_x[0].astype(F32)).astype(BF16)
    three_y = send(sums.at[2, low], last_y, plane, 4, near_y)
    one_y.wait_recv()
    sums[1, 2:4] = (sums[1, 2:4].astype(F32) + from_y[0].astype(F32)).astype(BF16)
    three_x = send(sums.at[1, high], last_x, plane, 5, near_x)
    two_x.wait_recv()
    two_y.wait_recv()
    three_y.wait_recv()
    three_x.wait_recv()
    low_sum = sums[3, 0:2].astype(F32) + from_x[1].astype(F32) + last_y[...].astype(F32)
    high_sum = sums[3, 2:4].astype(F32) + from_y[1].astype(F32) + last_x[...].astype(F32)
    sums[3, 0:2] = low_sum.astype(BF16)
    sums[3, 2:4] = high_sum.astype(BF16)
    for k, device in enumerate(far):
        copy = remote(sums.at[3], from_far.at[k], far_send.at[k], far_recv.at[k], device)
        copy.start()
        copy.wait()
        sums[3] = (sums[3].astype(F32) + from_far[k].astype(F32)).astype(BF16)
    crossing = []
    for step in (1, 2, 3):
        there = other_owner(own, step)
        crossing.append(
            send(sums.at[3, there], from_z.at[step - 1], (z_send, z_recv), step - 1, column[step - 1])
        )
    total = sums[3, own].astype(F32)
    for step in (1, 2, 3):
        crossing[step - 1].wait_recv()
        total = total + from_z[step - 1].astype(F32)
    moment[:, columns(piece)] = total.astype(BF16)

    def view(q, part):
        return moment.at[part_rows(part), columns(q)]

    gather = Gather(view, gather_send, gather_recv, 0)
    gather.first()

    def to_owner(k, s, q):
        matrix = MATRICES[k]
        there = (base + matrix["piece"], matrix["own"])
        src = moment.at[:, columns(piece)]
        dst = matrix_window.at[own, :, window_lanes(s)]
        return remote(src, dst, own_send.at[k], own_recv.at[OWNERS * s + own], there)

    for k, s, q in ROUTES:
        matrix = MATRICES[k]

        @pl.when((piece == q) & not_at(piece, own, matrix))
        def _(k=k, s=s, q=q):
            to_owner(k, s, q).start()

        @pl.when((piece == q) & is_at(piece, own, matrix))
        def _(s=s):
            matrix_window[own, :, window_lanes(s)] = moment[:, columns(piece)]

    gather.second()
    gather.third()
    gather.last()
    for k, s, q in ROUTES:
        matrix = MATRICES[k]

        @pl.when((piece == q) & not_at(piece, own, matrix))
        def _(k=k, s=s, q=q):
            to_owner(k, s, q).wait_send()

        @pl.when(is_at(piece, own, matrix))
        def _(matrix=matrix, s=s, q=q):
            for i in range(OWNERS):
                if q != matrix["piece"] or i != matrix["own"]:
                    dst = matrix_window.at[i, :, window_lanes(s)]
                    src = moment.at[:, columns(piece)]
                    sems = (own_send.at[0], own_recv.at[OWNERS * s + i])
                    remote(src, dst, sems[0], sems[1], (base + q, i)).wait_recv()

    gather.finish()
    for copy in started:
        copy.wait_send()


def reduce_grads(grads, extra):
    in_vmem = pl.BlockSpec(memory_space=pltpu.VMEM)

    def dma(n):
        return pltpu.SemaphoreType.DMA((max(n, 1),))

    part = (OWNERS, ROWS, PIECE)
    half = (2, ROWS, PIECE)
    return pl.pallas_call(
        functools.partial(reduce_kernel, extra),
        out_shape=(
            jax.ShapeDtypeStruct((ROWS, COLS), BF16),
            jax.ShapeDtypeStruct((OWNERS, ROWS, WINDOW), BF16),
        ),
        in_specs=[in_vmem],
        out_specs=(in_vmem,) * 2,
        scratch_shapes=[
            vmem((4,) + part, BF16),
            vmem((4,) + part, BF16),
            vmem((2,) + half, BF16),
            vmem((2,) + half, BF16),
            vmem(half, BF16),
            vmem(half, BF16),
            vmem((3, ROWS, PIECE), BF16),
            vmem((max(len(extra), 1),) + part, BF16),
            dma(4), dma(4), dma(6), dma(6), dma(3), dma(3), dma(len(extra)), dma(len(extra)),
            dma(Gather.SEMS), dma(Gather.SEMS), dma(6), dma(12),
        ],
        compiler_params=pltpu.CompilerParams(
            collective_id=1, has_side_effects=True, vmem_limit_bytes=48 << 20
        ),
        name="reduce_grads",
    )(grads)


def split(a):
    high = a.astype(BF16)
    return high, (a - high.astype(F32)).astype(BF16)


def dot_fine(a, b):
    a_high, a_low = split(a)
    b_high, b_low = split(b)
    return dot(a_high, b_high) + (dot(a_high, b_low) + dot(a_low, b_high))


def dot_low(a, b):
    return dot(a.astype(BF16), b.astype(BF16))


def polynomial_of(gram):
    size = gram.shape[0]
    eye = iota((size, size), 0) == iota((size, size), 1)
    unit = jnp.where(eye, 1.0, 0.0)
    power = jnp.sum(jnp.sum(jnp.where(eye, gram, 0.0), axis=1, keepdims=True), axis=0, keepdims=True)
    inverse = 1.0 / (jnp.sqrt(power) + NORM_FLOOR)
    current = gram * inverse * inverse
    result = None
    for step in range(NS_STEPS):
        square = dot_fine if step > 2 else dot_low
        poly = COEF_A * unit + COEF_B * current + COEF_C * square(current, current)
        result = poly if result is None else dot_low(poly, result)
        if step < NS_STEPS - 1:
            first = dot_fine if step < 2 else dot_low
            second = dot_fine if step < 1 else dot_low
            current = second(first(poly, current), poly)
    return result, inverse


def ortho_kernel(window, update, gram, poly):
    piece, own = lax.axis_index("dp") % PIECES, lax.axis_index("fsdp")
    owner = {"out": False, "conv": False, "in": False}
    low, high, factor = jnp.int32(0), jnp.int32(0), jnp.float32(0)
    for matrix in MATRICES:
        here = is_at(piece, own, matrix)
        owner[matrix["kind"]] = owner[matrix["kind"]] | here
        low = jnp.where(here, matrix["lanes"][0], low)
        high = jnp.where(here, matrix["lanes"][1], high)
        factor = jnp.where(here, MATRIX_RATE * matrix["scale"], factor)

    def half(h):
        return pl.ds(pl.multiple_of(low + 512 * h, 128), 512)

    def conv_part(k, width):
        lanes = pl.ds(pl.multiple_of(k * width, width), width)
        values = window[:, :, lanes].reshape(GROUPED, width)
        lane = iota((GROUPED, width), 1) + k * width
        return lanes, jnp.where((lane >= low) & (lane < high), values, jnp.zeros((), BF16))

    @pl.when(owner["in"])
    def _():
        a = window[:, :, half(0)].reshape(GROUPED, 512)
        b = window[:, :, half(1)].reshape(GROUPED, 512)
        gram[...] = dot_tn(a, a) + dot_tn(b, b)

    @pl.when(owner["out"])
    def _():
        gram[...] = jnp.zeros(gram.shape, F32)
        a = window[:, :, :PIECE].reshape(GROUPED, PIECE)
        gram[:GROUPED, :GROUPED] = dot_nt(a, a)

    @pl.when(owner["conv"])
    def _():
        gram[...] = jnp.zeros(gram.shape, F32)

        def body(k, carry):
            values = conv_part(k, 512)[1]
            gram[:GROUPED, :GROUPED] += dot_nt(values, values)
            return carry

        lax.fori_loop(0, 4, body, 0)

    @pl.when(owner["in"] | owner["out"] | owner["conv"])
    def _():
        result, inverse = polynomial_of(gram[...])
        poly[...] = (result * (inverse * factor)).astype(BF16)

    @pl.when(owner["in"])
    def _():
        update[...] = jnp.zeros(update.shape, BF16)
        for h in range(2):
            step = dot(window[:, :, half(h)].reshape(GROUPED, 512), poly[...])
            update[:, :, half(h)] = step.astype(BF16).reshape(OWNERS, ROWS, 512)

    @pl.when(owner["out"])
    def _():
        step = dot(poly[:GROUPED, :GROUPED], window[:, :, :PIECE].reshape(GROUPED, PIECE))
        update[:, :, :PIECE] = step.astype(BF16).reshape(OWNERS, ROWS, PIECE)

    @pl.when(owner["conv"])
    def _():
        update[:, :, 2048:] = jnp.zeros((OWNERS, ROWS, WINDOW - 2048), BF16)

        def body(k, carry):
            lanes, values = conv_part(k, 512)
            step = dot(poly[:GROUPED, :GROUPED], values)
            update[:, :, lanes] = step.astype(BF16).reshape(OWNERS, ROWS, 512)
            return carry

        lax.fori_loop(0, 4, body, 0)


def orthogonalize(window):
    in_vmem = pl.BlockSpec(memory_space=pltpu.VMEM)
    return pl.pallas_call(
        ortho_kernel,
        out_shape=jax.ShapeDtypeStruct(window.shape, BF16),
        in_specs=[in_vmem],
        out_specs=in_vmem,
        scratch_shapes=[vmem((512, 512), F32), vmem((512, 512), BF16)],
        compiler_params=pltpu.CompilerParams(vmem_limit_bytes=48 << 20),
        name="orthogonalize",
    )(window)


def slot_of(k, q):
    return sum(1 for j, s, other in ROUTES if other == q and j < k)


def spread_kernel(window, update, parts, send, recv, gather_send, gather_recv):
    base, piece, own = place()
    barrier = greet([(base + flip(piece, bit), own) for bit in (1, 2, 4)])
    greet_owners(barrier, base, piece, own)
    pl.semaphore_wait(barrier, 3 + owner_greetings(piece, own))

    def outgoing(s, q, slot, i):
        src = window.at[i, :, window_lanes(s)]
        return remote(src, parts.at[slot], send.at[OWNERS * s + i], recv.at[slot], (base + q, i))

    for k, s, q in ROUTES:
        matrix = MATRICES[k]
        slot = slot_of(k, q)

        @pl.when(is_at(piece, own, matrix))
        def _(matrix=matrix, s=s, q=q, slot=slot):
            for i in range(OWNERS):
                if q != matrix["piece"] or i != matrix["own"]:
                    outgoing(s, q, slot, i).start()
                else:
                    parts[slot] = window[i, :, window_lanes(s)]

    for k, s, q in ROUTES:
        matrix = MATRICES[k]
        slot = slot_of(k, q)

        @pl.when((piece == q) & not_at(piece, own, matrix))
        def _(matrix=matrix, slot=slot):
            there = (base + matrix["piece"], matrix["own"])
            remote(window.at[0, :, window_lanes(0)], parts.at[slot], send.at[0], recv.at[slot], there).wait_recv()

    shared = [q for q in range(PIECES) if sum(1 for r in ROUTES if r[2] == q) == 2]
    update[:, columns(piece)] = parts[0]
    for q in shared:

        @pl.when(piece == q)
        def _():
            update[:, columns(piece)] = parts[0] + parts[1]

    def view(q, part):
        return update.at[part_rows(part), columns(q)]

    gather = Gather(view, gather_send, gather_recv, 0)
    gather.first()
    gather.second()
    gather.third()
    gather.last()
    gather.finish()
    for k, s, q in ROUTES:
        matrix = MATRICES[k]

        @pl.when(is_at(piece, own, matrix))
        def _(matrix=matrix, s=s, q=q):
            for i in range(OWNERS):
                if q != matrix["piece"] or i != matrix["own"]:
                    outgoing(s, q, 0, i).wait_send()


def spread_steps(window):
    in_vmem = pl.BlockSpec(memory_space=pltpu.VMEM)

    def dma(n):
        return pltpu.SemaphoreType.DMA((n,))

    return pl.pallas_call(
        spread_kernel,
        out_shape=jax.ShapeDtypeStruct((ROWS, COLS), BF16),
        in_specs=[in_vmem],
        out_specs=in_vmem,
        scratch_shapes=[
            vmem((2, ROWS, PIECE), BF16),
            dma(12), dma(2), dma(Gather.SEMS), dma(Gather.SEMS),
        ],
        compiler_params=pltpu.CompilerParams(
            collective_id=2, has_side_effects=True, vmem_limit_bytes=40 << 20
        ),
        name="spread_steps",
    )(window)


def finish_kernel(
    vector_step, moment, update, conv, w_in, w_out, wide, narrow,
    mom_in, mom_conv, mom_out, mom_wide, mom_narrow,
    new_in, new_conv, new_out, new_wide, new_narrow, low_in, low_conv, low_out,
):
    lanes = slice(CONV_AT, CONV_AT + 3200)
    mom_conv[...] = moment[:SHARD, lanes].astype(F32)
    value = conv[...] - update[:SHARD, lanes].astype(F32)
    new_conv[...] = value
    low_conv[...] = value.astype(BF16)
    for b in range(2):
        lanes = slice(WO_AT[b], WO_AT[b] + D)
        mom_out[:, b, :] = moment[:SHARD, lanes].astype(F32)
        value = w_out[:, b, :] - update[:SHARD, lanes].astype(F32)
        new_out[:, b, :] = value
        low_out[b] = value.astype(BF16)
        for h in range(2):
            lanes = slice(WI_AT[b][h], WI_AT[b][h] + H)
            rows = slice(h * SHARD, (h + 1) * SHARD)
            mom_in[b, rows, :] = moment[:SHARD, lanes].astype(F32)
            value = w_in[b, rows, :] - update[:SHARD, lanes].astype(F32)
            new_in[b, rows, :] = value
            low_in[b, rows, :] = value.astype(BF16)
        lanes = slice(VEC_AT, VEC_AT + SHARD)
        vectors = moment[:, VEC_AT : VEC_AT + 128].astype(F32)
        for k in range(6):
            m = 6 * b + k
            value = vectors[m : m + 1, :SHARD]
            mom_narrow[k, b : b + 1, :] = value
            new_narrow[k, b : b + 1, :] = narrow[k, b : b + 1, :] - vector_step * value
        for k in range(3):
            for h in range(2):
                m = 16 + 16 * h + 3 * b + k
                lanes = slice(h * SHARD, (h + 1) * SHARD)
                value = vectors[m : m + 1, :SHARD]
                mom_wide[k, b : b + 1, lanes] = value
                new_wide[k, b : b + 1, lanes] = wide[k, b : b + 1, lanes] - vector_step * value


def finish(vector_step, moment, update, conv, w_in, w_out, wide, narrow):
    in_vmem = pl.BlockSpec(memory_space=pltpu.VMEM)
    shapes = [w_in.shape, conv.shape, w_out.shape, wide.shape, narrow.shape]
    outs = [jax.ShapeDtypeStruct(s, F32) for s in shapes + shapes]
    outs += [jax.ShapeDtypeStruct(s, BF16) for s in shapes[:2] + [(2, SHARD, D)]]
    return pl.pallas_call(
        functools.partial(finish_kernel, vector_step),
        out_shape=tuple(outs),
        in_specs=[in_vmem] * 7,
        out_specs=(in_vmem,) * len(outs),
        compiler_params=pltpu.CompilerParams(vmem_limit_bytes=40 << 20),
        name="finish",
    )(moment, update, conv, w_in, w_out, wide, narrow)


def shards(
    extra, vector_step, tokens, cotangent, lengths, dilation, proj_in, conv_weight, proj_out, vec_wide, vec_narrow,
    mom_in, mom_conv, mom_out, mom_wide, mom_narrow,
):
    proj_out, vec_wide, vec_narrow = swap(proj_out), swap(vec_wide), swap(vec_narrow)
    moments = (mom_conv, mom_in, swap(mom_out), swap(mom_wide), swap(mom_narrow))
    full = gather_weights(conv_weight, proj_in, proj_out, vec_wide, vec_narrow)
    out, grad_tokens, grads = compute(dilation, lengths, tokens.T, cotangent.T, full, moments)
    moment, window = reduce_grads(grads, extra)
    update = spread_steps(orthogonalize(window))
    rest = list(finish(vector_step, moment, update, conv_weight, proj_in, proj_out, vec_wide, vec_narrow))
    for k in (2, 3, 4, 7, 8, 9):
        rest[k] = swap(rest[k])
    return (out.T, grad_tokens.T) + tuple(rest)


def swap(array):
    return jnp.transpose(array, (1, 0, 2))


def solution(mesh):
    groups, owners = mesh.shape["dp"], mesh.shape["fsdp"]
    assert owners == OWNERS and groups % PIECES == 0
    extra, bit = [], PIECES
    while bit < groups:
        extra.append(bit)
        bit *= 2
    assert bit == groups
    vector_step = VECTOR_RATE / math.sqrt(TOK * groups * owners)
    tok, rep = P(("dp", "fsdp"), None), P()
    mid, first, final = P(None, "fsdp", None), P("fsdp", None), P(None, None, "fsdp")
    params = (mid, first, mid, final, final)
    return jax.shard_map(
        functools.partial(shards, tuple(extra), vector_step),
        mesh=mesh,
        in_specs=(tok, tok, tok, rep) + params + params,
        out_specs=(tok, tok) + params + params + (mid, first, mid),
        check_vma=False,
    )
```

```python
import functools
import math

import jax
import jax.numpy as jnp
from jax import lax
from jax.experimental import pallas as pl
from jax.experimental.pallas import tpu as pltpu
from jax.sharding import PartitionSpec as P

D = 800
H = 400
K_ENC = 5
K_DEC = 3
NS_STEPS = 5
EPSILON = 1e-05
NORM_FLOOR = 1e-07
COEF_A = 3.4445
COEF_B = -4.775
COEF_C = 2.0315
MOMENT_DECAY = 0.5
MATRIX_RATE = 0.5
VECTOR_RATE = 0.1

F32 = jnp.float32
BF16 = jnp.bfloat16
MESH = pl.DeviceIdType.MESH

OWNERS = 4
PIECES = 8
SHARD = 100
ROWS = 112
PIECE = 896
COLS = PIECES * PIECE
WO_AT = (0, 896)
CONV_AT = 1792
WI_AT = ((4992, 5504), (6016, 6528))
VEC_AT = 7040
SPLIT = K_ENC * H
TOK = 256
GROUPED = OWNERS * ROWS

GELU_K = math.sqrt(2.0 / math.pi)
GELU_C = 0.044715


def vmem(shape, dtype):
    return pltpu.VMEM(shape, dtype)


def dot(a, b):
    return lax.dot_general(a, b, (((1,), (0,)), ((), ())), preferred_element_type=F32)


def dot_nt(a, b):
    return lax.dot_general(a, b, (((1,), (1,)), ((), ())), preferred_element_type=F32)


def dot_tn(a, b):
    return lax.dot_general(a, b, (((0,), (0,)), ((), ())), preferred_element_type=F32)


def one_hot(mask):
    return jnp.where(mask, 1.0, 0.0).astype(BF16)


def pack(slab, conv, w_in, w_out, wide, narrow):
    slab[...] = jnp.zeros((ROWS, COLS), BF16)
    slab[:SHARD, CONV_AT : CONV_AT + 3200] = conv[...].astype(BF16)
    for b in range(2):
        slab[:SHARD, WO_AT[b] : WO_AT[b] + D] = w_out[:, b, :].astype(BF16)
        for h in range(2):
            at = WI_AT[b][h]
            slab[:SHARD, at : at + H] = w_in[b, h * SHARD : (h + 1) * SHARD, :].astype(BF16)
    for b in range(2):
        for k in range(6):
            m = 6 * b + k
            slab[m : m + 1, VEC_AT : VEC_AT + SHARD] = narrow[k, b : b + 1, :].astype(BF16)
        for k in range(3):
            for h in range(2):
                m = 16 + 16 * h + 3 * b + k
                part = wide[k, b : b + 1, h * SHARD : (h + 1) * SHARD]
                slab[m : m + 1, VEC_AT : VEC_AT + SHARD] = part.astype(BF16)


def place():
    at = lax.axis_index("dp")
    piece = at % PIECES
    return at - piece, piece, lax.axis_index("fsdp")


def flip(value, bit):
    return value + bit - 2 * bit * ((value // bit) % 2)


def other_owner(own, step):
    if step == 3:
        return 3 - own
    return flip(own, step)


def columns(piece):
    return pl.ds(pl.multiple_of(piece * PIECE, PIECE), PIECE)


def remote(src, dst, send, recv, device):
    return pltpu.make_async_remote_copy(
        src_ref=src,
        dst_ref=dst,
        send_sem=send,
        recv_sem=recv,
        device_id=device,
        device_id_type=MESH,
    )


def greet(devices):
    barrier = pltpu.get_barrier_semaphore()
    for device in devices:
        pl.semaphore_signal(barrier, inc=1, device_id=device, device_id_type=MESH)
    return barrier


class Gather:
    SEMS = 10

    def __init__(self, view, send, recv, at):
        base, piece, own = place()
        self.view, self.send, self.recv, self.at = view, send, recv, at
        self.piece = piece
        self.near = {bit: (base + flip(piece, bit), own) for bit in (1, 2, 4)}
        self.started = []

    def copy(self, bit, q, part, k):
        ref = self.view(q, part)
        sems = (self.send.at[self.at + k], self.recv.at[self.at + k])
        return remote(ref, ref, sems[0], sems[1], self.near[bit])

    def start(self, bit, q, part, k):
        copy = self.copy(bit, q, part, k)
        copy.start()
        self.started.append(copy)

    def first(self):
        p = self.piece
        self.start(4, p, 0, 0)
        self.start(2, p, 1, 1)

    def second(self):
        p = self.piece
        for k in (0, 1):
            self.started[k].wait_recv()
        self.start(2, p, 0, 2)
        self.start(2, flip(p, 4), 0, 3)
        self.start(4, p, 1, 4)
        self.start(4, flip(p, 2), 1, 5)
        self.start(1, p, None, 6)

    def third(self):
        p = self.piece
        for k in (2, 3, 4, 5):
            self.started[k].wait_recv()
        self.start(1, flip(p, 2), None, 7)
        self.start(1, flip(p, 4), None, 8)
        self.start(1, flip(flip(p, 2), 4), None, 9)

    def last(self):
        for k in (6, 7, 8, 9):
            self.started[k].wait_recv()

    def finish(self):
        for copy in self.started:
            copy.wait_send()


def part_rows(part):
    if part is None:
        return pl.ds(0, ROWS)
    return pl.ds(0, 64) if part == 0 else pl.ds(64, 48)


def gather_kernel(conv, w_in, w_out, wide, narrow, full, z_send, z_recv, send, recv):
    base, piece, own = place()
    me = base + piece
    near = [(base + flip(piece, bit), own) for bit in (1, 2, 4)]
    column = [(me, other_owner(own, step)) for step in (1, 2, 3)]
    barrier = greet(near + column)
    pack(full.at[own], conv, w_in, w_out, wide, narrow)
    pl.semaphore_wait(barrier, 6)
    mine = full.at[own, :, columns(piece)]
    crossing = []
    for step in (1, 2, 3):
        copy = remote(mine, mine, z_send.at[step - 1], z_recv.at[step - 1], column[step - 1])
        copy.start()
        crossing.append(copy)
    gathers = []
    for step in (1, 2, 3):
        there = other_owner(own, step)

        def view(q, part, there=there):
            return full.at[there, part_rows(part), columns(q)]

        gathers.append(Gather(view, send, recv, (step - 1) * Gather.SEMS))
    for step in (1, 2, 3):
        crossing[step - 1].wait_recv()
        gathers[step - 1].first()
    for one in gathers:
        one.second()
    for one in gathers:
        one.third()
    for one in gathers:
        one.last()
    for one in gathers:
        one.finish()
    for copy in crossing:
        copy.wait_send()


def norm_forward(src, width, chunk, gain, shift, act, unit, slope, spread):
    def body(k, carry):
        rows = pl.ds(pl.multiple_of(k * chunk, chunk), chunk)
        x = src[rows, :width].astype(F32)
        center = x - jnp.mean(x, axis=1, keepdims=True)
        scale = lax.rsqrt(jnp.mean(center * center, axis=1, keepdims=True) + EPSILON)
        xhat = center * scale
        a = xhat * gain + shift
        square = a * a
        half = 0.5 + 0.5 * jnp.tanh(a * (GELU_K + (GELU_K * GELU_C) * square))
        act[rows, :width] = (a * half).astype(BF16)
        unit[rows, :width] = xhat
        inner = GELU_K + (3.0 * GELU_K * GELU_C) * square
        slope[rows, :width] = half + (2.0 * a * inner) * (half * (1.0 - half))
        spread[rows, :] = jnp.broadcast_to(scale, (chunk, 128))
        return carry

    lax.fori_loop(0, TOK // chunk, body, 0)


def fold_rows(values):
    total = values[0:8]
    for k in range(1, values.shape[0] // 8):
        total = total + values[8 * k : 8 * k + 8]
    return total


def norm_backward(grad, width, chunk, gain, unit, slope, spread, finish):
    def body(k, sums):
        rows = pl.ds(pl.multiple_of(k * chunk, chunk), chunk)
        da = grad[rows, :width] * slope[rows, :width]
        xhat = unit[rows, :width]
        product = da * xhat
        dxhat = da * gain
        mean_one = jnp.mean(dxhat, axis=1, keepdims=True)
        mean_two = jnp.mean(dxhat * xhat, axis=1, keepdims=True)
        dx = spread[rows, 0:1] * (dxhat - mean_one - xhat * mean_two)
        finish(rows, dx)
        return (sums[0] + fold_rows(product), sums[1] + fold_rows(da), sums[2] + fold_rows(dx))

    zero = jnp.zeros((8, width), F32)
    sums = lax.fori_loop(0, TOK // chunk, body, (zero, zero, zero))
    return tuple(jnp.sum(s, axis=0, keepdims=True) for s in sums)


def iota(shape, dim):
    return lax.broadcasted_iota(jnp.int32, shape, dim)


def compute_kernel(
    dilation, lengths, tokens, cotangent, conv, in_shard, out_shard, wide_shard, narrow_shard,
    mom_conv, mom_in, mom_out, mom_wide, mom_narrow,
    out, grad_tokens, grads,
    full, z_send, z_recv, send, recv, far, perm_h, vec_w, vec_n, w_in, x_one, wide_grad, tall,
    act_d, act_h, act_g, hid, conv_in, spare, e_all,
    unit_d, slope_d, spread_d, unit_h, slope_h, spread_h,
):
    gather_kernel(
        conv, in_shard, out_shard, wide_shard, narrow_shard, full, z_send, z_recv, send, recv
    )
    own = lax.axis_index("fsdp")
    row, col = iota((TOK, TOK), 0), iota((TOK, TOK), 1)
    seg_row, seg_col = jnp.zeros((TOK, TOK), jnp.int32), jnp.zeros((TOK, TOK), jnp.int32)
    end = jnp.int32(0)
    for k in range(8):
        end = end + lengths[0, k]
        seg_row = seg_row + jnp.where(row >= end, 1, 0)
        seg_col = seg_col + jnp.where(col >= end, 1, 0)
    far[...] = jnp.where(seg_row == seg_col, col - row, 4 * TOK)

    def mover(offset):
        return one_hot(far[...] == offset)

    row, col = iota((H, GROUPED), 0), iota((H, GROUPED), 1)
    group = jnp.where(col >= ROWS, 1, 0) + jnp.where(col >= 2 * ROWS, 1, 0) + jnp.where(col >= 3 * ROWS, 1, 0)
    used = col - ROWS * group < SHARD
    perm_h[...] = one_hot((row == col - (ROWS - SHARD) * group) & used)

    row_n, col_n = iota((128, H), 0), iota((128, H), 1)
    row_w, col_w = iota((128, D), 0), iota((128, D), 1)
    total_n, total_w = jnp.zeros((16, H), F32), jnp.zeros((16, D), F32)
    put_n, put_w = [], []
    for i in range(OWNERS):
        lanes = slice(VEC_AT, VEC_AT + 128)
        put_n.append(one_hot((col_n == row_n + SHARD * i) & (row_n < SHARD)))
        total_n = total_n + dot(full[i, 0:16, lanes], put_n[i])
        for h in range(2):
            put_w.append(one_hot((col_w == row_w + SHARD * (2 * i + h)) & (row_w < SHARD)))
            total_w = total_w + dot(full[i, 16 + 16 * h : 32 + 16 * h, lanes], put_w[2 * i + h])
    vec_n[...] = total_n
    vec_w[...] = total_w

    def narrow(b, k):
        return vec_n[6 * b + k : 6 * b + k + 1, :]

    def wide(b, k):
        return vec_w[3 * b + k : 3 * b + k + 1, :]

    def weight_out(b):
        return full[:, :, WO_AT[b] : WO_AT[b] + D].reshape(GROUPED, D)

    for b in range(2):
        for i in range(OWNERS):
            for h in range(2):
                at = SHARD * (2 * i + h)
                lanes = slice(WI_AT[b][h], WI_AT[b][h] + H)
                w_in[b, at : at + SHARD, :] = full[i, 0:SHARD, lanes].astype(F32)

    def taps(b):
        if b == 0:
            return [(H * j, (j - K_ENC // 2) * dilation[0]) for j in range(K_ENC)]
        return [(SPLIT + H * j, -j * dilation[1]) for j in range(K_DEC)]

    def window(at):
        return at - at % 128

    x_one[...] = tokens[...].astype(F32).T
    for b in range(2):
        norm_forward(x_one, D, 128, wide(b, 0), wide(b, 1), act_d.at[b], unit_d.at[b], slope_d.at[b], spread_d.at[b])
        hid[:, :] = dot(act_d[b], w_in[b].astype(BF16)) + narrow(b, 0)
        norm_forward(hid, H, 128, narrow(b, 1), narrow(b, 2), act_h.at[0], unit_h.at[b, 0], slope_h.at[b, 0], spread_h.at[b, 0])
        act_g[b, 0] = dot(act_h[0], perm_h[...]).astype(BF16)
        for j, (at, offset) in enumerate(taps(b)):
            moved = dot(mover(offset), act_g[b, 0]).astype(BF16)
            low = CONV_AT + window(at)
            product = dot(moved, full[:, :, low : low + 512].reshape(GROUPED, 512))
            if at % 128:
                product = pltpu.roll(product, 512 - at % 128, 1)
            if j == 0:
                conv_in[...] = product
            else:
                conv_in[...] += product
        conv_in[:, :H] += narrow(b, 3)
        norm_forward(conv_in, H, 128, narrow(b, 4), narrow(b, 5), act_h.at[1], unit_h.at[b, 1], slope_h.at[b, 1], spread_h.at[b, 1])
        act_g[b, 1] = dot(act_h[1], perm_h[...]).astype(BF16)
        result = (x_one[...] + dot(act_g[b, 1], weight_out(b))) + wide(b, 2)
        if b == 0:
            x_one[...] = result
        else:
            out[...] = result.T.astype(BF16)

    grads[:, :, VEC_AT : VEC_AT + 128] = jnp.zeros((OWNERS, ROWS, 128), BF16)
    rows_w, rows_n = [None] * 6, [None] * 12
    for b in (1, 0):
        if b == 1:
            wide_grad[...] = cotangent[...].astype(F32).T
        rows_w[3 * b + 2] = jnp.sum(wide_grad[...], axis=0, keepdims=True)
        e3 = wide_grad[...].astype(BF16)
        grads[:, :, WO_AT[b] : WO_AT[b] + D] = dot_tn(act_g[b, 1], e3).astype(BF16).reshape(OWNERS, ROWS, D)
        grads[:, :, WO_AT[b] + D : WO_AT[b] + PIECE] = jnp.zeros((OWNERS, ROWS, PIECE - D), BF16)
        back = dot_nt(e3, weight_out(b)).astype(BF16)
        spare[...] = dot_nt(back, perm_h[...])

        def keep_low(rows, dx):
            act_h[0, rows, :] = dx.astype(BF16)

        sums = norm_backward(spare, H, 128, narrow(b, 4), unit_h.at[b, 1], slope_h.at[b, 1], spread_h.at[b, 1], keep_low)
        rows_n[6 * b + 4], rows_n[6 * b + 5], rows_n[6 * b + 3] = sums
        low_at, high_at = (1920, 3200) if b == 1 else (0, 2048)
        span = high_at - low_at
        e_all[:, :span] = jnp.zeros((TOK, span), BF16)
        for at, offset in taps(b):
            moved = dot(mover(-offset), act_h[0])
            moved = jnp.concatenate([moved, jnp.zeros((TOK, 512 - H), F32)], axis=1)
            if at % 128:
                moved = pltpu.roll(moved, at % 128, 1)
            low = window(at) - low_at
            e_all[:, low : low + 512] += moved.astype(BF16)
        piece = dot_tn(act_g[b, 0], e_all[:, :span]).astype(BF16).reshape(OWNERS, ROWS, span)
        low, high = CONV_AT + low_at, CONV_AT + high_at
        if b == 1:
            grads[:, :, low:high] = piece
        else:
            grads[:, :, low : high - 128] = piece[:, :, : span - 128]
            grads[:, :, high - 128 : high] += piece[:, :, span - 128 :]
        back = dot_nt(e_all[:, :span], full[:, :, low:high].reshape(GROUPED, span)).astype(BF16)
        spare[...] = dot_nt(back, perm_h[...])
        sums = norm_backward(spare, H, 128, narrow(b, 1), unit_h.at[b, 0], slope_h.at[b, 0], spread_h.at[b, 0], keep_low)
        rows_n[6 * b + 1], rows_n[6 * b + 2], rows_n[6 * b + 0] = sums
        tall[:, :] = dot_tn(act_d[b], act_h[0])
        for i in range(OWNERS):
            for h in range(2):
                at = SHARD * (2 * i + h)
                low = WI_AT[b][h]
                grads[i, 0:SHARD, low : low + H] = tall[at : at + SHARD, :].astype(BF16)
                grads[i, SHARD:ROWS, low : low + H] = jnp.zeros((ROWS - SHARD, H), BF16)
                grads[i, :, low + H : low + 512] = jnp.zeros((ROWS, 512 - H), BF16)
        wide_back = dot_nt(act_h[0], w_in[b].astype(BF16))
        x_one[...] = wide_back

        def add_up(rows, dx):
            wide_grad[rows, :] += dx

        sums = norm_backward(x_one, D, 128, wide(b, 0), unit_d.at[b], slope_d.at[b], spread_d.at[b], add_up)
        rows_w[3 * b + 0], rows_w[3 * b + 1] = sums[0], sums[1]
    grad_tokens[...] = wide_grad[...].T
    for m in range(12):
        vec_n[m : m + 1, :] = rows_n[m]
    for m in range(6):
        vec_w[m : m + 1, :] = rows_w[m]
    low_n, low_w = vec_n[...].astype(BF16), vec_w[...].astype(BF16)
    lanes = slice(VEC_AT, VEC_AT + 128)
    for i in range(OWNERS):
        grads[i, 0:16, lanes] = dot_nt(low_n, put_n[i]).astype(BF16)
        for h in range(2):
            grads[i, 16 + 16 * h : 32 + 16 * h, lanes] = dot_nt(low_w, put_w[2 * i + h]).astype(BF16)

    @pl.when(lax.axis_index("dp") == 0)
    def _():
        slab = grads.at[own]

        def add(rows, lanes, value):
            slab[rows, lanes] = (slab[rows, lanes].astype(F32) + MOMENT_DECAY * value).astype(BF16)

        full_rows = slice(0, SHARD)
        add(full_rows, slice(CONV_AT, CONV_AT + 3200), mom_conv[...])
        for b in range(2):
            add(full_rows, slice(WO_AT[b], WO_AT[b] + D), mom_out[:, b, :])
            for h in range(2):
                at = WI_AT[b][h]
                add(full_rows, slice(at, at + H), mom_in[b, h * SHARD : (h + 1) * SHARD, :])
            for k in range(6):
                m = 6 * b + k
                add(slice(m, m + 1), slice(VEC_AT, VEC_AT + SHARD), mom_narrow[k, b : b + 1, :])
            for k in range(3):
                for h in range(2):
                    m = 16 + 16 * h + 3 * b + k
                    part = mom_wide[k, b : b + 1, h * SHARD : (h + 1) * SHARD]
                    add(slice(m, m + 1), slice(VEC_AT, VEC_AT + SHARD), part)


def compute(dilation, lengths, tokens, cotangent, params, moments):
    in_vmem = pl.BlockSpec(memory_space=pltpu.VMEM)
    in_smem = pl.BlockSpec(memory_space=pltpu.SMEM)
    return pl.pallas_call(
        compute_kernel,
        out_shape=(
            jax.ShapeDtypeStruct((D, TOK), BF16),
            jax.ShapeDtypeStruct((D, TOK), F32),
            jax.ShapeDtypeStruct((OWNERS, ROWS, COLS), BF16),
        ),
        in_specs=[in_smem] * 2 + [in_vmem] * 12,
        out_specs=(in_vmem,) * 3,
        scratch_shapes=[
            vmem((OWNERS, ROWS, COLS), BF16),
            pltpu.SemaphoreType.DMA((3,)),
            pltpu.SemaphoreType.DMA((3,)),
            pltpu.SemaphoreType.DMA((3 * Gather.SEMS,)),
            pltpu.SemaphoreType.DMA((3 * Gather.SEMS,)),
            vmem((TOK, TOK), jnp.int32),
            vmem((H, GROUPED), BF16),
            vmem((16, D), F32),
            vmem((16, H), F32),
            vmem((2, D, H), F32),
            vmem((TOK, D), F32),
            vmem((TOK, D), F32),
            vmem((D, H), F32),
            vmem((2, TOK, D), BF16),
            vmem((2, TOK, H), BF16),
            vmem((2, 2, TOK, GROUPED), BF16),
            vmem((TOK, H), F32),
            vmem((TOK, 512), F32),
            vmem((TOK, H), F32),
            vmem((TOK, 2048), BF16),
            vmem((2, TOK, D), F32),
            vmem((2, TOK, D), F32),
            vmem((2, TOK, 128), F32),
            vmem((2, 2, TOK, H), F32),
            vmem((2, 2, TOK, H), F32),
            vmem((2, 2, TOK, 128), F32),
        ],
        compiler_params=pltpu.CompilerParams(
            collective_id=0, has_side_effects=True, vmem_limit_bytes=58 << 20
        ),
        name="blocks",
    )(dilation, lengths, tokens, cotangent, *params, *moments)


MATRICES = (
    dict(kind="out", pieces=(0,), piece=0, own=2, lanes=(0, D), scale=math.sqrt(D / H)),
    dict(kind="out", pieces=(1,), piece=1, own=1, lanes=(0, D), scale=math.sqrt(D / H)),
    dict(kind="conv", pieces=(2, 3, 4), piece=3, own=1, lanes=(0, 2000), scale=1.0),
    dict(kind="conv", pieces=(4, 5), piece=4, own=2, lanes=(208, 1408), scale=1.0),
    dict(kind="in", pieces=(5, 6), piece=6, own=2, lanes=(512, 1536), scale=1.0),
    dict(kind="in", pieces=(6, 7), piece=7, own=1, lanes=(640, 1664), scale=1.0),
)
WINDOW = 3 * PIECE
ROUTES = tuple((k, s, q) for k, m in enumerate(MATRICES) for s, q in enumerate(m["pieces"]))


def is_at(piece, own, matrix):
    return (piece == matrix["piece"]) & (own == matrix["own"])


def not_at(piece, own, matrix):
    return (piece != matrix["piece"]) | (own != matrix["own"])


def window_lanes(s):
    return pl.ds(s * PIECE, PIECE)


def greet_owners(barrier, base, piece, own):
    for k, s, q in ROUTES:
        matrix = MATRICES[k]
        there = (base + matrix["piece"], matrix["own"])

        @pl.when((piece == q) & not_at(piece, own, matrix))
        def _(there=there):
            pl.semaphore_signal(barrier, inc=1, device_id=there, device_id_type=MESH)

    for k, s, q in ROUTES:
        matrix = MATRICES[k]

        @pl.when(is_at(piece, own, matrix))
        def _(matrix=matrix, q=q):
            for i in range(OWNERS):
                if q != matrix["piece"] or i != matrix["own"]:
                    pl.semaphore_signal(barrier, inc=1, device_id=(base + q, i), device_id_type=MESH)


def owner_greetings(piece, own):
    count = jnp.int32(0)
    for k, s, q in ROUTES:
        matrix = MATRICES[k]
        holds = (piece == q) & not_at(piece, own, matrix)
        count = count + jnp.where(holds, 1, 0)
        count = count + jnp.where(is_at(piece, own, matrix), OWNERS - (1 if q == matrix["piece"] else 0), 0)
    return count


def reduce_kernel(
    extra, grads, moment, matrix_window,
    from_core, sums, from_x, from_y, last_x, last_y, from_z, from_far,
    core_send, core_recv, plane_send, plane_recv, z_send, z_recv, far_send, far_recv,
    gather_send, gather_recv, own_send, own_recv,
):
    base, piece, own = place()
    me = base + piece
    core, near_x, near_y = [(base + flip(piece, bit), own) for bit in (1, 2, 4)]
    column = [(me, other_owner(own, step)) for step in (1, 2, 3)]
    far = [(flip(me, bit), own) for bit in extra]
    barrier = greet([core, near_x, near_y] + column + far)
    greet_owners(barrier, base, piece, own)
    pl.semaphore_wait(barrier, 6 + len(extra) + owner_greetings(piece, own))

    parity = piece % 2
    at = piece // 2
    at_x, at_y, at_xy = flip(at, 1), flip(at, 2), 3 - at
    order = (at_xy, at_x, at_y, at)
    started = []

    def send(src, dst, sems, k, device):
        copy = remote(src, dst, sems[0].at[k], sems[1].at[k], device)
        copy.start()
        started.append(copy)
        return copy

    crossing = []
    for k, m in enumerate(order):
        theirs = grads.at[:, :, columns(2 * m + 1 - parity)]
        crossing.append(send(theirs, from_core.at[k], (core_send, core_recv), k, core))

    def merge(k, m):
        crossing[k].wait_recv()
        mine = grads[:, :, columns(2 * m + parity)].astype(F32)
        sums[k] = (mine + from_core[k].astype(F32)).astype(BF16)

    plane = (plane_send, plane_recv)
    low, high = pl.ds(0, 2), pl.ds(2, 2)
    merge(0, at_xy)
    one_x = send(sums.at[0, low], from_x.at[0], plane, 0, near_x)
    one_y = send(sums.at[0, high], from_y.at[0], plane, 1, near_y)
    merge(1, at_x)
    two_x = send(sums.at[1, low], from_x.at[1], plane, 2, near_x)
    merge(2, at_y)
    two_y = send(sums.at[2, high], from_y.at[1], plane, 3, near_y)
    merge(3, at)
    one_x.wait_recv()
    sums[2, 0:2] = (sums[2, 0:2].astype(F32) + from_x[0].astype(F32)).astype(BF16)
    three_y = send(sums.at[2, low], last_y, plane, 4, near_y)
    one_y.wait_recv()
    sums[1, 2:4] = (sums[1, 2:4].astype(F32) + from_y[0].astype(F32)).astype(BF16)
    three_x = send(sums.at[1, high], last_x, plane, 5, near_x)
    two_x.wait_recv()
    two_y.wait_recv()
    three_y.wait_recv()
    three_x.wait_recv()
    low_sum = sums[3, 0:2].astype(F32) + from_x[1].astype(F32) + last_y[...].astype(F32)
    high_sum = sums[3, 2:4].astype(F32) + from_y[1].astype(F32) + last_x[...].astype(F32)
    sums[3, 0:2] = low_sum.astype(BF16)
    sums[3, 2:4] = high_sum.astype(BF16)
    for k, device in enumerate(far):
        copy = remote(sums.at[3], from_far.at[k], far_send.at[k], far_recv.at[k], device)
        copy.start()
        copy.wait()
        sums[3] = (sums[3].astype(F32) + from_far[k].astype(F32)).astype(BF16)
    crossing = []
    for step in (1, 2, 3):
        there = other_owner(own, step)
        crossing.append(
            send(sums.at[3, there], from_z.at[step - 1], (z_send, z_recv), step - 1, column[step - 1])
        )
    total = sums[3, own].astype(F32)
    for step in (1, 2, 3):
        crossing[step - 1].wait_recv()
        total = total + from_z[step - 1].astype(F32)
    moment[:, columns(piece)] = total.astype(BF16)

    def view(q, part):
        return moment.at[part_rows(part), columns(q)]

    gather = Gather(view, gather_send, gather_recv, 0)
    gather.first()

    def to_owner(k, s, q):
        matrix = MATRICES[k]
        there = (base + matrix["piece"], matrix["own"])
        src = moment.at[:, columns(piece)]
        dst = matrix_window.at[own, :, window_lanes(s)]
        return remote(src, dst, own_send.at[k], own_recv.at[OWNERS * s + own], there)

    for k, s, q in ROUTES:
        matrix = MATRICES[k]

        @pl.when((piece == q) & not_at(piece, own, matrix))
        def _(k=k, s=s, q=q):
            to_owner(k, s, q).start()

        @pl.when((piece == q) & is_at(piece, own, matrix))
        def _(s=s):
            matrix_window[own, :, window_lanes(s)] = moment[:, columns(piece)]

    gather.second()
    gather.third()
    gather.last()
    for k, s, q in ROUTES:
        matrix = MATRICES[k]

        @pl.when((piece == q) & not_at(piece, own, matrix))
        def _(k=k, s=s, q=q):
            to_owner(k, s, q).wait_send()

        @pl.when(is_at(piece, own, matrix))
        def _(matrix=matrix, s=s, q=q):
            for i in range(OWNERS):
                if q != matrix["piece"] or i != matrix["own"]:
                    dst = matrix_window.at[i, :, window_lanes(s)]
                    src = moment.at[:, columns(piece)]
                    sems = (own_send.at[0], own_recv.at[OWNERS * s + i])
                    remote(src, dst, sems[0], sems[1], (base + q, i)).wait_recv()

    gather.finish()
    for copy in started:
        copy.wait_send()


def reduce_grads(grads, extra):
    in_vmem = pl.BlockSpec(memory_space=pltpu.VMEM)

    def dma(n):
        return pltpu.SemaphoreType.DMA((max(n, 1),))

    part = (OWNERS, ROWS, PIECE)
    half = (2, ROWS, PIECE)
    return pl.pallas_call(
        functools.partial(reduce_kernel, extra),
        out_shape=(
            jax.ShapeDtypeStruct((ROWS, COLS), BF16),
            jax.ShapeDtypeStruct((OWNERS, ROWS, WINDOW), BF16),
        ),
        in_specs=[in_vmem],
        out_specs=(in_vmem,) * 2,
        scratch_shapes=[
            vmem((4,) + part, BF16),
            vmem((4,) + part, BF16),
            vmem((2,) + half, BF16),
            vmem((2,) + half, BF16),
            vmem(half, BF16),
            vmem(half, BF16),
            vmem((3, ROWS, PIECE), BF16),
            vmem((max(len(extra), 1),) + part, BF16),
            dma(4), dma(4), dma(6), dma(6), dma(3), dma(3), dma(len(extra)), dma(len(extra)),
            dma(Gather.SEMS), dma(Gather.SEMS), dma(6), dma(12),
        ],
        compiler_params=pltpu.CompilerParams(
            collective_id=1, has_side_effects=True, vmem_limit_bytes=48 << 20
        ),
        name="reduce_grads",
    )(grads)


def split(a):
    high = a.astype(BF16)
    return high, (a - high.astype(F32)).astype(BF16)


def dot_fine(a, b):
    a_high, a_low = split(a)
    b_high, b_low = split(b)
    return dot(a_high, b_high) + (dot(a_high, b_low) + dot(a_low, b_high))


def dot_low(a, b):
    return dot(a.astype(BF16), b.astype(BF16))


def polynomial_of(gram):
    size = gram.shape[0]
    eye = iota((size, size), 0) == iota((size, size), 1)
    unit = jnp.where(eye, 1.0, 0.0)
    power = jnp.sum(jnp.sum(jnp.where(eye, gram, 0.0), axis=1, keepdims=True), axis=0, keepdims=True)
    inverse = 1.0 / (jnp.sqrt(power) + NORM_FLOOR)
    current = gram * inverse * inverse
    result = None
    for step in range(NS_STEPS):
        square = dot_fine if step > 2 else dot_low
        poly = COEF_A * unit + COEF_B * current + COEF_C * square(current, current)
        result = poly if result is None else dot_low(poly, result)
        if step < NS_STEPS - 1:
            first = dot_fine if step < 2 else dot_low
            second = dot_fine if step < 1 else dot_low
            current = second(first(poly, current), poly)
    return result, inverse


def ortho_kernel(window, update, gram, poly):
    piece, own = lax.axis_index("dp") % PIECES, lax.axis_index("fsdp")
    owner = {"out": False, "conv": False, "in": False}
    low, high, factor = jnp.int32(0), jnp.int32(0), jnp.float32(0)
    for matrix in MATRICES:
        here = is_at(piece, own, matrix)
        owner[matrix["kind"]] = owner[matrix["kind"]] | here
        low = jnp.where(here, matrix["lanes"][0], low)
        high = jnp.where(here, matrix["lanes"][1], high)
        factor = jnp.where(here, MATRIX_RATE * matrix["scale"], factor)

    def half(h):
        return pl.ds(pl.multiple_of(low + 512 * h, 128), 512)

    def conv_part(k, width):
        lanes = pl.ds(pl.multiple_of(k * width, width), width)
        values = window[:, :, lanes].reshape(GROUPED, width)
        lane = iota((GROUPED, width), 1) + k * width
        return lanes, jnp.where((lane >= low) & (lane < high), values, jnp.zeros((), BF16))

    @pl.when(owner["in"])
    def _():
        a = window[:, :, half(0)].reshape(GROUPED, 512)
        b = window[:, :, half(1)].reshape(GROUPED, 512)
        gram[...] = dot_tn(a, a) + dot_tn(b, b)

    @pl.when(owner["out"])
    def _():
        gram[...] = jnp.zeros(gram.shape, F32)
        a = window[:, :, :PIECE].reshape(GROUPED, PIECE)
        gram[:GROUPED, :GROUPED] = dot_nt(a, a)

    @pl.when(owner["conv"])
    def _():
        gram[...] = jnp.zeros(gram.shape, F32)

        def body(k, carry):
            values = conv_part(k, 512)[1]
            gram[:GROUPED, :GROUPED] += dot_nt(values, values)
            return carry

        lax.fori_loop(0, 4, body, 0)

    @pl.when(owner["in"] | owner["out"] | owner["conv"])
    def _():
        result, inverse = polynomial_of(gram[...])
        poly[...] = (result * (inverse * factor)).astype(BF16)

    @pl.when(owner["in"])
    def _():
        update[...] = jnp.zeros(update.shape, BF16)
        for h in range(2):
            step = dot(window[:, :, half(h)].reshape(GROUPED, 512), poly[...])
            update[:, :, half(h)] = step.astype(BF16).reshape(OWNERS, ROWS, 512)

    @pl.when(owner["out"])
    def _():
        step = dot(poly[:GROUPED, :GROUPED], window[:, :, :PIECE].reshape(GROUPED, PIECE))
        update[:, :, :PIECE] = step.astype(BF16).reshape(OWNERS, ROWS, PIECE)

    @pl.when(owner["conv"])
    def _():
        update[:, :, 2048:] = jnp.zeros((OWNERS, ROWS, WINDOW - 2048), BF16)

        def body(k, carry):
            lanes, values = conv_part(k, 512)
            step = dot(poly[:GROUPED, :GROUPED], values)
            update[:, :, lanes] = step.astype(BF16).reshape(OWNERS, ROWS, 512)
            return carry

        lax.fori_loop(0, 4, body, 0)


def orthogonalize(window):
    in_vmem = pl.BlockSpec(memory_space=pltpu.VMEM)
    return pl.pallas_call(
        ortho_kernel,
        out_shape=jax.ShapeDtypeStruct(window.shape, BF16),
        in_specs=[in_vmem],
        out_specs=in_vmem,
        scratch_shapes=[vmem((512, 512), F32), vmem((512, 512), BF16)],
        compiler_params=pltpu.CompilerParams(vmem_limit_bytes=48 << 20),
        name="orthogonalize",
    )(window)


def slot_of(k, q):
    return sum(1 for j, s, other in ROUTES if other == q and j < k)


def spread_kernel(window, update, parts, send, recv, gather_send, gather_recv):
    base, piece, own = place()
    barrier = greet([(base + flip(piece, bit), own) for bit in (1, 2, 4)])
    greet_owners(barrier, base, piece, own)
    pl.semaphore_wait(barrier, 3 + owner_greetings(piece, own))

    def outgoing(s, q, slot, i):
        src = window.at[i, :, window_lanes(s)]
        return remote(src, parts.at[slot], send.at[OWNERS * s + i], recv.at[slot], (base + q, i))

    for k, s, q in ROUTES:
        matrix = MATRICES[k]
        slot = slot_of(k, q)

        @pl.when(is_at(piece, own, matrix))
        def _(matrix=matrix, s=s, q=q, slot=slot):
            for i in range(OWNERS):
                if q != matrix["piece"] or i != matrix["own"]:
                    outgoing(s, q, slot, i).start()
                else:
                    parts[slot] = window[i, :, window_lanes(s)]

    for k, s, q in ROUTES:
        matrix = MATRICES[k]
        slot = slot_of(k, q)

        @pl.when((piece == q) & not_at(piece, own, matrix))
        def _(matrix=matrix, slot=slot):
            there = (base + matrix["piece"], matrix["own"])
            remote(window.at[0, :, window_lanes(0)], parts.at[slot], send.at[0], recv.at[slot], there).wait_recv()

    shared = [q for q in range(PIECES) if sum(1 for r in ROUTES if r[2] == q) == 2]
    update[:, columns(piece)] = parts[0]
    for q in shared:

        @pl.when(piece == q)
        def _():
            update[:, columns(piece)] = parts[0] + parts[1]

    def view(q, part):
        return update.at[part_rows(part), columns(q)]

    gather = Gather(view, gather_send, gather_recv, 0)
    gather.first()
    gather.second()
    gather.third()
    gather.last()
    gather.finish()
    for k, s, q in ROUTES:
        matrix = MATRICES[k]

        @pl.when(is_at(piece, own, matrix))
        def _(matrix=matrix, s=s, q=q):
            for i in range(OWNERS):
                if q != matrix["piece"] or i != matrix["own"]:
                    outgoing(s, q, 0, i).wait_send()


def spread_steps(window):
    in_vmem = pl.BlockSpec(memory_space=pltpu.VMEM)

    def dma(n):
        return pltpu.SemaphoreType.DMA((n,))

    return pl.pallas_call(
        spread_kernel,
        out_shape=jax.ShapeDtypeStruct((ROWS, COLS), BF16),
        in_specs=[in_vmem],
        out_specs=in_vmem,
        scratch_shapes=[
            vmem((2, ROWS, PIECE), BF16),
            dma(12), dma(2), dma(Gather.SEMS), dma(Gather.SEMS),
        ],
        compiler_params=pltpu.CompilerParams(
            collective_id=2, has_side_effects=True, vmem_limit_bytes=40 << 20
        ),
        name="spread_steps",
    )(window)


def finish_kernel(
    vector_step, moment, update, conv, w_in, w_out, wide, narrow,
    mom_in, mom_conv, mom_out, mom_wide, mom_narrow,
    new_in, new_conv, new_out, new_wide, new_narrow, low_in, low_conv, low_out,
):
    lanes = slice(CONV_AT, CONV_AT + 3200)
    mom_conv[...] = moment[:SHARD, lanes].astype(F32)
    value = conv[...] - update[:SHARD, lanes].astype(F32)
    new_conv[...] = value
    low_conv[...] = value.astype(BF16)
    for b in range(2):
        lanes = slice(WO_AT[b], WO_AT[b] + D)
        mom_out[:, b, :] = moment[:SHARD, lanes].astype(F32)
        value = w_out[:, b, :] - update[:SHARD, lanes].astype(F32)
        new_out[:, b, :] = value
        low_out[b] = value.astype(BF16)
        for h in range(2):
            lanes = slice(WI_AT[b][h], WI_AT[b][h] + H)
            rows = slice(h * SHARD, (h + 1) * SHARD)
            mom_in[b, rows, :] = moment[:SHARD, lanes].astype(F32)
            value = w_in[b, rows, :] - update[:SHARD, lanes].astype(F32)
            new_in[b, rows, :] = value
            low_in[b, rows, :] = value.astype(BF16)
        lanes = slice(VEC_AT, VEC_AT + SHARD)
        vectors = moment[:, VEC_AT : VEC_AT + 128].astype(F32)
        for k in range(6):
            m = 6 * b + k
            value = vectors[m : m + 1, :SHARD]
            mom_narrow[k, b : b + 1, :] = value
            new_narrow[k, b : b + 1, :] = narrow[k, b : b + 1, :] - vector_step * value
        for k in range(3):
            for h in range(2):
                m = 16 + 16 * h + 3 * b + k
                lanes = slice(h * SHARD, (h + 1) * SHARD)
                value = vectors[m : m + 1, :SHARD]
                mom_wide[k, b : b + 1, lanes] = value
                new_wide[k, b : b + 1, lanes] = wide[k, b : b + 1, lanes] - vector_step * value


def finish(vector_step, moment, update, conv, w_in, w_out, wide, narrow):
    in_vmem = pl.BlockSpec(memory_space=pltpu.VMEM)
    shapes = [w_in.shape, conv.shape, w_out.shape, wide.shape, narrow.shape]
    outs = [jax.ShapeDtypeStruct(s, F32) for s in shapes + shapes]
    outs += [jax.ShapeDtypeStruct(s, BF16) for s in shapes[:2] + [(2, SHARD, D)]]
    return pl.pallas_call(
        functools.partial(finish_kernel, vector_step),
        out_shape=tuple(outs),
        in_specs=[in_vmem] * 7,
        out_specs=(in_vmem,) * len(outs),
        compiler_params=pltpu.CompilerParams(vmem_limit_bytes=40 << 20),
        name="finish",
    )(moment, update, conv, w_in, w_out, wide, narrow)


def shards(
    extra, vector_step, tokens, cotangent, lengths, dilation, proj_in, conv_weight, proj_out, vec_wide, vec_narrow,
    mom_in, mom_conv, mom_out, mom_wide, mom_narrow,
):
    proj_out, vec_wide, vec_narrow = swap(proj_out), swap(vec_wide), swap(vec_narrow)
    moments = (mom_conv, mom_in, swap(mom_out), swap(mom_wide), swap(mom_narrow))
    params = (conv_weight, proj_in, proj_out, vec_wide, vec_narrow)
    out, grad_tokens, grads = compute(dilation, lengths, tokens.T, cotangent.T, params, moments)
    moment, window = reduce_grads(grads, extra)
    update = spread_steps(orthogonalize(window))
    rest = list(finish(vector_step, moment, update, conv_weight, proj_in, proj_out, vec_wide, vec_narrow))
    for k in (2, 3, 4, 7, 8, 9):
        rest[k] = swap(rest[k])
    return (out.T, grad_tokens.T) + tuple(rest)


def swap(array):
    return jnp.transpose(array, (1, 0, 2))


def solution(mesh):
    groups, owners = mesh.shape["dp"], mesh.shape["fsdp"]
    assert owners == OWNERS and groups % PIECES == 0
    extra, bit = [], PIECES
    while bit < groups:
        extra.append(bit)
        bit *= 2
    assert bit == groups
    vector_step = VECTOR_RATE / math.sqrt(TOK * groups * owners)
    tok, rep = P(("dp", "fsdp"), None), P()
    mid, first, final = P(None, "fsdp", None), P("fsdp", None), P(None, None, "fsdp")
    params = (mid, first, mid, final, final)
    return jax.shard_map(
        functools.partial(shards, tuple(extra), vector_step),
        mesh=mesh,
        in_specs=(tok, tok, tok, rep) + params + params,
        out_specs=(tok, tok) + params + params + (mid, first, mid),
        check_vma=False,
    )
```

```python
import functools
import math

import jax
import jax.numpy as jnp
from jax import lax
from jax.experimental import pallas as pl
from jax.experimental.pallas import tpu as pltpu
from jax.sharding import PartitionSpec as P

D = 800
H = 400
K_ENC = 5
K_DEC = 3
NS_STEPS = 5
EPSILON = 1e-05
NORM_FLOOR = 1e-07
COEF_A = 3.4445
COEF_B = -4.775
COEF_C = 2.0315
MOMENT_DECAY = 0.5
MATRIX_RATE = 0.5
VECTOR_RATE = 0.1

F32 = jnp.float32
BF16 = jnp.bfloat16
MESH = pl.DeviceIdType.MESH

OWNERS = 4
PIECES = 8
SHARD = 100
ROWS = 112
MIX, ENC, DEC = 0, 1, 2
WIDTH = (256, 256, 384)
IN_AT = ((MIX, 0), (DEC, 1280))
OUT_AT = ((MIX, 896), (DEC, 2176))
CONV_AT = ((ENC, 0), (DEC, 0))
CONV_LANES = ((0, 2048), (1920, 3200))
VEC_AT = 1792
SPLIT = K_ENC * H
TOK = 256
GROUPED = OWNERS * ROWS
WINDOW = 2048

GELU_K = math.sqrt(2.0 / math.pi)
GELU_C = 0.044715


def vmem(shape, dtype):
    return pltpu.VMEM(shape, dtype)


def dot(a, b):
    return lax.dot_general(a, b, (((1,), (0,)), ((), ())), preferred_element_type=F32)


def dot_nt(a, b):
    return lax.dot_general(a, b, (((1,), (1,)), ((), ())), preferred_element_type=F32)


def dot_tn(a, b):
    return lax.dot_general(a, b, (((0,), (0,)), ((), ())), preferred_element_type=F32)


def one_hot(mask):
    return jnp.where(mask, 1.0, 0.0).astype(BF16)


def iota(shape, dim):
    return lax.broadcasted_iota(jnp.int32, shape, dim)


def add_low(*parts):
    total = parts[0].astype(F32)
    for part in parts[1:]:
        total = total + part.astype(F32)
    return total.astype(BF16)


def spans(chunk, low, high):
    width = WIDTH[chunk]
    for q in range(low // width, -(-high // width)):
        yield q, max(low - q * width, 0), min(high - q * width, width)


def load(ref, chunk, low, high, lead=(), rows=slice(None)):
    parts = []
    for q, start, stop in spans(chunk, low, high):
        parts.append(ref[lead + (q // 4, q // 2 % 2, q % 2, rows, slice(start, stop))])
    return parts[0] if len(parts) == 1 else jnp.concatenate(parts, axis=-1)


def store(ref, chunk, low, value, lead=(), rows=slice(None), add=False):
    at = 0
    for q, start, stop in spans(chunk, low, low + value.shape[-1]):
        index = lead + (q // 4, q // 2 % 2, q % 2, rows, slice(start, stop))
        part = value[..., at : at + stop - start]
        ref[index] = add_low(ref[index], part) if add else part
        at += stop - start


def lay_out(conv, w_in, w_out, wide, narrow, put):
    for b in range(2):
        chunk, at = CONV_AT[b]
        lanes = CONV_LANES[b]
        put(chunk, at, slice(0, SHARD), conv[:, lanes[0] : lanes[1]])
        chunk, at = OUT_AT[b]
        put(chunk, at, slice(0, SHARD), w_out[:, b, :])
        chunk, at = IN_AT[b]
        first, second = w_in[b, :SHARD, :], w_in[b, SHARD:, :]
        zeros = jnp.zeros((SHARD, 512 - H), F32)
        low = jnp.concatenate([first, zeros], axis=1)
        high = pltpu.roll(jnp.concatenate([second, zeros], axis=1), H % 128, 1)
        put(chunk, at, slice(0, SHARD), low[:, :384])
        put(chunk, at + 384, slice(0, SHARD), low[:, 384:] + high[:, :128])
        put(chunk, at + 512, slice(0, SHARD), high[:, 128:])
    for b in range(2):
        for k in range(6):
            m = 6 * b + k
            put(MIX, VEC_AT, slice(m, m + 1), narrow[k, b : b + 1, :])
        for k in range(3):
            for h in range(2):
                m = 16 + 16 * h + 3 * b + k
                put(MIX, VEC_AT, slice(m, m + 1), wide[k, b : b + 1, h * SHARD : (h + 1) * SHARD])


def flip(value, bit):
    return value + bit - 2 * bit * ((value // bit) % 2)


def other_owner(own, step):
    if step == 0:
        return own
    if step == 3:
        return 3 - own
    return flip(own, step)


def remote(src, dst, send, recv, device):
    return pltpu.make_async_remote_copy(
        src_ref=src,
        dst_ref=dst,
        send_sem=send,
        recv_sem=recv,
        device_id=device,
        device_id_type=MESH,
    )


class Place:
    def __init__(self, send, recv, extra):
        at = lax.axis_index("dp")
        self.piece = at % PIECES
        self.base = at - self.piece
        self.me = at
        self.own = lax.axis_index("fsdp")
        self.y, self.x, self.c = self.piece // 4, self.piece // 2 % 2, self.piece % 2
        self.core, self.near_x, self.near_y = [
            (self.base + flip(self.piece, bit), self.own) for bit in (1, 2, 4)
        ]
        self.column = [(at, other_owner(self.own, step)) for step in (1, 2, 3)]
        self.far = [(flip(at, bit), self.own) for bit in extra]
        self.send, self.recv, self.used = send, recv, 0
        self.started = []

    def take(self, count):
        first = self.used
        self.used += count
        return first

    def start(self, src, dst, device):
        k = self.take(1)
        copy = remote(src, dst, self.send.at[k], self.recv.at[k], device)
        copy.start()
        self.started.append(copy)
        return copy

    def finish(self):
        for copy in self.started:
            copy.wait_send()


class Gather:
    LOW, HIGH, ALL = pl.ds(0, 64), pl.ds(64, 48), slice(None)

    def __init__(self, place, view):
        self.place, self.view = place, view

    def move(self, device, *index):
        ref = self.view(*index)
        return self.place.start(ref, ref, device)

    def first(self):
        p = self.place
        self.a = self.move(p.near_y, p.y, p.x, p.c, self.LOW)
        self.b = self.move(p.near_x, p.y, p.x, p.c, self.HIGH)

    def second(self):
        p = self.place
        self.a.wait_recv()
        self.a = self.move(p.near_x, self.ALL, p.x, p.c, self.LOW)
        self.b.wait_recv()
        self.b = self.move(p.near_y, p.y, self.ALL, p.c, self.HIGH)

    def third(self):
        p = self.place
        self.a.wait_recv()
        self.b.wait_recv()
        self.a = self.move(p.core, self.ALL, self.ALL, p.c, self.ALL)

    def last(self):
        self.a.wait_recv()


class WeightGather(Gather):
    def __init__(self, place, ref):
        def view(y, x, c, rows):
            return ref.at[pl.ds(1, 3), y, x, c, rows]

        super().__init__(place, view)
        self.ref = ref

    def cross(self):
        p = self.place
        mine = self.ref.at[0, p.y, p.x, p.c]
        self.crossing = [
            p.start(mine, self.ref.at[step, p.y, p.x, p.c], p.column[step - 1]) for step in (1, 2, 3)
        ]

    def first(self):
        for copy in self.crossing:
            copy.wait_recv()
        super().first()


class Reduce:
    def __init__(self, place, grads, moment, room):
        self.place, self.grads, self.moment = place, grads, moment
        self.from_core, self.sums, self.from_x, self.from_y = room[:4]
        self.last_x, self.last_y, self.from_z, self.from_far = room[4:]

    def core(self):
        p = self.place
        self.halves = []
        for y in (1 - p.y, p.y):
            src = self.grads.at[:, y, :, 1 - p.c]
            self.halves.append((y, p.start(src, self.from_core.at[:, y], p.core)))

    def plane(self):
        p = self.place
        self.a = []
        for k, (y, copy) in enumerate(self.halves):
            copy.wait_recv()
            self.sums[:, y] = add_low(self.grads[:, y, :, p.c], self.from_core[:, y])
            self.a.append(
                p.start(self.sums.at[0:2, y, 1 - p.x], self.from_x.at[:, y], p.near_x)
            )
            if k == 0:
                self.b = p.start(self.sums.at[2:4, y], self.from_y, p.near_y)

    def turn(self):
        p = self.place
        y, x = 1 - p.y, 1 - p.x
        self.a[0].wait_recv()
        self.sums[0:2, y, p.x] = add_low(self.sums[0:2, y, p.x], self.from_x[:, y])
        self.y_last = p.start(self.sums.at[0:2, y, p.x], self.last_y, p.near_y)
        self.b.wait_recv()
        self.sums[2:4, p.y, x] = add_low(self.sums[2:4, p.y, x], self.from_y[:, x])
        self.x_last = p.start(self.sums.at[2:4, p.y, x], self.last_x, p.near_x)

    def cross(self):
        p = self.place
        y, x = p.y, p.x
        self.a[1].wait_recv()
        self.y_last.wait_recv()
        self.sums[0:2, y, x] = add_low(self.sums[0:2, y, x], self.from_x[:, y], self.last_y[...])
        self.x_last.wait_recv()
        self.sums[2:4, y, x] = add_low(self.sums[2:4, y, x], self.from_y[:, x], self.last_x[...])
        for k, device in enumerate(p.far):
            p.start(self.sums.at[:, y, x], self.from_far.at[k], device).wait_recv()
            p.started.pop().wait_send()
            self.sums[:, y, x] = add_low(self.sums[:, y, x], self.from_far[k])
        self.crossing = [
            p.start(self.sums.at[step, y, x], self.from_z.at[step - 1], p.column[step - 1])
            for step in (1, 2, 3)
        ]

    def finish(self):
        p = self.place
        for copy in self.crossing:
            copy.wait_recv()
        parts = [self.sums[0, p.y, p.x]] + [self.from_z[k] for k in range(3)]
        self.moment[p.y, p.x, p.c] = add_low(*parts)


def reduce_room(chunk, extra):
    width = WIDTH[chunk]
    shapes = (
        (OWNERS, 2, 2), (OWNERS, 2, 2), (2, 2), (2, 2), (2,), (2,), (3,), (max(len(extra), 1), OWNERS),
    )
    return [vmem(shape + (ROWS, width), BF16) for shape in shapes]


MATRICES = (
    dict(kind="row", chunk=DEC, first=0, last=3, piece=2, own=2, lanes=(80, 1280), slot=0, scale=1.0),
    dict(kind="in", chunk=DEC, first=3, last=5, piece=4, own=2, lanes=(128, 928), slot=1, scale=1.0),
    dict(kind="row", chunk=DEC, first=5, last=7, piece=6, own=1, lanes=(256, 1056), slot=0, scale=math.sqrt(D / H)),
    dict(kind="row", chunk=ENC, first=0, last=7, piece=0, own=1, lanes=(0, 2000), slot=0, scale=1.0),
    dict(kind="in", chunk=MIX, first=0, last=3, piece=5, own=1, lanes=(0, 800), slot=0, scale=1.0),
    dict(kind="row", chunk=MIX, first=3, last=6, piece=3, own=1, lanes=(128, 928), slot=1, scale=math.sqrt(D / H)),
)


class Owner:
    def __init__(self, place, matrix):
        self.place, self.matrix = place, matrix
        self.width = WIDTH[matrix["chunk"]]
        self.count = OWNERS * (matrix["last"] - matrix["first"] + 1)
        p = place
        self.here = (p.piece == matrix["piece"]) & (p.own == matrix["own"])
        self.away = (p.piece != matrix["piece"]) | (p.own != matrix["own"])
        self.holds = (p.piece >= matrix["first"]) & (p.piece <= matrix["last"])
        self.device = (p.base + matrix["piece"], matrix["own"])
        inside = matrix["first"] <= matrix["piece"] <= matrix["last"]
        self.self_at = OWNERS * (matrix["piece"] - matrix["first"]) + matrix["own"] if inside else -1

    def holder(self, r):
        return (self.place.base + self.matrix["first"] + r // OWNERS, r % OWNERS)

    def each_holder(self, act):
        def body(r, carry):
            @pl.when(r != self.self_at)
            def _():
                act(r)

            return carry

        lax.fori_loop(0, self.count, body, 0)

    def lanes(self, k):
        return pl.ds(pl.multiple_of(k * self.width, 128), self.width)

    def greet(self, barrier):
        @pl.when(self.holds & self.away)
        def _():
            pl.semaphore_signal(barrier, inc=1, device_id=self.device, device_id_type=MESH)

        @pl.when(self.here)
        def _():
            def signal(r):
                pl.semaphore_signal(barrier, inc=1, device_id=self.holder(r), device_id_type=MESH)

            self.each_holder(signal)

    def greetings(self):
        others = self.count - (1 if self.self_at >= 0 else 0)
        return jnp.where(self.holds & self.away, 1, 0) + jnp.where(self.here, others, 0)

    def to_owner(self, moment, window, send, recv, k):
        p = self.place
        at = p.piece - self.matrix["first"]
        src = moment.at[p.y, p.x, p.c]
        dst = window.at[p.own, :, self.lanes(at)]
        return remote(src, dst, send.at[k], recv.at[OWNERS * at + p.own], self.device)

    def gather(self, moment, window, send, recv, k):
        @pl.when(self.holds & self.away)
        def _():
            self.to_owner(moment, window, send, recv, k).start()

        if self.self_at >= 0:

            @pl.when(self.here)
            def _():
                p = self.place
                at = p.piece - self.matrix["first"]
                window[p.own, :, self.lanes(at)] = moment[p.y, p.x, p.c]

    def gather_sent(self, moment, window, send, recv, k):
        @pl.when(self.holds & self.away)
        def _():
            self.to_owner(moment, window, send, recv, k).wait_send()

    def gathered(self, moment, window, send, recv, k):
        def wait(r):
            dst = window.at[r % OWNERS, :, self.lanes(r // OWNERS)]
            p = self.place
            src = moment.at[p.y, p.x, p.c]
            remote(src, dst, send.at[k], recv.at[r], self.holder(r)).wait_recv()

        self.each_holder(wait)

    def outgoing(self, window, parts, send, recv, r):
        src = window.at[r % OWNERS, :, self.lanes(r // OWNERS)]
        dst = parts.at[self.matrix["slot"]]
        return remote(src, dst, send.at[r], recv.at[2 * self.matrix["chunk"] + self.matrix["slot"]], self.holder(r))

    def spread(self, window, parts, send, recv):
        self.each_holder(lambda r: self.outgoing(window, parts, send, recv, r).start())
        if self.self_at >= 0:
            p = self.place
            at = p.piece - self.matrix["first"]
            parts[self.matrix["slot"]] = window[p.own, :, self.lanes(at)]

    def spread_sent(self, window, parts, send, recv):
        @pl.when(self.here)
        def _():
            self.each_holder(lambda r: self.outgoing(window, parts, send, recv, r).wait_send())

    def arrived(self, window, parts, send, recv):
        @pl.when(self.holds & self.away)
        def _():
            src = window.at[0, :, self.lanes(0)]
            dst = parts.at[self.matrix["slot"]]
            sems = (send.at[0], recv.at[2 * self.matrix["chunk"] + self.matrix["slot"]])
            remote(src, dst, sems[0], sems[1], self.device).wait_recv()


def split(a):
    high = a.astype(BF16)
    return high, (a - high.astype(F32)).astype(BF16)


def dot_fine(a, b):
    a_high, a_low = split(a)
    b_high, b_low = split(b)
    return dot(a_high, b_high) + (dot(a_high, b_low) + dot(a_low, b_high))


def dot_low(a, b):
    return dot(a.astype(BF16), b.astype(BF16))


def polynomial_of(gram):
    size = gram.shape[0]
    eye = iota((size, size), 0) == iota((size, size), 1)
    unit = jnp.where(eye, 1.0, 0.0)
    power = jnp.sum(jnp.sum(jnp.where(eye, gram, 0.0), axis=1, keepdims=True), axis=0, keepdims=True)
    inverse = 1.0 / (jnp.sqrt(power) + NORM_FLOOR)
    current = gram * inverse * inverse
    result = None
    for step in range(NS_STEPS):
        square = dot_fine if step > 2 else dot_low
        poly = COEF_A * unit + COEF_B * current + COEF_C * square(current, current)
        result = poly if result is None else dot_low(poly, result)
        if step < NS_STEPS - 1:
            first = dot_fine if step < 2 else dot_low
            second = dot_fine if step < 1 else dot_low
            current = second(first(poly, current), poly)
    return result, inverse


def orthogonalize(owners, window, gram, poly, halves):
    is_in, is_row = False, False
    low, high, factor, parts = jnp.int32(0), jnp.int32(0), jnp.float32(0), jnp.int32(0)
    for owner in owners:
        matrix, here = owner.matrix, owner.here
        if matrix["kind"] == "in":
            is_in = is_in | here
        else:
            is_row = is_row | here
        low = jnp.where(here, matrix["lanes"][0], low)
        high = jnp.where(here, matrix["lanes"][1], high)
        parts = jnp.where(here, -(-matrix["lanes"][1] // 512), parts)
        factor = jnp.where(here, MATRIX_RATE * matrix["scale"], factor)

    def part(k):
        lanes = pl.ds(pl.multiple_of(k * 512, 512), 512)
        values = window[:, :, lanes].reshape(GROUPED, 512)
        lane = iota((GROUPED, 512), 1) + k * 512
        return lanes, jnp.where((lane >= low) & (lane < high), values, jnp.zeros((), BF16))

    def half(h):
        return pl.ds(pl.multiple_of(low + 384 * h, 128), 512)

    @pl.when(is_in)
    def _():
        valid = iota((GROUPED, 512), 1) < H
        for h in range(2):
            values = window[:, :, half(h)].reshape(GROUPED, 512).astype(F32)
            if h:
                values = pltpu.roll(values, 512 - H % 128, 1)
            halves[h] = jnp.where(valid, values, 0.0).astype(BF16)
        gram[...] = dot_tn(halves[0], halves[0]) + dot_tn(halves[1], halves[1])

    @pl.when(is_row)
    def _():
        gram[...] = jnp.zeros(gram.shape, F32)

        def body(k, carry):
            values = part(k)[1]
            gram[:GROUPED, :GROUPED] += dot_nt(values, values)
            return carry

        lax.fori_loop(0, parts, body, 0)

    @pl.when(is_in | is_row)
    def _():
        result, inverse = polynomial_of(gram[...])
        poly[...] = (result * (inverse * factor)).astype(BF16)

    @pl.when(is_in)
    def _():
        window[:, :, :1152] = jnp.zeros((OWNERS, ROWS, 1152), BF16)
        window[:, :, half(0)] = dot(halves[0], poly[...]).astype(BF16).reshape(OWNERS, ROWS, 512)
        step = pltpu.roll(dot(halves[1], poly[...]), H % 128, 1).reshape(OWNERS, ROWS, 512)
        window[:, :, half(1)] = add_low(window[:, :, half(1)], step)

    @pl.when(is_row)
    def _():
        def body(k, carry):
            lanes, values = part(k)
            step = dot(poly[:GROUPED, :GROUPED], values)
            window[:, :, lanes] = step.astype(BF16).reshape(OWNERS, ROWS, 512)
            return carry

        lax.fori_loop(0, parts, body, 0)


def norm_forward(src, width, gain, shift, act, unit, slope, spread, chunk=128):
    def body(k, carry):
        rows = pl.ds(pl.multiple_of(k * chunk, chunk), chunk)
        x = src[rows, :width].astype(F32)
        center = x - jnp.mean(x, axis=1, keepdims=True)
        scale = lax.rsqrt(jnp.mean(center * center, axis=1, keepdims=True) + EPSILON)
        xhat = center * scale
        a = xhat * gain + shift
        square = a * a
        half = 0.5 + 0.5 * jnp.tanh(a * (GELU_K + (GELU_K * GELU_C) * square))
        act[rows, :width] = (a * half).astype(BF16)
        unit[rows, :width] = xhat.astype(BF16)
        inner = GELU_K + (3.0 * GELU_K * GELU_C) * square
        slope[rows, :width] = (half + (2.0 * a * inner) * (half * (1.0 - half))).astype(BF16)
        spread[rows, :] = jnp.broadcast_to(scale, (chunk, 128))
        return carry

    lax.fori_loop(0, TOK // chunk, body, 0)


def fold_rows(values):
    total = values[0:8]
    for k in range(1, values.shape[0] // 8):
        total = total + values[8 * k : 8 * k + 8]
    return total


def norm_backward(grad, width, gain, unit, slope, spread, finish, chunk=128):
    def body(k, sums):
        rows = pl.ds(pl.multiple_of(k * chunk, chunk), chunk)
        da = grad[rows, :width] * slope[rows, :width].astype(F32)
        xhat = unit[rows, :width].astype(F32)
        product = da * xhat
        dxhat = da * gain
        mean_one = jnp.mean(dxhat, axis=1, keepdims=True)
        mean_two = jnp.mean(dxhat * xhat, axis=1, keepdims=True)
        dx = spread[rows, 0:1] * (dxhat - mean_one - xhat * mean_two)
        finish(rows, dx)
        return (sums[0] + fold_rows(product), sums[1] + fold_rows(da), sums[2] + fold_rows(dx))

    zero = jnp.zeros((8, width), F32)
    sums = lax.fori_loop(0, TOK // chunk, body, (zero, zero, zero))
    return tuple(jnp.sum(s, axis=0, keepdims=True) for s in sums)


def step_kernel(
    extra,
    dilation, lengths, tokens_hbm, cotangent_hbm,
    conv_hbm, in_hbm, out_hbm, wide_hbm, narrow_hbm,
    mom_conv_hbm, mom_in_hbm, mom_out_hbm, mom_wide_hbm, mom_narrow_hbm,
    out, grad_tokens, moment_mix, moment_enc, moment_dec, update_mix, update_enc, update_dec,
    send, recv, own_send, own_recv, back_send, back_recv, local,
    full_mix, full_enc, full_dec, grads_mix, grads_enc, grads_dec, parts_mix, parts_enc, parts_dec, window,
    tokens, cotangent, conv, in_shard, out_shard, wide_shard, narrow_shard,
    far, perm_h, vec_w, vec_n, w_in, x_one, wide_grad, tall,
    act_d, act_h, act_g, act_t, e_all,
    unit_d, slope_d, spread_d, unit_h, slope_h, spread_h,
    gram, poly, halves, *rooms,
):
    place = Place(send, recv, extra)
    own = place.own
    full = (full_mix, full_enc, full_dec)
    grads = (grads_mix, grads_enc, grads_dec)
    moments = (moment_mix, moment_enc, moment_dec)
    updates = (update_mix, update_enc, update_dec)
    parts = (parts_mix, parts_enc, parts_dec)
    owners = [Owner(place, matrix) for matrix in MATRICES]
    conv_in, spare = gram.at[:TOK], gram.at[TOK:]
    hid = spare

    sources = (conv_hbm, in_hbm, out_hbm, wide_hbm, narrow_hbm, tokens_hbm, cotangent_hbm)
    shard = (conv, in_shard, out_shard, wide_shard, narrow_shard)
    targets = shard + (tokens, cotangent)
    fetches = [pltpu.make_async_copy(s, t, local.at[k]) for k, (s, t) in enumerate(zip(sources, targets))]
    for fetch in fetches:
        fetch.start()
    for ref in parts:
        ref[...] = jnp.zeros(ref.shape, BF16)
    barrier = pltpu.get_barrier_semaphore()
    for device in [place.core, place.near_x, place.near_y] + place.column + place.far:
        pl.semaphore_signal(barrier, inc=1, device_id=device, device_id_type=MESH)
    for owner in owners:
        owner.greet(barrier)
    for ref in full:
        ref[0] = jnp.zeros(ref.shape[1:], BF16)

    def put_weights(chunk, low, rows, values):
        store(full[chunk], chunk, low, values.astype(BF16), lead=(0,), rows=rows)

    for fetch in fetches[:5]:
        fetch.wait()
    lay_out(*shard, put_weights)
    sources = (mom_conv_hbm, mom_in_hbm, mom_out_hbm, mom_wide_hbm, mom_narrow_hbm)
    moment_fetches = [pltpu.make_async_copy(s, t, local.at[7 + k]) for k, (s, t) in enumerate(zip(sources, shard))]
    for fetch in moment_fetches:
        fetch.start()
    greetings = 6 + len(extra)
    for owner in owners:
        greetings = greetings + owner.greetings()
    pl.semaphore_wait(barrier, greetings)

    gathers = [WeightGather(place, ref) for ref in full]
    for gather in gathers:
        gather.cross()

    row, col = iota((TOK, TOK), 0), iota((TOK, TOK), 1)
    seg_row, seg_col = jnp.zeros((TOK, TOK), jnp.int32), jnp.zeros((TOK, TOK), jnp.int32)
    end = jnp.int32(0)
    for k in range(8):
        end = end + lengths[0, k]
        seg_row = seg_row + jnp.where(row >= end, 1, 0)
        seg_col = seg_col + jnp.where(col >= end, 1, 0)
    far[...] = jnp.where(seg_row == seg_col, col - row, 4 * TOK)

    def mover(offset):
        return one_hot(far[...] == offset)

    gathers[MIX].first()
    row, col = iota((H, GROUPED), 0), iota((H, GROUPED), 1)
    used = jnp.zeros((H, GROUPED), jnp.int32)
    for s in range(OWNERS):
        r = col - ROWS * s
        inside = (r >= 0) & (r < SHARD) & (row == r + SHARD * other_owner(own, s))
        used = used + jnp.where(inside, 1, 0)
    perm_h[...] = used.astype(F32).astype(BF16)
    gathers[MIX].second()
    gathers[ENC].first()
    fetches[5].wait()
    x_one[...] = tokens[...].astype(F32).T
    gathers[MIX].third()
    gathers[ENC].second()
    gathers[DEC].first()
    fetches[6].wait()
    wide_grad[...] = cotangent[...].astype(F32).T
    gathers[MIX].last()

    row_n, col_n = iota((128, H), 0), iota((128, H), 1)
    row_w, col_w = iota((128, D), 0), iota((128, D), 1)

    def put_narrow(s):
        return one_hot((col_n == row_n + SHARD * other_owner(own, s)) & (row_n < SHARD))

    def put_wide(s, h):
        return one_hot((col_w == row_w + SHARD * (2 * other_owner(own, s) + h)) & (row_w < SHARD))

    total_n, total_w = jnp.zeros((16, H), F32), jnp.zeros((16, D), F32)
    for s in range(OWNERS):
        vectors = load(full[MIX], MIX, VEC_AT, VEC_AT + 128, lead=(s,))
        total_n = total_n + dot(vectors[0:16], put_narrow(s))
        for h in range(2):
            total_w = total_w + dot(vectors[16 + 16 * h : 32 + 16 * h], put_wide(s, h))
    vec_n[...] = total_n
    vec_w[...] = total_w

    def narrow(b, k):
        return vec_n[6 * b + k : 6 * b + k + 1, :]

    def wide(b, k):
        return vec_w[3 * b + k : 3 * b + k + 1, :]

    def weights(chunk, low, high):
        return load(full[chunk], chunk, low, high, lead=(slice(None),)).reshape(GROUPED, high - low)

    def weight_out(b):
        chunk, at = OUT_AT[b]
        return weights(chunk, at, at + 896)[:, :D]

    def place_in(b):
        chunk, at = IN_AT[b]
        for i in range(OWNERS):
            slot = other_owner(own, i)
            values = load(full[chunk], chunk, at, at + 896, lead=(slot,)).astype(F32)[:SHARD]
            tall[2 * SHARD * i : 2 * SHARD * i + SHARD, :] = values[:, :H]
            high = pltpu.roll(values[:, 384:], 512 - H % 128, 1)
            tall[2 * SHARD * i + SHARD : 2 * SHARD * (i + 1), :] = high[:, :H]
        w_in[b] = tall[...].astype(BF16)

    def taps(b):
        if b == 0:
            return [(H * j, (j - K_ENC // 2) * dilation[0]) for j in range(K_ENC)]
        return [(SPLIT - CONV_LANES[1][0] + H * j, -j * dilation[1]) for j in range(K_DEC)]

    def forward_in(b):
        norm_forward(x_one, D, wide(b, 0), wide(b, 1), act_d.at[b], unit_d.at[b], slope_d.at[b], spread_d.at[b])
        place_in(b)
        hid[:, :H] = dot(act_d[b], w_in[b]) + narrow(b, 0)
        norm_forward(
            hid, H, narrow(b, 1), narrow(b, 2), act_h.at[0], unit_h.at[b, 0], slope_h.at[b, 0], spread_h.at[b, 0]
        )
        act_g[b, 0] = dot(act_h[0], perm_h[...]).astype(BF16)

    def forward_conv(b):
        for j, (at, offset) in enumerate(taps(b)):
            moved = dot(mover(offset), act_g[b, 0]).astype(BF16)
            low = at - at % 128
            product = dot(moved, weights(CONV_AT[b][0], low, low + 512))
            if at % 128:
                product = pltpu.roll(product, 512 - at % 128, 1)
            if j == 0:
                conv_in[...] = product
            else:
                conv_in[...] += product
        conv_in[:, :H] += narrow(b, 3)

    def forward_out(b):
        norm_forward(
            conv_in, H, narrow(b, 4), narrow(b, 5), act_h.at[1], unit_h.at[b, 1], slope_h.at[b, 1], spread_h.at[b, 1]
        )
        act_g[b, 1] = dot(act_h[1], perm_h[...]).astype(BF16)
        return (x_one[...] + dot(act_g[b, 1], weight_out(b))) + wide(b, 2)

    forward_in(0)
    gathers[ENC].third()
    gathers[DEC].second()
    gathers[ENC].last()
    forward_conv(0)
    gathers[DEC].third()
    x_one[...] = forward_out(0)
    gathers[DEC].last()
    forward_in(1)
    forward_conv(1)
    out[...] = forward_out(1).T.astype(BF16)

    reduces = [
        Reduce(place, grads[k], moments[k], rooms[8 * k : 8 * k + 8]) for k in range(3)
    ]
    once = lax.axis_index("dp") == 0
    grouped = (slice(None),)

    def put_grads(chunk, low, values, add=False):
        store(grads[chunk], chunk, low, values.reshape(OWNERS, ROWS, values.shape[-1]), lead=grouped, add=add)

    def fold_moment(chosen):
        @pl.when(once)
        def _():
            def put(chunk, low, rows, values):
                if chunk == chosen:
                    half = (MOMENT_DECAY * values).astype(F32)
                    store(grads[chunk], chunk, low, half, lead=(0,), rows=rows, add=True)

            lay_out(*shard, put)

    rows_w, rows_n = [None] * 6, [None] * 12

    def keep_low(rows, dx):
        act_h[0, rows, :] = dx.astype(BF16)

    def backward_out(b):
        rows_w[3 * b + 2] = jnp.sum(wide_grad[...], axis=0, keepdims=True)
        e3 = wide_grad[...].astype(BF16)
        chunk, at = OUT_AT[b]
        product = dot_tn(act_g[b, 1], e3).astype(BF16)
        put_grads(chunk, at, jnp.concatenate([product, jnp.zeros((GROUPED, 896 - D), BF16)], axis=1))
        back = dot_nt(e3, weight_out(b)).astype(BF16)
        spare[:, :H] = dot_nt(back, perm_h[...])
        sums = norm_backward(
            spare, H, narrow(b, 4), unit_h.at[b, 1], slope_h.at[b, 1], spread_h.at[b, 1], keep_low
        )
        rows_n[6 * b + 4], rows_n[6 * b + 5], rows_n[6 * b + 3] = sums

    def backward_conv(b):
        span = CONV_LANES[b][1] - CONV_LANES[b][0]
        e_all[:, :span] = jnp.zeros((TOK, span), BF16)
        for at, offset in taps(b):
            moved = dot(mover(-offset), act_h[0])
            moved = jnp.concatenate([moved, jnp.zeros((TOK, 512 - H), F32)], axis=1)
            if at % 128:
                moved = pltpu.roll(moved, at % 128, 1)
            low = at - at % 128
            e_all[:, low : low + 512] += moved.astype(BF16)
        chunk = CONV_AT[b][0]
        width = WIDTH[chunk]
        act_t[...] = act_g[b, 0].T

        def piece(q):
            lanes = pl.ds(pl.multiple_of(q * width, 128), width)
            return (q // 4, q // 2 % 2, q % 2), lanes

        def body(q, carry):
            at, lanes = piece(q)
            product = dot(act_t[...], e_all[:, lanes]).astype(BF16)
            grads[chunk][(slice(None),) + at] = product.reshape(OWNERS, ROWS, width)
            return carry

        lax.fori_loop(0, span // width, body, 0)
        rest = span // width * width
        if rest < span:
            put_grads(chunk, rest, dot(act_t[...], e_all[:, rest:span]).astype(BF16))

    def backward_hidden(b):
        span = CONV_LANES[b][1] - CONV_LANES[b][0]
        chunk = CONV_AT[b][0]
        width = WIDTH[chunk]

        def body(q, total):
            lanes = pl.ds(pl.multiple_of(q * width, 128), width)
            values = full[chunk][:, q // 4, q // 2 % 2, q % 2].reshape(GROUPED, width)
            return total + dot_nt(e_all[:, lanes], values)

        back = lax.fori_loop(0, span // width, body, jnp.zeros((TOK, GROUPED), F32))
        rest = span // width * width
        if rest < span:
            back = back + dot_nt(e_all[:, rest:span], weights(chunk, rest, span))
        spare[:, :H] = dot_nt(back.astype(BF16), perm_h[...])
        sums = norm_backward(
            spare, H, narrow(b, 1), unit_h.at[b, 0], slope_h.at[b, 0], spread_h.at[b, 0], keep_low
        )
        rows_n[6 * b + 1], rows_n[6 * b + 2], rows_n[6 * b + 0] = sums

    def backward_weight_in(b):
        chunk, at = IN_AT[b]
        tall[...] = dot_tn(act_d[b], act_h[0])
        zeros = jnp.zeros((SHARD, 512 - H), F32)
        for i in range(OWNERS):
            slot = other_owner(own, i)
            first = tall[2 * SHARD * i : 2 * SHARD * i + SHARD, :]
            second = tall[2 * SHARD * i + SHARD : 2 * SHARD * (i + 1), :]
            low = jnp.concatenate([first, zeros], axis=1)
            high = pltpu.roll(jnp.concatenate([second, zeros], axis=1), H % 128, 1)
            whole = jnp.concatenate([low[:, :384], low[:, 384:] + high[:, :128], high[:, 128:]], axis=1)
            store(grads[chunk], chunk, at, whole.astype(BF16), lead=(slot,), rows=slice(0, SHARD))
        store(
            grads[chunk], chunk, at, jnp.zeros((OWNERS, ROWS - SHARD, 896), BF16), lead=grouped, rows=slice(SHARD, ROWS)
        )

    def backward_in(b):
        x_one[...] = dot_nt(act_h[0], w_in[b])

        def add_up(rows, dx):
            wide_grad[rows, :] += dx

        sums = norm_backward(
            x_one, D, wide(b, 0), unit_d.at[b], slope_d.at[b], spread_d.at[b], add_up
        )
        rows_w[3 * b + 0], rows_w[3 * b + 1] = sums[0], sums[1]

    for fetch in moment_fetches:
        fetch.wait()
    backward_out(1)
    backward_conv(1)
    backward_hidden(1)
    backward_weight_in(1)
    fold_moment(DEC)
    reduces[DEC].core()
    backward_in(1)
    backward_out(0)
    reduces[DEC].plane()
    backward_conv(0)
    fold_moment(ENC)
    reduces[ENC].core()
    reduces[DEC].turn()
    backward_hidden(0)
    reduces[ENC].plane()
    backward_weight_in(0)
    reduces[DEC].cross()
    backward_in(0)
    for m in range(12):
        vec_n[m : m + 1, :] = rows_n[m]
    for m in range(6):
        vec_w[m : m + 1, :] = rows_w[m]
    low_n, low_w = vec_n[...].astype(BF16), vec_w[...].astype(BF16)
    for s in range(OWNERS):
        three = [dot_nt(low_n, put_narrow(s))] + [dot_nt(low_w, put_wide(s, h)) for h in range(2)]
        three.append(jnp.zeros((ROWS - 48, 128), F32))
        store(grads[MIX], MIX, VEC_AT, jnp.concatenate(three, axis=0).astype(BF16), lead=(s,))
        store(grads[MIX], MIX, VEC_AT + 128, jnp.zeros((ROWS, 128), BF16), lead=(s,))
    fold_moment(MIX)
    reduces[MIX].core()
    grad_tokens[...] = wide_grad[...].T
    reduces[ENC].turn()
    reduces[MIX].plane()

    spread_moments = []

    def to_owners(chunk):
        reduces[chunk].finish()
        for k, owner in enumerate(owners):
            if owner.matrix["chunk"] == chunk:
                owner.gather(moments[chunk], window, own_send, own_recv, k)

        def view(y, x, c, rows):
            return moments[chunk].at[y, x, c, rows]

        spread_moments.append(Gather(place, view))
        spread_moments[-1].first()

    to_owners(DEC)
    reduces[ENC].cross()
    reduces[MIX].turn()
    to_owners(ENC)
    reduces[MIX].cross()
    to_owners(MIX)
    for k, owner in enumerate(owners):

        @pl.when(owner.here)
        def _(owner=owner, k=k):
            owner.gathered(moments[owner.matrix["chunk"]], window, own_send, own_recv, k)

    orthogonalize(owners, window, gram, poly, halves)
    for owner in owners:

        @pl.when(owner.here)
        def _(owner=owner):
            owner.spread(window, parts[owner.matrix["chunk"]], back_send, back_recv)

    for gather in spread_moments:
        gather.second()
    for gather in spread_moments:
        gather.third()
    spread_updates = []
    for chunk in (DEC, MIX, ENC):
        for owner in owners:
            if owner.matrix["chunk"] == chunk:
                owner.arrived(window, parts[chunk], back_send, back_recv)
        updates[chunk][place.y, place.x, place.c] = parts[chunk][0] + parts[chunk][1]

        def view(y, x, c, rows, chunk=chunk):
            return updates[chunk].at[y, x, c, rows]

        spread_updates.append(Gather(place, view))
        spread_updates[-1].first()
    for gather in spread_updates:
        gather.second()
    for gather in spread_updates:
        gather.third()
    for gather in spread_moments + spread_updates:
        gather.last()
    for k, owner in enumerate(owners):
        chunk = owner.matrix["chunk"]
        owner.gather_sent(moments[chunk], window, own_send, own_recv, k)
        owner.spread_sent(window, parts[chunk], back_send, back_recv)
    place.finish()


def run_step(extra, dilation, lengths, params, tokens, cotangent, moments):
    in_vmem = pl.BlockSpec(memory_space=pltpu.VMEM)
    in_smem = pl.BlockSpec(memory_space=pltpu.SMEM)
    anywhere = pl.BlockSpec(memory_space=pl.ANY)

    def dma(n):
        return pltpu.SemaphoreType.DMA((n,))

    def pieces(chunk, lead, dtype=BF16):
        return vmem(lead + (2, 2, 2, ROWS, WIDTH[chunk]), dtype)

    shared = [jax.ShapeDtypeStruct((2, 2, 2, ROWS, w), BF16) for w in WIDTH]
    scratch = [dma(96), dma(96), dma(6), dma(32), dma(32), dma(6), dma(12)]
    scratch += [pieces(k, (OWNERS,)) for k in range(3)] * 2
    scratch += [vmem((2, ROWS, w), BF16) for w in WIDTH]
    scratch += [vmem((OWNERS, ROWS, WINDOW), BF16)]
    scratch += [vmem(a.shape, a.dtype) for a in (tokens, cotangent) + tuple(params)]
    scratch += [
        vmem((TOK, TOK), jnp.int32),
        vmem((H, GROUPED), BF16),
        vmem((16, D), F32),
        vmem((16, H), F32),
        vmem((2, D, H), BF16),
        vmem((TOK, D), F32),
        vmem((TOK, D), F32),
        vmem((D, H), F32),
        vmem((2, TOK, D), BF16),
        vmem((2, TOK, H), BF16),
        vmem((2, 2, TOK, GROUPED), BF16),
        vmem((GROUPED, TOK), BF16),
        vmem((TOK, 2048), BF16),
        vmem((2, TOK, D), BF16),
        vmem((2, TOK, D), BF16),
        vmem((2, TOK, 128), F32),
        vmem((2, 2, TOK, H), BF16),
        vmem((2, 2, TOK, H), BF16),
        vmem((2, 2, TOK, 128), F32),
        vmem((512, 512), F32),
        vmem((512, 512), BF16),
        vmem((2, GROUPED, 512), BF16),
    ]
    for chunk in range(3):
        scratch += reduce_room(chunk, extra)
    return pl.pallas_call(
        functools.partial(step_kernel, extra),
        out_shape=(
            jax.ShapeDtypeStruct((D, TOK), BF16),
            jax.ShapeDtypeStruct((D, TOK), F32),
            *shared,
            *shared,
        ),
        in_specs=[in_smem] * 2 + [anywhere] * 12,
        out_specs=(in_vmem,) * 8,
        scratch_shapes=scratch,
        compiler_params=pltpu.CompilerParams(
            collective_id=0, has_side_effects=True, vmem_limit_bytes=60 << 20
        ),
        name="step",
    )(dilation, lengths, tokens, cotangent, *params, *moments)


def finish_kernel(
    vector_step, moment_mix, moment_enc, moment_dec, update_mix, update_enc, update_dec,
    conv, w_in, w_out, wide, narrow,
    mom_in, mom_conv, mom_out, mom_wide, mom_narrow,
    new_in, new_conv, new_out, new_wide, new_narrow, low_in, low_conv, low_out,
):
    moments = (moment_mix, moment_enc, moment_dec)
    updates = (update_mix, update_enc, update_dec)

    def conv_lanes(refs, low, high):
        if high <= 1920:
            return load(refs[ENC], ENC, low, high, rows=slice(0, SHARD)).astype(F32)
        if low >= 2048:
            return load(refs[DEC], DEC, low - 1920, high - 1920, rows=slice(0, SHARD)).astype(F32)
        enc = load(refs[ENC], ENC, 1920, 2048, rows=slice(0, SHARD)).astype(F32)
        dec = load(refs[DEC], DEC, 0, 128, rows=slice(0, SHARD)).astype(F32)
        return jnp.where(iota((SHARD, 128), 1) < SPLIT - 1920, enc, dec)

    for low, high in ((0, 1920), (1920, 2048), (2048, 3200)):
        lanes = slice(low, high)
        mom_conv[:, lanes] = conv_lanes(moments, low, high)
        value = conv[:, lanes] - conv_lanes(updates, low, high)
        new_conv[:, lanes] = value
        low_conv[:, lanes] = value.astype(BF16)
    vectors = load(moment_mix, MIX, VEC_AT, VEC_AT + 128).astype(F32)
    for b in range(2):
        chunk, at = OUT_AT[b]

        def out_lanes(refs):
            return load(refs[chunk], chunk, at, at + 896, rows=slice(0, SHARD)).astype(F32)[:, :D]

        mom_out[:, b, :] = out_lanes(moments)
        value = w_out[:, b, :] - out_lanes(updates)
        new_out[:, b, :] = value
        low_out[b] = value.astype(BF16)
        chunk, at = IN_AT[b]

        def in_lanes(refs, h):
            values = load(refs[chunk], chunk, at + 384 * h, at + 384 * h + 512, rows=slice(0, SHARD)).astype(F32)
            if h:
                values = pltpu.roll(values, 512 - H % 128, 1)
            return values[:, :H]

        for h in range(2):
            rows = slice(h * SHARD, (h + 1) * SHARD)
            mom_in[b, rows, :] = in_lanes(moments, h)
            value = w_in[b, rows, :] - in_lanes(updates, h)
            new_in[b, rows, :] = value
            low_in[b, rows, :] = value.astype(BF16)
        for k in range(6):
            m = 6 * b + k
            value = vectors[m : m + 1, :SHARD]
            mom_narrow[k, b : b + 1, :] = value
            new_narrow[k, b : b + 1, :] = narrow[k, b : b + 1, :] - vector_step * value
        for k in range(3):
            for h in range(2):
                m = 16 + 16 * h + 3 * b + k
                lanes = slice(h * SHARD, (h + 1) * SHARD)
                value = vectors[m : m + 1, :SHARD]
                mom_wide[k, b : b + 1, lanes] = value
                new_wide[k, b : b + 1, lanes] = wide[k, b : b + 1, lanes] - vector_step * value


def finish(vector_step, shared, params):
    in_vmem = pl.BlockSpec(memory_space=pltpu.VMEM)
    conv, w_in, w_out, wide, narrow = params
    shapes = [w_in.shape, conv.shape, w_out.shape, wide.shape, narrow.shape]
    outs = [jax.ShapeDtypeStruct(s, F32) for s in shapes + shapes]
    outs += [jax.ShapeDtypeStruct(s, BF16) for s in shapes[:2] + [(2, SHARD, D)]]
    return pl.pallas_call(
        functools.partial(finish_kernel, vector_step),
        out_shape=tuple(outs),
        in_specs=[in_vmem] * 11,
        out_specs=(in_vmem,) * len(outs),
        compiler_params=pltpu.CompilerParams(vmem_limit_bytes=40 << 20),
        name="finish",
    )(*shared, *params)


def swap(array):
    return jnp.transpose(array, (1, 0, 2))


def shards(
    extra, vector_step, tokens, cotangent, lengths, dilation, proj_in, conv_weight, proj_out, vec_wide, vec_narrow,
    mom_in, mom_conv, mom_out, mom_wide, mom_narrow,
):
    params = (conv_weight, proj_in, swap(proj_out), swap(vec_wide), swap(vec_narrow))
    moments = (mom_conv, mom_in, swap(mom_out), swap(mom_wide), swap(mom_narrow))
    out, grad_tokens, *shared = run_step(extra, dilation, lengths, params, tokens.T, cotangent.T, moments)
    rest = list(finish(vector_step, shared, params))
    for k in (2, 3, 4, 7, 8, 9):
        rest[k] = swap(rest[k])
    return (out.T, grad_tokens.T) + tuple(rest)


def solution(mesh):
    groups, owners = mesh.shape["dp"], mesh.shape["fsdp"]
    assert owners == OWNERS and groups % PIECES == 0
    extra, bit = [], PIECES
    while bit < groups:
        extra.append(bit)
        bit *= 2
    assert bit == groups
    vector_step = VECTOR_RATE / math.sqrt(TOK * groups * owners)
    tok, rep = P(("dp", "fsdp"), None), P()
    mid, first, final = P(None, "fsdp", None), P("fsdp", None), P(None, None, "fsdp")
    params = (mid, first, mid, final, final)
    return jax.shard_map(
        functools.partial(shards, tuple(extra), vector_step),
        mesh=mesh,
        in_specs=(tok, tok, tok, rep) + params + params,
        out_specs=(tok, tok) + params + params + (mid, first, mid),
        check_vma=False,
    )
```

```python
import functools
import math

import jax
import jax.numpy as jnp
from jax import lax
from jax.experimental import pallas as pl
from jax.experimental.pallas import tpu as pltpu
from jax.sharding import PartitionSpec as P

D = 800
H = 400
K_ENC = 5
K_DEC = 3
NS_STEPS = 5
EPSILON = 1e-05
NORM_FLOOR = 1e-07
COEF_A = 3.4445
COEF_B = -4.775
COEF_C = 2.0315
MOMENT_DECAY = 0.5
MATRIX_RATE = 0.5
VECTOR_RATE = 0.1

F32 = jnp.float32
BF16 = jnp.bfloat16
MESH = pl.DeviceIdType.MESH

OWNERS = 4
PIECES = 8
SHARD = 100
ROWS = 112
IN0, CONV0, OUT0, MID1, OUT1 = range(5)
WIDTH = (128, 256, 128, 256, 128)
UNITS = range(len(WIDTH))
IN_AT = ((IN0, 0), (MID1, 1200))
OUT_AT = ((OUT0, 0), (OUT1, 0))
CONV_AT = ((CONV0, 0), (MID1, 0))
CONV_SPAN = (2048, 1280)
VEC_AT = 896
SPLIT = K_ENC * H
TOK = 256
GROUPED = OWNERS * ROWS
WINDOW = 2048

GELU_K = math.sqrt(2.0 / math.pi)
GELU_C = 0.044715


def vmem(shape, dtype):
    return pltpu.VMEM(shape, dtype)


def dot(a, b):
    return lax.dot_general(a, b, (((1,), (0,)), ((), ())), preferred_element_type=F32)


def dot_nt(a, b):
    return lax.dot_general(a, b, (((1,), (1,)), ((), ())), preferred_element_type=F32)


def dot_tn(a, b):
    return lax.dot_general(a, b, (((0,), (0,)), ((), ())), preferred_element_type=F32)


def one_hot(mask):
    return jnp.where(mask, 1.0, 0.0).astype(BF16)


def iota(shape, dim):
    return lax.broadcasted_iota(jnp.int32, shape, dim)


def add_low(*parts):
    total = parts[0].astype(F32)
    for part in parts[1:]:
        total = total + part.astype(F32)
    return total.astype(BF16)


def spans(chunk, low, high):
    width = WIDTH[chunk]
    for q in range(low // width, -(-high // width)):
        yield q, max(low - q * width, 0), min(high - q * width, width)


def load(ref, chunk, low, high, lead=(), rows=slice(None)):
    parts = []
    for q, start, stop in spans(chunk, low, high):
        parts.append(ref[lead + (q // 4, q // 2 % 2, q % 2, rows, slice(start, stop))])
    return parts[0] if len(parts) == 1 else jnp.concatenate(parts, axis=-1)


def store(ref, chunk, low, value, lead=(), rows=slice(None), add=False):
    at = 0
    for q, start, stop in spans(chunk, low, low + value.shape[-1]):
        index = lead + (q // 4, q // 2 % 2, q % 2, rows, slice(start, stop))
        part = value[..., at : at + stop - start]
        ref[index] = add_low(ref[index], part) if add else part
        at += stop - start


def shifted(values, at, low, high):
    rows, count = values.shape
    base = at - at % 128
    width = -(-(at % 128 + count) // 128) * 128
    parts = []
    if base > low:
        parts.append(jnp.zeros((rows, base - low), F32))
    if width > count:
        values = jnp.concatenate([values, jnp.zeros((rows, width - count), F32)], axis=1)
    parts.append(pltpu.roll(values, at % 128, 1) if at % 128 else values)
    if high > base + width:
        parts.append(jnp.zeros((rows, high - base - width), F32))
    return parts[0] if len(parts) == 1 else jnp.concatenate(parts, axis=1)


def lane_window(at, count):
    return at - at % 128, -(-(at + count) // 128) * 128


def unshifted(values, at, count):
    if at % 128:
        values = pltpu.roll(values, values.shape[1] - at % 128, 1)
    return values[:, :count]


def lay_out(unit, conv, w_in, w_out, wide, narrow, put):
    rows = slice(0, SHARD)
    for b in range(2):
        if unit == CONV_AT[b][0]:
            low, high = (0, SPLIT) if b == 0 else (SPLIT, SPLIT + K_DEC * H)
            start, stop = lane_window(low, high - low)
            stop = min(stop, 3200)
            values = unshifted(conv[:, start:stop], low, high - low)
            put(0, rows, values, False)
        if unit == OUT_AT[b][0]:
            put(0, rows, w_out[:, b, :], False)
        if unit == IN_AT[b][0]:
            at = IN_AT[b][1]
            low, high = lane_window(at, 2 * H)
            values = shifted(w_in[b, :SHARD, :], at, low, high) + shifted(w_in[b, SHARD:, :], at + H, low, high)
            put(low, rows, values, True)
    if unit == IN0:
        for b in range(2):
            for k in range(6):
                m = 6 * b + k
                put(VEC_AT, slice(m, m + 1), narrow[k, b : b + 1, :], False)
            for k in range(3):
                for h in range(2):
                    m = 16 + 16 * h + 3 * b + k
                    put(VEC_AT, slice(m, m + 1), wide[k, b : b + 1, h * SHARD : (h + 1) * SHARD], False)


def flip(value, bit):
    return value + bit - 2 * bit * ((value // bit) % 2)


def other_owner(own, step):
    if step == 0:
        return own
    if step == 3:
        return 3 - own
    return flip(own, step)


def remote(src, dst, send, recv, device):
    return pltpu.make_async_remote_copy(
        src_ref=src,
        dst_ref=dst,
        send_sem=send,
        recv_sem=recv,
        device_id=device,
        device_id_type=MESH,
    )


class Place:
    def __init__(self, send, recv, extra):
        at = lax.axis_index("dp")
        self.piece = at % PIECES
        self.base = at - self.piece
        self.me = at
        self.own = lax.axis_index("fsdp")
        self.y, self.x, self.c = self.piece // 4, self.piece // 2 % 2, self.piece % 2
        self.core, self.near_x, self.near_y = [
            (self.base + flip(self.piece, bit), self.own) for bit in (1, 2, 4)
        ]
        self.near_xy = (self.base + flip(flip(self.piece, 2), 4), self.own)
        self.column = [(at, other_owner(self.own, step)) for step in (1, 2, 3)]
        self.far = [(flip(at, bit), self.own) for bit in extra]
        self.inner = (self.own == 1) | (self.own == 2)
        self.send, self.recv, self.used = send, recv, 0
        self.started = []

    def take(self, count):
        first = self.used
        self.used += count
        return first

    def start(self, src, dst, device):
        k = self.take(1)
        copy = remote(src, dst, self.send.at[k], self.recv.at[k], device)
        copy.start()
        self.started.append(copy)
        return copy

    def sent(self):
        for copy in self.started:
            copy.wait_send()
        self.started = []


class Direct:
    ALL = slice(None)

    def __init__(self, place, ref):
        self.place, self.ref = place, ref

    def first(self):
        p = self.place
        mine = self.ref.at[p.y, p.x, p.c]
        self.copies = [p.start(mine, mine, device) for device in (p.near_x, p.near_y, p.near_xy)]

    def second(self):
        p = self.place
        for copy in self.copies:
            copy.wait_recv()
        pieces = self.ref.at[self.ALL, self.ALL, p.c]
        self.copies = [p.start(pieces, pieces, p.core)]

    def last(self):
        self.copies[0].wait_recv()


class Gather:
    LOW, HIGH, ALL = pl.ds(0, 64), pl.ds(64, 48), slice(None)

    def __init__(self, place, view):
        self.place, self.view = place, view

    def move(self, device, *index):
        ref = self.view(*index)
        return self.place.start(ref, ref, device)

    def first(self):
        p = self.place
        self.a = self.move(p.near_y, p.y, p.x, p.c, self.LOW)
        self.b = self.move(p.near_x, p.y, p.x, p.c, self.HIGH)

    def second(self):
        p = self.place
        self.a.wait_recv()
        self.a = self.move(p.near_x, self.ALL, p.x, p.c, self.LOW)
        self.b.wait_recv()
        self.b = self.move(p.near_y, p.y, self.ALL, p.c, self.HIGH)

    def third(self):
        p = self.place
        self.a.wait_recv()
        self.b.wait_recv()
        self.a = self.move(p.core, self.ALL, self.ALL, p.c, self.ALL)

    def last(self):
        self.a.wait_recv()


class WeightGather(Gather):
    def __init__(self, place, ref, low, width):
        lanes = pl.ds(low, width)

        def view(y, x, c, rows):
            return ref.at[pl.ds(1, 3), y, x, c, rows, lanes]

        super().__init__(place, view)
        self.ref, self.lanes = ref, lanes

    def slot(self, step):
        p = self.place
        return self.ref.at[step, p.y, p.x, p.c, :, self.lanes]

    def cross(self):
        p = self.place
        self.crossing = [p.start(self.slot(0), self.slot(step), p.column[step - 1]) for step in (1, 2)]
        k = p.take(1)
        self.direct = remote(self.slot(0), self.slot(3), p.send.at[k], p.recv.at[k], p.column[2])
        relay = p.take(1)
        self.relay = remote(self.slot(2), self.slot(3), p.send.at[relay], p.recv.at[k], p.column[0])

        @pl.when(p.inner)
        def _():
            self.direct.start()

    def first(self, followers=()):
        p = self.place
        self.crossing[1].wait_recv()

        @pl.when(p.inner)
        def _():
            self.relay.start()

        self.crossing[0].wait_recv()
        self.direct.wait_recv()
        for follower in followers:
            follower.cross()
        super().first()

    def finish(self):
        @pl.when(self.place.inner)
        def _():
            self.direct.wait_send()
            self.relay.wait_send()


class Reduce:
    def __init__(self, place, grads, moment, room):
        self.place, self.grads, self.moment = place, grads, moment
        self.from_core, self.sums, self.from_x, self.from_y = room[:4]
        self.last_x, self.last_y, self.from_z, self.from_far = room[4:]

    def core(self):
        p = self.place
        self.halves = []
        for y in (1 - p.y, p.y):
            src = self.grads.at[:, y, :, 1 - p.c]
            self.halves.append((y, p.start(src, self.from_core.at[:, y], p.core)))

    def plane(self):
        p = self.place
        self.a = []
        for k, (y, copy) in enumerate(self.halves):
            copy.wait_recv()
            self.sums[:, y] = add_low(self.grads[:, y, :, p.c], self.from_core[:, y])
            self.a.append(
                p.start(self.sums.at[0:2, y, 1 - p.x], self.from_x.at[:, y], p.near_x)
            )
            if k == 0:
                self.b = p.start(self.sums.at[2:4, y], self.from_y, p.near_y)

    def turn(self):
        p = self.place
        y, x = 1 - p.y, 1 - p.x
        self.a[0].wait_recv()
        self.sums[0:2, y, p.x] = add_low(self.sums[0:2, y, p.x], self.from_x[:, y])
        self.y_last = p.start(self.sums.at[0:2, y, p.x], self.last_y, p.near_y)
        self.b.wait_recv()
        self.sums[2:4, p.y, x] = add_low(self.sums[2:4, p.y, x], self.from_y[:, x])
        self.x_last = p.start(self.sums.at[2:4, p.y, x], self.last_x, p.near_x)

    def cross(self):
        p = self.place
        y, x = p.y, p.x
        self.a[1].wait_recv()
        self.y_last.wait_recv()
        self.sums[0:2, y, x] = add_low(self.sums[0:2, y, x], self.from_x[:, y], self.last_y[...])
        self.x_last.wait_recv()
        self.sums[2:4, y, x] = add_low(self.sums[2:4, y, x], self.from_y[:, x], self.last_x[...])
        for k, device in enumerate(p.far):
            p.start(self.sums.at[:, y, x], self.from_far.at[k], device).wait_recv()
            p.started.pop().wait_send()
            self.sums[:, y, x] = add_low(self.sums[:, y, x], self.from_far[k])
        self.crossing = [
            p.start(self.sums.at[step, y, x], self.from_z.at[step - 1], p.column[step - 1])
            for step in (1, 2, 3)
        ]

    def finish(self):
        p = self.place
        for copy in self.crossing:
            copy.wait_recv()
        parts = [self.sums[0, p.y, p.x]] + [self.from_z[k] for k in range(3)]
        self.moment[p.y, p.x, p.c] = add_low(self.moment[p.y, p.x, p.c], *parts)


def reduce_room(chunk, extra):
    width = WIDTH[chunk]
    shapes = (
        (OWNERS, 2, 2), (OWNERS, 2, 2), (2, 2), (2, 2), (2,), (2,), (3,), (max(len(extra), 1), OWNERS),
    )
    return [vmem(shape + (ROWS, width), BF16) for shape in shapes]


MATRICES = (
    dict(kind="row", unit=OUT1, first=0, last=6, piece=6, lanes=(0, D), slot=0, scale=math.sqrt(D / H)),
    dict(kind="row", unit=MID1, first=0, last=4, piece=2, lanes=(0, K_DEC * H), slot=0, scale=1.0),
    dict(kind="in", unit=MID1, first=4, last=7, piece=4, lanes=(176, 976), slot=1, scale=1.0),
    dict(kind="row", unit=OUT0, first=0, last=6, piece=3, lanes=(0, D), slot=0, scale=math.sqrt(D / H)),
    dict(kind="row", unit=CONV0, first=0, last=7, piece=0, lanes=(0, SPLIT), slot=0, scale=1.0),
    dict(kind="in", unit=IN0, first=0, last=6, piece=5, lanes=(0, D), slot=0, scale=1.0),
)
OWNED_AT = (1, 2)


class Owner:
    def __init__(self, place, matrix, half):
        self.place, self.matrix, self.half = place, matrix, half
        at = self.at = OWNED_AT[half]
        self.width = WIDTH[matrix["unit"]]
        self.count = OWNERS * (matrix["last"] - matrix["first"] + 1)
        p = place
        self.here = (p.piece == matrix["piece"]) & (p.own == at)
        self.away = (p.piece != matrix["piece"]) | (p.own != at)
        self.holds = (p.piece >= matrix["first"]) & (p.piece <= matrix["last"])
        self.served = p.own // 2 == half
        self.device = (p.base + matrix["piece"], at)
    def each_served(self, act):
        def body(k, carry):
            piece, own = self.matrix["first"] + k // 2, 2 * self.half + k % 2

            @pl.when((piece != self.matrix["piece"]) | (own != self.at))
            def _():
                act(k // 2, own, (self.place.base + piece, own))

            return carry

        lax.fori_loop(0, self.count // 2, body, 0)

    def lanes(self, k):
        return pl.ds(pl.multiple_of(k * self.width, 128), self.width)

    def to_owner(self, moment, window, send, recv, k):
        p = self.place
        at = p.piece - self.matrix["first"]
        src = moment.at[p.y, p.x, p.c]
        dst = window.at[p.own, :, self.lanes(at)]
        return remote(src, dst, send.at[k], recv.at[0], self.device)

    def gather(self, moment, window, send, recv, k):
        @pl.when(self.holds & self.away)
        def _():
            self.to_owner(moment, window, send, recv, k).start()

        @pl.when(self.here)
        def _():
            p = self.place
            at = p.piece - self.matrix["first"]
            pltpu.make_async_copy(
                moment.at[p.y, p.x, p.c], window.at[p.own, :, self.lanes(at)], recv.at[0]
            ).start()

    def gather_sent(self, moment, window, send, recv, k):
        @pl.when(self.holds & self.away)
        def _():
            self.to_owner(moment, window, send, recv, k).wait_send()

    def whole(self, window, slots, sem):
        values = window.at[slots, :, pl.ds(0, self.count // OWNERS * self.width)]
        return pltpu.make_async_copy(values, values, sem.at[0])

    def gathered(self, window, recv):
        self.whole(window, pl.ds(0, OWNERS), recv).wait()

    def spread(self, window, parts, send, recv, k):
        p = self.place
        slot = parts.at[self.matrix["slot"]]

        def act(at, own, device):
            remote(window.at[own, :, self.lanes(at)], slot, send.at[0], recv.at[k], device).start()

        self.each_served(act)
        at = p.piece - self.matrix["first"]
        pltpu.make_async_copy(window.at[p.own, :, self.lanes(at)], slot, send.at[0]).start()

    def arrived(self, window, parts, send, recv, k):
        @pl.when(self.here)
        def _():
            self.whole(window, pl.ds(2 * self.half, 2), send).wait()

        @pl.when(self.holds & self.served & self.away)
        def _():
            src = window.at[0, :, self.lanes(0)]
            dst = parts.at[self.matrix["slot"]]
            remote(src, dst, send.at[0], recv.at[k], self.device).wait_recv()


def split(a):
    high = a.astype(BF16)
    return high, (a - high.astype(F32)).astype(BF16)


def dot_fine(a, b):
    a_high, a_low = split(a)
    b_high, b_low = split(b)
    return dot(a_high, b_high) + (dot(a_high, b_low) + dot(a_low, b_high))


def dot_low(a, b):
    return dot(a.astype(BF16), b.astype(BF16))


def polynomial_of(gram):
    size = gram.shape[0]
    eye = iota((size, size), 0) == iota((size, size), 1)
    unit = jnp.where(eye, 1.0, 0.0)
    power = jnp.sum(jnp.sum(jnp.where(eye, gram, 0.0), axis=1, keepdims=True), axis=0, keepdims=True)
    inverse = 1.0 / (jnp.sqrt(power) + NORM_FLOOR)
    current = gram * inverse * inverse
    result = None
    for step in range(NS_STEPS):
        square = dot_fine if step > 2 else dot_low
        poly = COEF_A * unit + COEF_B * current + COEF_C * square(current, current)
        result = poly if result is None else dot_low(poly, result)
        if step < NS_STEPS - 1:
            first = dot_fine if step < 2 else dot_low
            second = dot_fine if step < 1 else dot_low
            current = second(first(poly, current), poly)
    return result, inverse


def orthogonalize(owners, window, gram, poly, halves):
    is_row = False
    high, factor, parts = jnp.int32(0), jnp.float32(0), jnp.int32(0)
    half_at = owners[0].place.own // 2
    two = pl.ds(2 * half_at, 2)
    served = pl.ds(pl.multiple_of(2 * ROWS * half_at, 2 * ROWS), 2 * ROWS)
    for owner in owners:
        matrix, here = owner.matrix, owner.here
        if matrix["kind"] == "row":
            is_row = is_row | here
        high = jnp.where(here, matrix["lanes"][1], high)
        parts = jnp.where(here, -(-matrix["lanes"][1] // 512), parts)
        factor = jnp.where(here, MATRIX_RATE * matrix["scale"], factor)
    ins = {}
    for owner in owners:
        if owner.matrix["kind"] == "in":
            at = owner.matrix["lanes"][0]
            ins[at] = ins.get(at, False) | owner.here
    is_in = False
    for here in ins.values():
        is_in = is_in | here

    def part(k):
        lanes = pl.ds(pl.multiple_of(k * 512, 512), 512)
        values = window[:, :, lanes].reshape(GROUPED, 512)
        lane = iota((GROUPED, 512), 1) + k * 512
        return lanes, jnp.where(lane < high, values, jnp.zeros((), BF16))

    for at, here in ins.items():

        @pl.when(here)
        def _(at=at):
            valid = iota((GROUPED, 512), 1) < H
            for h in range(2):
                low = (at + H * h) // 128 * 128
                values = window[:, :, low : low + 512].reshape(GROUPED, 512).astype(F32)
                if (at + H * h) % 128:
                    values = pltpu.roll(values, 512 - (at + H * h) % 128, 1)
                halves[h] = jnp.where(valid, values, 0.0).astype(BF16)

    @pl.when(is_in)
    def _():
        gram[...] = dot_tn(halves[0], halves[0]) + dot_tn(halves[1], halves[1])

    @pl.when(is_row)
    def _():
        gram[...] = jnp.zeros(gram.shape, F32)

        def body(k, carry):
            values = part(k)[1]
            gram[:GROUPED, :GROUPED] += dot_nt(values, values)
            return carry

        lax.fori_loop(0, parts, body, 0)

    @pl.when(is_in | is_row)
    def _():
        result, inverse = polynomial_of(gram[...])
        poly[...] = (result * (inverse * factor)).astype(BF16)

    for at, here in ins.items():

        @pl.when(here)
        def _(at=at):
            window[:, :, :1024] = jnp.zeros((OWNERS, ROWS, 1024), BF16)
            for h in range(2):
                low = (at + H * h) // 128 * 128
                step = dot_nt(halves[h, served], poly[...])
                if (at + H * h) % 128:
                    step = pltpu.roll(step, (at + H * h) % 128, 1)
                lanes = slice(low, low + 512)
                window[two, :, lanes] = add_low(window[two, :, lanes], step.reshape(2, ROWS, 512))

    @pl.when(is_row)
    def _():
        def body(k, carry):
            lanes, values = part(k)
            step = dot(poly[served, :GROUPED], values)
            window[two, :, lanes] = step.astype(BF16).reshape(2, ROWS, 512)
            return carry

        lax.fori_loop(0, parts, body, 0)


def norm_forward(src, width, gain, shift, act, unit, slope, spread, chunk=128):
    def body(k, carry):
        rows = pl.ds(pl.multiple_of(k * chunk, chunk), chunk)
        x = src[rows, :width].astype(F32)
        center = x - jnp.mean(x, axis=1, keepdims=True)
        scale = lax.rsqrt(jnp.mean(center * center, axis=1, keepdims=True) + EPSILON)
        xhat = center * scale
        a = xhat * gain + shift
        square = a * a
        half = 0.5 + 0.5 * jnp.tanh(a * (GELU_K + (GELU_K * GELU_C) * square))
        act[rows, :width] = (a * half).astype(BF16)
        unit[rows, :width] = xhat.astype(BF16)
        inner = GELU_K + (3.0 * GELU_K * GELU_C) * square
        slope[rows, :width] = (half + (2.0 * a * inner) * (half * (1.0 - half))).astype(BF16)
        spread[rows, :] = jnp.broadcast_to(scale, (chunk, 128))
        return carry

    lax.fori_loop(0, TOK // chunk, body, 0)


def fold_rows(values):
    total = values[0:8]
    for k in range(1, values.shape[0] // 8):
        total = total + values[8 * k : 8 * k + 8]
    return total


def norm_backward(grad, width, gain, unit, slope, spread, finish, chunk=128):
    def body(k, sums):
        rows = pl.ds(pl.multiple_of(k * chunk, chunk), chunk)
        da = grad[rows, :width] * slope[rows, :width].astype(F32)
        xhat = unit[rows, :width].astype(F32)
        product = da * xhat
        dxhat = da * gain
        mean_one = jnp.mean(dxhat, axis=1, keepdims=True)
        mean_two = jnp.mean(dxhat * xhat, axis=1, keepdims=True)
        dx = spread[rows, 0:1] * (dxhat - mean_one - xhat * mean_two)
        finish(rows, dx)
        return (sums[0] + fold_rows(product), sums[1] + fold_rows(da), sums[2] + fold_rows(dx))

    zero = jnp.zeros((8, width), F32)
    sums = lax.fori_loop(0, TOK // chunk, body, (zero, zero, zero))
    return tuple(jnp.sum(s, axis=0, keepdims=True) for s in sums)


def step_kernel(
    extra,
    dilation, lengths, tokens_hbm, cotangent_hbm,
    conv_hbm, in_hbm, out_hbm, wide_hbm, narrow_hbm,
    mom_conv_hbm, mom_in_hbm, mom_out_hbm, mom_wide_hbm, mom_narrow_hbm,
    *refs,
):
    results = refs[:12]
    refs = refs[12:]
    out, grad_tokens, moments, updates = refs[0], refs[1], refs[2:7], refs[7:12]
    refs = refs[2:]
    send, recv, own_send, own_recv, back_send, back_recv, local = refs[10:17]
    full, grads, parts = refs[17:22], refs[22:27], refs[27:32]
    rooms = refs[32:72]
    (
        window,
        tokens, cotangent, conv, in_shard, out_shard, wide_shard, narrow_shard,
        far, perm_h, vec_w, vec_n, w_in, x_one, wide_grad, tall,
        masks, act_d, act_h, act_g, act_t, e_all,
        unit_d, slope_d, spread_d, unit_h, slope_h, spread_h,
        gram, poly, halves,
    ) = refs[72:]
    place = Place(send, recv, extra)
    own = place.own
    owners = [Owner(place, matrix, half) for matrix in MATRICES for half in range(2)]
    conv_in, spare = gram.at[:TOK], gram.at[TOK:]
    hid = spare

    results = [
        pltpu.make_async_copy(source, target, local.at[12 + k])
        for k, (source, target) in enumerate(zip((out, grad_tokens) + moments + updates, results))
    ]

    sources = (conv_hbm, in_hbm, out_hbm, wide_hbm, narrow_hbm, tokens_hbm, cotangent_hbm)
    shard = (conv, in_shard, out_shard, wide_shard, narrow_shard)
    targets = shard + (tokens, cotangent)
    fetches = [pltpu.make_async_copy(s, t, local.at[k]) for k, (s, t) in enumerate(zip(sources, targets))]
    for fetch in fetches:
        fetch.start()
    barrier = pltpu.get_barrier_semaphore()
    for device in [place.core, place.near_x, place.near_y] + place.column + place.far:
        pl.semaphore_signal(barrier, inc=1, device_id=device, device_id_type=MESH)

    def pack(unit):
        full[unit][0] = jnp.zeros(full[unit].shape[1:], BF16)

        def put(low, rows, values, add):
            store(full[unit], unit, low, values.astype(BF16), lead=(0,), rows=rows, add=add)

        lay_out(unit, *shard, put)

    in_unit = WeightGather(place, full[IN0], 0, 128)
    conv_unit = WeightGather(place, full[CONV0], 0, 256)
    out_unit = WeightGather(place, full[OUT0], 0, 128)
    mid_unit = WeightGather(place, full[MID1], 0, 256)
    last_unit = WeightGather(place, full[OUT1], 0, 128)

    for k in (1, 3, 4):
        fetches[k].wait()
    pack(IN0)
    pl.semaphore_wait(barrier, 6 + len(extra))
    in_unit.cross()
    fetches[0].wait()
    pack(CONV0)
    conv_unit.cross()
    fetches[2].wait()
    for unit in (OUT0, MID1, OUT1):
        pack(unit)
    sources = (mom_conv_hbm, mom_in_hbm, mom_out_hbm, mom_wide_hbm, mom_narrow_hbm)
    moment_fetches = [pltpu.make_async_copy(s, t, local.at[7 + k]) for k, (s, t) in enumerate(zip(sources, shard))]
    for fetch in moment_fetches:
        fetch.start()

    row, col = iota((TOK, TOK), 0), iota((TOK, TOK), 1)
    seg_row, seg_col = jnp.zeros((TOK, TOK), jnp.int32), jnp.zeros((TOK, TOK), jnp.int32)
    end = jnp.int32(0)
    for k in range(8):
        end = end + lengths[0, k]
        seg_row = seg_row + jnp.where(row >= end, 1, 0)
        seg_col = seg_col + jnp.where(col >= end, 1, 0)
    far[...] = jnp.where(seg_row == seg_col, col - row, 4 * TOK)

    enc_shifts = [(j - K_ENC // 2) * dilation[0] for j in range(K_ENC)]
    dec_shifts = [j * dilation[1] for j in range(1 - K_DEC, K_DEC)]
    for k, shift in enumerate(enc_shifts + dec_shifts):
        masks[k] = one_hot(far[...] == shift)
    tap_masks = (
        [(j, K_ENC - 1 - j) for j in range(K_ENC)],
        [(K_ENC + K_DEC - 1 - j, K_ENC + K_DEC - 1 + j) for j in range(K_DEC)],
    )

    in_unit.first([out_unit, mid_unit])
    row, col = iota((H, GROUPED), 0), iota((H, GROUPED), 1)
    used = jnp.zeros((H, GROUPED), jnp.int32)
    for s in range(OWNERS):
        r = col - ROWS * s
        inside = (r >= 0) & (r < SHARD) & (row == r + SHARD * other_owner(own, s))
        used = used + jnp.where(inside, 1, 0)
    perm_h[...] = used.astype(F32).astype(BF16)
    in_unit.second()
    conv_unit.first([last_unit])
    fetches[5].wait()
    x_one[...] = tokens[...].astype(F32).T
    in_unit.third()
    conv_unit.second()
    fetches[6].wait()
    wide_grad[...] = cotangent[...].astype(F32).T
    in_unit.last()

    row_n, col_n = iota((128, H), 0), iota((128, H), 1)
    row_w, col_w = iota((128, D), 0), iota((128, D), 1)

    def put_narrow(s):
        return one_hot((col_n == row_n + SHARD * other_owner(own, s)) & (row_n < SHARD))

    def put_wide(s, h):
        return one_hot((col_w == row_w + SHARD * (2 * other_owner(own, s) + h)) & (row_w < SHARD))

    total_n, total_w = jnp.zeros((16, H), F32), jnp.zeros((16, D), F32)
    for s in range(OWNERS):
        vectors = load(full[IN0], IN0, VEC_AT, VEC_AT + 128, lead=(s,))
        total_n = total_n + dot(vectors[0:16], put_narrow(s))
        for h in range(2):
            total_w = total_w + dot(vectors[16 + 16 * h : 32 + 16 * h], put_wide(s, h))
    vec_n[...] = total_n
    vec_w[...] = total_w

    def narrow(b, k):
        return vec_n[6 * b + k : 6 * b + k + 1, :]

    def wide(b, k):
        return vec_w[3 * b + k : 3 * b + k + 1, :]

    def weights(unit, low, high):
        return load(full[unit], unit, low, high, lead=(slice(None),)).reshape(GROUPED, high - low)

    def weight_out(b):
        return weights(OUT_AT[b][0], 0, 896)[:, :D]

    def place_in(b):
        unit, at = IN_AT[b]
        for i in range(OWNERS):
            slot = other_owner(own, i)
            for h in range(2):
                low, high = lane_window(at + H * h, H)
                values = load(full[unit], unit, low, high, lead=(slot,)).astype(F32)[:SHARD]
                row_at = SHARD * (2 * i + h)
                tall[row_at : row_at + SHARD, :] = unshifted(values, at + H * h, H)
        w_in[b] = tall[...].astype(BF16)

    def taps(b):
        return [(H * j, forward, backward) for j, (forward, backward) in enumerate(tap_masks[b])]

    def forward_in(b):
        norm_forward(x_one, D, wide(b, 0), wide(b, 1), act_d.at[b], unit_d.at[b], slope_d.at[b], spread_d.at[b])
        place_in(b)
        hid[:, :H] = dot(act_d[b], w_in[b]) + narrow(b, 0)
        norm_forward(
            hid, H, narrow(b, 1), narrow(b, 2), act_h.at[0], unit_h.at[b, 0], slope_h.at[b, 0], spread_h.at[b, 0]
        )
        act_g[b, 0] = dot(act_h[0], perm_h[...]).astype(BF16)

    def forward_conv(b):
        for j, (at, mask, unused) in enumerate(taps(b)):
            moved = dot(masks[mask], act_g[b, 0]).astype(BF16)
            low = at - at % 128
            product = dot(moved, weights(CONV_AT[b][0], low, low + 512))
            if at % 128:
                product = pltpu.roll(product, 512 - at % 128, 1)
            if j == 0:
                conv_in[...] = product
            else:
                conv_in[...] += product
        conv_in[:, :H] += narrow(b, 3)

    def forward_out(b):
        norm_forward(
            conv_in, H, narrow(b, 4), narrow(b, 5), act_h.at[1], unit_h.at[b, 1], slope_h.at[b, 1], spread_h.at[b, 1]
        )
        act_g[b, 1] = dot(act_h[1], perm_h[...]).astype(BF16)
        return (x_one[...] + dot(act_g[b, 1], weight_out(b))) + wide(b, 2)

    forward_in(0)
    out_unit.first()
    mid_unit.first()
    conv_unit.third()

    for fetch in moment_fetches:
        fetch.wait()
    for unit in UNITS:
        moments[unit][...] = jnp.zeros(moments[unit].shape, BF16)

        def put_moment(low, rows, values, add, unit=unit):
            store(moments[unit], unit, low, (MOMENT_DECAY * values).astype(BF16), rows=rows, add=add)

        lay_out(unit, *shard, put_moment)
        parts[unit][...] = jnp.zeros(parts[unit].shape, BF16)

    out_unit.second()
    mid_unit.second()
    last_unit.first()
    conv_unit.last()
    forward_conv(0)
    out_unit.third()
    mid_unit.third()
    last_unit.second()
    out_unit.last()
    x_one[...] = forward_out(0)
    last_unit.third()
    mid_unit.last()
    forward_in(1)
    forward_conv(1)
    last_unit.last()
    out[...] = forward_out(1).T.astype(BF16)
    results[0].start()
    for unit in (in_unit, conv_unit, out_unit, mid_unit, last_unit):
        unit.finish()
    place.sent()
    gathers_used = place.used

    reduces = [Reduce(place, grads[k], moments[k], rooms[8 * k : 8 * k + 8]) for k in UNITS]
    grouped = (slice(None),)

    def put_grads(unit, low, values, add=False):
        store(grads[unit], unit, low, values.reshape(OWNERS, ROWS, values.shape[-1]), lead=grouped, add=add)

    rows_w, rows_n = [None] * 6, [None] * 12

    def keep_low(rows, dx):
        act_h[0, rows, :] = dx.astype(BF16)

    def backward_weight_out(b):
        rows_w[3 * b + 2] = jnp.sum(wide_grad[...], axis=0, keepdims=True)
        product = dot_tn(act_g[b, 1], wide_grad[...].astype(BF16)).astype(BF16)
        put_grads(OUT_AT[b][0], 0, jnp.concatenate([product, jnp.zeros((GROUPED, 1024 - D), BF16)], axis=1))

    def backward_out(b):
        back = dot_nt(wide_grad[...].astype(BF16), weight_out(b)).astype(BF16)
        spare[:, :H] = dot_nt(back, perm_h[...])
        sums = norm_backward(
            spare, H, narrow(b, 4), unit_h.at[b, 1], slope_h.at[b, 1], spread_h.at[b, 1], keep_low
        )
        rows_n[6 * b + 4], rows_n[6 * b + 5], rows_n[6 * b + 3] = sums

    def backward_conv(b):
        span = CONV_SPAN[b]
        e_all[:, :span] = jnp.zeros((TOK, span), BF16)
        for at, unused, mask in taps(b):
            moved = dot(masks[mask], act_h[0])
            moved = jnp.concatenate([moved, jnp.zeros((TOK, 512 - H), F32)], axis=1)
            if at % 128:
                moved = pltpu.roll(moved, at % 128, 1)
            low = at - at % 128
            e_all[:, low : low + 512] += moved.astype(BF16)
        act_t[...] = act_g[b, 0].T
        for low in range(0, span, 512):
            high = min(low + 512, span)
            put_grads(CONV_AT[b][0], low, dot(act_t[...], e_all[:, low:high]).astype(BF16))

    def backward_hidden(b):
        span = CONV_SPAN[b]
        back = None
        for low in range(0, span, 512):
            high = min(low + 512, span)
            part = dot_nt(e_all[:, low:high], weights(CONV_AT[b][0], low, high))
            back = part if back is None else back + part
        spare[:, :H] = dot_nt(back.astype(BF16), perm_h[...])
        sums = norm_backward(
            spare, H, narrow(b, 1), unit_h.at[b, 0], slope_h.at[b, 0], spread_h.at[b, 0], keep_low
        )
        rows_n[6 * b + 1], rows_n[6 * b + 2], rows_n[6 * b + 0] = sums

    def backward_weight_in(b):
        unit, at = IN_AT[b]
        tall[...] = dot_tn(act_d[b], act_h[0])
        low, high = lane_window(at, 2 * H)
        spare_rows = slice(SHARD, ROWS)
        if at % 128:
            rest = jnp.zeros((OWNERS, ROWS - SHARD, high - low - 128), BF16)
            store(grads[unit], unit, low + 128, rest, lead=grouped, rows=spare_rows)
        else:
            rest = jnp.zeros((OWNERS, ROWS - SHARD, high - low), BF16)
            store(grads[unit], unit, low, rest, lead=grouped, rows=spare_rows)
        for i in range(OWNERS):
            slot = other_owner(own, i)
            first = tall[2 * SHARD * i : 2 * SHARD * i + SHARD, :]
            second = tall[2 * SHARD * i + SHARD : 2 * SHARD * (i + 1), :]
            whole = shifted(first, at, low, high) + shifted(second, at + H, low, high)
            where = dict(lead=(slot,), rows=slice(0, SHARD))
            if at % 128:
                store(grads[unit], unit, low, whole[:, :128], add=True, **where)
                store(grads[unit], unit, low + 128, whole[:, 128:].astype(BF16), **where)
            else:
                store(grads[unit], unit, low, whole.astype(BF16), **where)

    def backward_in(b):
        x_one[...] = dot_nt(act_h[0], w_in[b])

        def add_up(rows, dx):
            wide_grad[rows, :] += dx

        sums = norm_backward(
            x_one, D, wide(b, 0), unit_d.at[b], slope_d.at[b], spread_d.at[b], add_up
        )
        rows_w[3 * b + 0], rows_w[3 * b + 1] = sums[0], sums[1]

    spread_moments = []

    def to_owners(unit):
        reduces[unit].finish()
        for k, owner in enumerate(owners):
            if owner.matrix["unit"] == unit:
                owner.gather(moments[unit], window, own_send, own_recv, k)
        spread_moments.append(Direct(place, moments[unit]))

    backward_weight_out(1)
    reduces[OUT1].core()
    backward_out(1)
    reduces[OUT1].plane()
    backward_conv(1)
    backward_hidden(1)
    reduces[OUT1].turn()
    backward_weight_in(1)
    reduces[MID1].core()
    backward_in(1)
    reduces[OUT1].cross()
    backward_weight_out(0)
    reduces[OUT0].core()
    reduces[MID1].plane()
    backward_out(0)
    backward_conv(0)
    reduces[CONV0].core()
    reduces[OUT0].plane()
    to_owners(OUT1)
    backward_hidden(0)
    reduces[MID1].turn()
    reduces[CONV0].plane()
    backward_weight_in(0)
    reduces[OUT0].turn()
    backward_in(0)
    for m in range(12):
        vec_n[m : m + 1, :] = rows_n[m]
    for m in range(6):
        vec_w[m : m + 1, :] = rows_w[m]
    low_n, low_w = vec_n[...].astype(BF16), vec_w[...].astype(BF16)
    for s in range(OWNERS):
        three = [dot_nt(low_n, put_narrow(s))] + [dot_nt(low_w, put_wide(s, h)) for h in range(2)]
        three.append(jnp.zeros((ROWS - 48, 128), F32))
        store(grads[IN0], IN0, VEC_AT, jnp.concatenate(three, axis=0).astype(BF16), lead=(s,))
    reduces[IN0].core()
    reduces[MID1].cross()
    grad_tokens[...] = wide_grad[...].T
    results[1].start()
    reduces[CONV0].turn()
    reduces[IN0].plane()
    reduces[OUT0].cross()
    to_owners(MID1)
    reduces[IN0].turn()
    reduces[CONV0].cross()
    to_owners(OUT0)
    reduces[IN0].cross()
    to_owners(CONV0)
    to_owners(IN0)
    reduces_used, place.used = place.used, 0
    for gather in spread_moments:
        gather.first()
    for owner in owners:

        @pl.when(owner.here)
        def _(owner=owner):
            owner.gathered(window, own_recv)

    orthogonalize(owners, window, gram, poly, halves)
    for k, owner in enumerate(owners):

        @pl.when(owner.here)
        def _(owner=owner, k=k):
            owner.spread(window, parts[owner.matrix["unit"]], back_send, back_recv, k // 2)

    for gather in spread_moments:
        gather.second()
    spread_updates = []

    def take_updates(unit):
        for k, owner in enumerate(owners):
            if owner.matrix["unit"] == unit:
                owner.arrived(window, parts[unit], back_send, back_recv, k // 2)
        total = parts[unit][0]
        if unit == MID1:
            total = total + parts[unit][1]
        updates[unit][place.y, place.x, place.c] = total
        spread_updates.append(Direct(place, updates[unit]))
        spread_updates[-1].first()

    for unit in (OUT1, OUT0, IN0, MID1, CONV0):
        take_updates(unit)
    for gather in spread_moments:
        gather.last()
    for copy in results[2:7]:
        copy.start()
    for gather in spread_updates:
        gather.second()
    for k, unit in enumerate((OUT1, OUT0, IN0, MID1, CONV0)):
        spread_updates[k].last()
        results[7 + unit].start()
    assert place.used <= gathers_used
    for k, owner in enumerate(owners):
        owner.gather_sent(moments[owner.matrix["unit"]], window, own_send, own_recv, k)
    place.sent()
    for copy in results:
        copy.wait()


def run_step(extra, dilation, lengths, params, tokens, cotangent, moments):
    in_smem = pl.BlockSpec(memory_space=pltpu.SMEM)
    anywhere = pl.BlockSpec(memory_space=pltpu.HBM)

    def dma(n):
        return pltpu.SemaphoreType.DMA((n,))

    def pieces(chunk, lead, dtype=BF16):
        return vmem(lead + (2, 2, 2, ROWS, WIDTH[chunk]), dtype)

    shared = [jax.ShapeDtypeStruct((2, 2, 2, ROWS, w), BF16) for w in WIDTH]
    results = [jax.ShapeDtypeStruct((D, TOK), BF16), jax.ShapeDtypeStruct((D, TOK), F32)] + shared + shared
    count = 9 * len(WIDTH) + (10 + len(extra)) * len(WIDTH)
    scratch = [vmem(a.shape, a.dtype) for a in results]
    scratch += [dma(count), dma(count), dma(2 * len(MATRICES)), dma(1), dma(1), dma(len(MATRICES)), dma(24)]
    scratch += [pieces(k, (OWNERS,)) for k in UNITS] * 2
    scratch += [vmem((2 if k == MID1 else 1, ROWS, w), BF16) for k, w in enumerate(WIDTH)]
    for unit in UNITS:
        scratch += reduce_room(unit, extra)
    scratch += [vmem((OWNERS, ROWS, WINDOW), BF16)]
    scratch += [vmem(a.shape, a.dtype) for a in (tokens, cotangent) + tuple(params)]
    scratch += [
        vmem((TOK, TOK), jnp.int32),
        vmem((H, GROUPED), BF16),
        vmem((16, D), F32),
        vmem((16, H), F32),
        vmem((2, D, H), BF16),
        vmem((TOK, D), F32),
        vmem((TOK, D), F32),
        vmem((D, H), F32),
        vmem((K_ENC + 2 * K_DEC - 1, TOK, TOK), BF16),
        vmem((2, TOK, D), BF16),
        vmem((2, TOK, H), BF16),
        vmem((2, 2, TOK, GROUPED), BF16),
        vmem((GROUPED, TOK), BF16),
        vmem((TOK, 2048), BF16),
        vmem((2, TOK, D), BF16),
        vmem((2, TOK, D), BF16),
        vmem((2, TOK, 128), F32),
        vmem((2, 2, TOK, H), BF16),
        vmem((2, 2, TOK, H), BF16),
        vmem((2, 2, TOK, 128), F32),
        vmem((512, 512), F32),
        vmem((512, 512), BF16),
        vmem((2, GROUPED, 512), BF16),
    ]
    return pl.pallas_call(
        functools.partial(step_kernel, extra),
        out_shape=tuple(results),
        in_specs=[in_smem] * 2 + [anywhere] * 12,
        out_specs=(anywhere,) * 12,
        scratch_shapes=scratch,
        compiler_params=pltpu.CompilerParams(
            collective_id=0, has_side_effects=True, vmem_limit_bytes=62 << 20
        ),
        name="step",
    )(dilation, lengths, tokens, cotangent, *params, *moments)


def finish_kernel(
    vector_step, *refs,
):
    in_hbm, out_to_hbm, ins, outs = refs[:17], refs[17:32], refs[32:49], refs[49:62]
    in_sems, out_sems = refs[62:]
    moments, updates = ins[2:7], ins[7:12]
    conv, w_in, w_out, wide, narrow = ins[12:]
    (
        mom_in, mom_conv, mom_out, mom_wide, mom_narrow,
        new_in, new_conv, new_out, new_wide, new_narrow, low_in, low_conv, low_out,
    ) = outs
    arrivals = [pltpu.make_async_copy(s, t, in_sems.at[k]) for k, (s, t) in enumerate(zip(in_hbm, ins))]
    sources = outs + ins[:2]
    targets = out_to_hbm[2:] + out_to_hbm[:2]
    departures = [pltpu.make_async_copy(s, t, out_sems.at[k]) for k, (s, t) in enumerate(zip(sources, targets))]
    arrivals = arrivals[2:] + arrivals[:2]
    for copy in arrivals:
        copy.start()
    rows = slice(0, SHARD)

    def conv_parts(refs):
        enc = load(refs[CONV0], CONV0, 0, 2048, rows=rows).astype(F32)
        dec = load(refs[MID1], MID1, 0, 1280, rows=rows).astype(F32)
        dec = pltpu.roll(dec, SPLIT % 128, 1)
        middle = jnp.where(iota((SHARD, 128), 1) < SPLIT % 128, enc[:, 1920:], dec[:, :128])
        return ((0, enc[:, :1920]), (1920, middle), (2048, dec[:, 128:]))

    def out_lanes(refs, b):
        return load(refs[OUT_AT[b][0]], OUT_AT[b][0], 0, 896, rows=rows).astype(F32)[:, :D]

    def in_lanes(refs, b, h):
        unit, at = IN_AT[b]
        low, high = lane_window(at + H * h, H)
        return unshifted(load(refs[unit], unit, low, high, rows=rows).astype(F32), at + H * h, H)

    for copy in arrivals[:5]:
        copy.wait()
    for low, values in conv_parts(moments):
        mom_conv[:, low : low + values.shape[1]] = values
    departures[1].start()
    for b in range(2):
        mom_out[:, b, :] = out_lanes(moments, b)
        for h in range(2):
            mom_in[b, h * SHARD : (h + 1) * SHARD, :] = in_lanes(moments, b, h)
    departures[0].start()
    departures[2].start()
    for copy in arrivals[15:]:
        copy.wait()
    for copy in departures[13:]:
        copy.start()
    for copy in arrivals[5:15]:
        copy.wait()
    for low, values in conv_parts(updates):
        lanes = slice(low, low + values.shape[1])
        value = conv[:, lanes] - values
        new_conv[:, lanes] = value
        low_conv[:, lanes] = value.astype(BF16)
    departures[6].start()
    departures[11].start()
    for b in range(2):
        value = w_out[:, b, :] - out_lanes(updates, b)
        new_out[:, b, :] = value
        for h in range(2):
            here = slice(h * SHARD, (h + 1) * SHARD)
            value = w_in[b, here, :] - in_lanes(updates, b, h)
            new_in[b, here, :] = value
            low_in[b, here, :] = value.astype(BF16)
    low_out[...] = new_out[...].astype(BF16)
    for k in (5, 7, 10, 12):
        departures[k].start()
    vectors = load(moments[IN0], IN0, VEC_AT, VEC_AT + 128).astype(F32)
    for b in range(2):
        for k in range(6):
            m = 6 * b + k
            value = vectors[m : m + 1, :SHARD]
            mom_narrow[k, b : b + 1, :] = value
            new_narrow[k, b : b + 1, :] = narrow[k, b : b + 1, :] - vector_step * value
        for k in range(3):
            for h in range(2):
                m = 16 + 16 * h + 3 * b + k
                lanes = slice(h * SHARD, (h + 1) * SHARD)
                value = vectors[m : m + 1, :SHARD]
                mom_wide[k, b : b + 1, lanes] = value
                new_wide[k, b : b + 1, lanes] = wide[k, b : b + 1, lanes] - vector_step * value
    for k in (3, 4, 8, 9):
        departures[k].start()
    for copy in departures:
        copy.wait()


def finish(vector_step, shared, params):
    in_hbm = pl.BlockSpec(memory_space=pltpu.HBM)
    conv, w_in, w_out, wide, narrow = params
    shapes = [w_in.shape, conv.shape, w_out.shape, wide.shape, narrow.shape]
    outs = [jax.ShapeDtypeStruct(a.shape, a.dtype) for a in shared[:2]]
    outs += [jax.ShapeDtypeStruct(s, F32) for s in shapes + shapes]
    outs += [jax.ShapeDtypeStruct(s, BF16) for s in shapes[:3]]
    ins = tuple(shared) + tuple(params)
    return pl.pallas_call(
        functools.partial(finish_kernel, vector_step),
        out_shape=tuple(outs),
        in_specs=[in_hbm] * len(ins),
        out_specs=(in_hbm,) * len(outs),
        scratch_shapes=[vmem(a.shape, a.dtype) for a in ins + tuple(outs[2:])]
        + [pltpu.SemaphoreType.DMA((17,)), pltpu.SemaphoreType.DMA((15,))],
        compiler_params=pltpu.CompilerParams(vmem_limit_bytes=62 << 20),
        name="finish",
    )(*ins)


def swap(array):
    return jnp.transpose(array, (1, 0, 2))


def shards(
    extra, vector_step, tokens, cotangent, lengths, dilation, proj_in, conv_weight, proj_out, vec_wide, vec_narrow,
    mom_in, mom_conv, mom_out, mom_wide, mom_narrow,
):
    params = (conv_weight, proj_in, swap(proj_out), swap(vec_wide), swap(vec_narrow))
    moments = (mom_conv, mom_in, swap(mom_out), swap(mom_wide), swap(mom_narrow))
    shared = run_step(extra, dilation, lengths, params, tokens.T, cotangent.T, moments)
    outs = list(finish(vector_step, shared, params))
    for k in (0, 1):
        outs[k] = outs[k].T
    for k in (4, 5, 6, 9, 10, 11, 14):
        outs[k] = swap(outs[k])
    return tuple(outs)


def solution(mesh):
    groups, owners = mesh.shape["dp"], mesh.shape["fsdp"]
    assert owners == OWNERS and groups % PIECES == 0
    extra, bit = [], PIECES
    while bit < groups:
        extra.append(bit)
        bit *= 2
    assert bit == groups
    vector_step = VECTOR_RATE / math.sqrt(TOK * groups * owners)
    tok, rep = P(("dp", "fsdp"), None), P()
    mid, first, final = P(None, "fsdp", None), P("fsdp", None), P(None, None, "fsdp")
    params = (mid, first, mid, final, final)
    return jax.shard_map(
        functools.partial(shards, tuple(extra), vector_step),
        mesh=mesh,
        in_specs=(tok, tok, tok, rep) + params + params,
        out_specs=(tok, tok) + params + params + (mid, first, mid),
        check_vma=False,
    )
```

```python
import functools
import math

import jax
import jax.numpy as jnp
from jax import lax
from jax.experimental import pallas as pl
from jax.experimental.pallas import tpu as pltpu
from jax.sharding import PartitionSpec as P

D = 800
H = 400
K_ENC = 5
K_DEC = 3
NS_STEPS = 5
EPSILON = 1e-05
NORM_FLOOR = 1e-07
COEF_A = 3.4445
COEF_B = -4.775
COEF_C = 2.0315
MOMENT_DECAY = 0.5
MATRIX_RATE = 0.5
VECTOR_RATE = 0.1

F32 = jnp.float32
BF16 = jnp.bfloat16
MESH = pl.DeviceIdType.MESH

OWNERS = 4
PIECES = 8
SHARD = 100
ROWS = 112
IN0, CONV0, OUT0, MID1, OUT1 = range(5)
WIDTH = (128, 256, 128, 256, 128)
UNITS = range(len(WIDTH))
IN_AT = ((IN0, 0), (MID1, 1200))
OUT_AT = ((OUT0, 0), (OUT1, 0))
CONV_AT = ((CONV0, 0), (MID1, 0))
CONV_SPAN = (2048, 1280)
VEC_AT = 896
SPLIT = K_ENC * H
TOK = 256
GROUPED = OWNERS * ROWS
WINDOW = 2048

GELU_K = math.sqrt(2.0 / math.pi)
GELU_C = 0.044715


def vmem(shape, dtype):
    return pltpu.VMEM(shape, dtype)


def dot(a, b):
    return lax.dot_general(a, b, (((1,), (0,)), ((), ())), preferred_element_type=F32)


def dot_nt(a, b):
    return lax.dot_general(a, b, (((1,), (1,)), ((), ())), preferred_element_type=F32)


def dot_tn(a, b):
    return lax.dot_general(a, b, (((0,), (0,)), ((), ())), preferred_element_type=F32)


def one_hot(mask):
    return jnp.where(mask, 1.0, 0.0).astype(BF16)


def iota(shape, dim):
    return lax.broadcasted_iota(jnp.int32, shape, dim)


def add_low(*parts):
    total = parts[0].astype(F32)
    for part in parts[1:]:
        total = total + part.astype(F32)
    return total.astype(BF16)


def spans(chunk, low, high):
    width = WIDTH[chunk]
    for q in range(low // width, -(-high // width)):
        yield q, max(low - q * width, 0), min(high - q * width, width)


def load(ref, chunk, low, high, lead=(), rows=slice(None)):
    parts = []
    for q, start, stop in spans(chunk, low, high):
        parts.append(ref[lead + (q // 4, q // 2 % 2, q % 2, rows, slice(start, stop))])
    return parts[0] if len(parts) == 1 else jnp.concatenate(parts, axis=-1)


def store(ref, chunk, low, value, lead=(), rows=slice(None), add=False):
    at = 0
    for q, start, stop in spans(chunk, low, low + value.shape[-1]):
        index = lead + (q // 4, q // 2 % 2, q % 2, rows, slice(start, stop))
        part = value[..., at : at + stop - start]
        ref[index] = add_low(ref[index], part) if add else part
        at += stop - start


def shifted(values, at, low, high):
    rows, count = values.shape
    base = at - at % 128
    width = -(-(at % 128 + count) // 128) * 128
    parts = []
    if base > low:
        parts.append(jnp.zeros((rows, base - low), F32))
    if width > count:
        values = jnp.concatenate([values, jnp.zeros((rows, width - count), F32)], axis=1)
    parts.append(pltpu.roll(values, at % 128, 1) if at % 128 else values)
    if high > base + width:
        parts.append(jnp.zeros((rows, high - base - width), F32))
    return parts[0] if len(parts) == 1 else jnp.concatenate(parts, axis=1)


def lane_window(at, count):
    return at - at % 128, -(-(at + count) // 128) * 128


def unshifted(values, at, count):
    if at % 128:
        values = pltpu.roll(values, values.shape[1] - at % 128, 1)
    return values[:, :count]


def lay_out(unit, conv, w_in, w_out, wide, narrow, put):
    rows = slice(0, SHARD)
    for b in range(2):
        if unit == CONV_AT[b][0]:
            low, high = (0, SPLIT) if b == 0 else (SPLIT, SPLIT + K_DEC * H)
            start, stop = lane_window(low, high - low)
            stop = min(stop, 3200)
            values = unshifted(conv[:, start:stop], low, high - low)
            put(0, rows, values, False)
        if unit == OUT_AT[b][0]:
            put(0, rows, w_out[:, b, :], False)
        if unit == IN_AT[b][0]:
            at = IN_AT[b][1]
            low, high = lane_window(at, 2 * H)
            values = shifted(w_in[b, :SHARD, :], at, low, high) + shifted(w_in[b, SHARD:, :], at + H, low, high)
            put(low, rows, values, True)
    if unit == IN0:
        for b in range(2):
            for k in range(6):
                m = 6 * b + k
                put(VEC_AT, slice(m, m + 1), narrow[k, b : b + 1, :], False)
            for k in range(3):
                for h in range(2):
                    m = 16 + 16 * h + 3 * b + k
                    put(VEC_AT, slice(m, m + 1), wide[k, b : b + 1, h * SHARD : (h + 1) * SHARD], False)


def flip(value, bit):
    return value + bit - 2 * bit * ((value // bit) % 2)


def other_owner(own, step):
    if step == 0:
        return own
    if step == 3:
        return 3 - own
    return flip(own, step)


def remote(src, dst, send, recv, device):
    return pltpu.make_async_remote_copy(
        src_ref=src,
        dst_ref=dst,
        send_sem=send,
        recv_sem=recv,
        device_id=device,
        device_id_type=MESH,
    )


class Place:
    def __init__(self, send, recv, extra):
        at = lax.axis_index("dp")
        self.piece = at % PIECES
        self.base = at - self.piece
        self.me = at
        self.own = lax.axis_index("fsdp")
        self.y, self.x, self.c = self.piece // 4, self.piece // 2 % 2, self.piece % 2
        self.core, self.near_x, self.near_y = [
            (self.base + flip(self.piece, bit), self.own) for bit in (1, 2, 4)
        ]
        self.near_xy = (self.base + flip(flip(self.piece, 2), 4), self.own)
        self.column = [(at, other_owner(self.own, step)) for step in (1, 2, 3)]
        self.far = [(flip(at, bit), self.own) for bit in extra]
        self.send, self.recv, self.used = send, recv, 0
        self.started = []

    def take(self, count):
        first = self.used
        self.used += count
        return first

    def start(self, src, dst, device):
        k = self.take(1)
        copy = remote(src, dst, self.send.at[k], self.recv.at[k], device)
        copy.start()
        self.started.append(copy)
        return copy

    def sent(self):
        for copy in self.started:
            copy.wait_send()
        self.started = []


class Direct:
    ALL = slice(None)

    def __init__(self, place, ref):
        self.place, self.ref = place, ref

    def first(self):
        p = self.place
        mine = self.ref.at[p.y, p.x, p.c]
        self.copies = [p.start(mine, mine, device) for device in (p.near_x, p.near_y, p.near_xy)]

    def second(self):
        p = self.place
        for copy in self.copies:
            copy.wait_recv()
        pieces = self.ref.at[self.ALL, self.ALL, p.c]
        self.copies = [p.start(pieces, pieces, p.core)]

    def last(self):
        self.copies[0].wait_recv()


class Gather:
    LOW, HIGH, ALL = pl.ds(0, 64), pl.ds(64, 48), slice(None)

    def __init__(self, place, view):
        self.place, self.view = place, view

    def move(self, device, *index):
        ref = self.view(*index)
        return self.place.start(ref, ref, device)

    def first(self):
        p = self.place
        self.a = self.move(p.near_y, p.y, p.x, p.c, self.LOW)
        self.b = self.move(p.near_x, p.y, p.x, p.c, self.HIGH)

    def second(self):
        p = self.place
        self.a.wait_recv()
        self.a = self.move(p.near_x, self.ALL, p.x, p.c, self.LOW)
        self.b.wait_recv()
        self.b = self.move(p.near_y, p.y, self.ALL, p.c, self.HIGH)

    def third(self):
        p = self.place
        self.a.wait_recv()
        self.b.wait_recv()
        self.a = self.move(p.core, self.ALL, self.ALL, p.c, self.ALL)

    def last(self):
        self.a.wait_recv()


class WeightGather(Gather):
    def __init__(self, place, ref, low, width):
        lanes = pl.ds(low, width)

        def view(y, x, c, rows):
            return ref.at[pl.ds(1, 3), y, x, c, rows, lanes]

        super().__init__(place, view)
        self.ref, self.lanes = ref, lanes

    def cross(self):
        p = self.place
        index = (p.y, p.x, p.c, self.ALL, self.lanes)
        mine = self.ref.at[(0,) + index]
        self.crossing = [
            p.start(mine, self.ref.at[(step,) + index], p.column[step - 1]) for step in (1, 2, 3)
        ]

    def first(self, follower=None):
        for copy in self.crossing:
            copy.wait_recv()
        if follower is not None:
            follower.cross()
        super().first()


class Reduce:
    def __init__(self, place, grads, moment, room):
        self.place, self.grads, self.moment = place, grads, moment
        self.from_core, self.sums, self.from_x, self.from_y = room[:4]
        self.last_x, self.last_y, self.from_z, self.from_far = room[4:]

    def core(self):
        p = self.place
        self.halves = []
        for y in (1 - p.y, p.y):
            src = self.grads.at[:, y, :, 1 - p.c]
            self.halves.append((y, p.start(src, self.from_core.at[:, y], p.core)))

    def plane(self):
        p = self.place
        self.a = []
        for k, (y, copy) in enumerate(self.halves):
            copy.wait_recv()
            self.sums[:, y] = add_low(self.grads[:, y, :, p.c], self.from_core[:, y])
            self.a.append(
                p.start(self.sums.at[0:2, y, 1 - p.x], self.from_x.at[:, y], p.near_x)
            )
            if k == 0:
                self.b = p.start(self.sums.at[2:4, y], self.from_y, p.near_y)

    def turn(self):
        p = self.place
        y, x = 1 - p.y, 1 - p.x
        self.a[0].wait_recv()
        self.sums[0:2, y, p.x] = add_low(self.sums[0:2, y, p.x], self.from_x[:, y])
        self.y_last = p.start(self.sums.at[0:2, y, p.x], self.last_y, p.near_y)
        self.b.wait_recv()
        self.sums[2:4, p.y, x] = add_low(self.sums[2:4, p.y, x], self.from_y[:, x])
        self.x_last = p.start(self.sums.at[2:4, p.y, x], self.last_x, p.near_x)

    def cross(self):
        p = self.place
        y, x = p.y, p.x
        self.a[1].wait_recv()
        self.y_last.wait_recv()
        self.sums[0:2, y, x] = add_low(self.sums[0:2, y, x], self.from_x[:, y], self.last_y[...])
        self.x_last.wait_recv()
        self.sums[2:4, y, x] = add_low(self.sums[2:4, y, x], self.from_y[:, x], self.last_x[...])
        for k, device in enumerate(p.far):
            p.start(self.sums.at[:, y, x], self.from_far.at[k], device).wait_recv()
            p.started.pop().wait_send()
            self.sums[:, y, x] = add_low(self.sums[:, y, x], self.from_far[k])
        self.crossing = [
            p.start(self.sums.at[step, y, x], self.from_z.at[step - 1], p.column[step - 1])
            for step in (1, 2, 3)
        ]

    def finish(self):
        p = self.place
        for copy in self.crossing:
            copy.wait_recv()
        parts = [self.sums[0, p.y, p.x]] + [self.from_z[k] for k in range(3)]
        self.moment[p.y, p.x, p.c] = add_low(self.moment[p.y, p.x, p.c], *parts)


def reduce_room(chunk, extra):
    width = WIDTH[chunk]
    shapes = (
        (OWNERS, 2, 2), (OWNERS, 2, 2), (2, 2), (2, 2), (2,), (2,), (3,), (max(len(extra), 1), OWNERS),
    )
    return [vmem(shape + (ROWS, width), BF16) for shape in shapes]


MATRICES = (
    dict(
        kind="row", unit=OUT1, first=0, last=6, piece=5, lanes=(0, D), slot=0, scale=math.sqrt(D / H),
        owners=((0, 0, 2), (3, 2, 2)),
    ),
    dict(
        kind="row", unit=MID1, first=0, last=4, piece=2, lanes=(0, K_DEC * H), slot=0, scale=1.0,
        owners=((0, 0, 2), (3, 2, 2)),
    ),
    dict(
        kind="in", unit=MID1, first=4, last=7, piece=4, lanes=(176, 976), slot=1, scale=1.0,
        owners=((0, 0, 2), (3, 2, 2)),
    ),
    dict(
        kind="row", unit=OUT0, first=0, last=6, piece=3, lanes=(0, D), slot=0, scale=math.sqrt(D / H),
        owners=((1, 0, 2), (2, 2, 2)),
    ),
    dict(
        kind="row", unit=CONV0, first=0, last=7, piece=0, lanes=(0, SPLIT), slot=0, scale=1.0,
        owners=((1, 0, 2), (2, 2, 2)),
    ),
    dict(
        kind="in", unit=IN0, first=0, last=6, piece=6, lanes=(0, D), slot=0, scale=1.0,
        owners=((1, 0, 2), (2, 2, 2)),
    ),
)


class Owner:
    def __init__(self, place, k, owner):
        self.place, self.k = place, k
        matrix = self.matrix = MATRICES[k]
        at, self.first, self.shards = owner
        self.at = at
        self.width = WIDTH[matrix["unit"]]
        self.count = OWNERS * (matrix["last"] - matrix["first"] + 1)
        p = place
        self.here = (p.piece == matrix["piece"]) & (p.own == at)
        self.away = (p.piece != matrix["piece"]) | (p.own != at)
        self.holds = (p.piece >= matrix["first"]) & (p.piece <= matrix["last"])
        self.served = (p.own >= self.first) & (p.own < self.first + self.shards)
        self.device = (p.base + matrix["piece"], at)
    def each_served(self, act):
        def body(k, carry):
            piece = self.matrix["first"] + k // self.shards
            own = self.first + k % self.shards

            @pl.when((piece != self.matrix["piece"]) | (own != self.at))
            def _():
                act(k // self.shards, own, (self.place.base + piece, own))

            return carry

        lax.fori_loop(0, self.count // OWNERS * self.shards, body, 0)

    def lanes(self, k):
        return pl.ds(pl.multiple_of(k * self.width, 128), self.width)

    def to_owner(self, moment, window, send, recv, k):
        p = self.place
        at = p.piece - self.matrix["first"]
        src = moment.at[p.y, p.x, p.c]
        dst = window.at[p.own, :, self.lanes(at)]
        return remote(src, dst, send.at[k], recv.at[0], self.device)

    def gather(self, moment, window, send, recv, k):
        @pl.when(self.holds & self.away)
        def _():
            self.to_owner(moment, window, send, recv, k).start()

        @pl.when(self.here)
        def _():
            p = self.place
            at = p.piece - self.matrix["first"]
            pltpu.make_async_copy(
                moment.at[p.y, p.x, p.c], window.at[p.own, :, self.lanes(at)], recv.at[0]
            ).start()

    def gather_sent(self, moment, window, send, recv, k):
        @pl.when(self.holds & self.away)
        def _():
            self.to_owner(moment, window, send, recv, k).wait_send()

    def whole(self, window, slots, sem):
        values = window.at[slots, :, pl.ds(0, self.count // OWNERS * self.width)]
        return pltpu.make_async_copy(values, values, sem.at[0])

    def gathered(self, window, recv):
        self.whole(window, pl.ds(0, OWNERS), recv).wait()

    def spread(self, window, parts, send, recv, k):
        p = self.place
        slot = parts.at[self.matrix["slot"]]

        def act(at, own, device):
            remote(window.at[own, :, self.lanes(at)], slot, send.at[0], recv.at[k], device).start()

        self.each_served(act)
        if self.first <= self.at < self.first + self.shards:
            at = p.piece - self.matrix["first"]
            pltpu.make_async_copy(window.at[p.own, :, self.lanes(at)], slot, send.at[0]).start()

    def arrived(self, window, parts, send, recv, k):
        @pl.when(self.here)
        def _():
            self.whole(window, pl.ds(self.first, self.shards), send).wait()

        @pl.when(self.holds & self.served & self.away)
        def _():
            src = window.at[0, :, self.lanes(0)]
            dst = parts.at[self.matrix["slot"]]
            remote(src, dst, send.at[0], recv.at[k], self.device).wait_recv()


def split(a):
    high = a.astype(BF16)
    return high, (a - high.astype(F32)).astype(BF16)


def dot_fine(a, b):
    a_high, a_low = split(a)
    b_high, b_low = split(b)
    return dot(a_high, b_high) + (dot(a_high, b_low) + dot(a_low, b_high))


def dot_low(a, b):
    return dot(a.astype(BF16), b.astype(BF16))


def polynomial_of(gram):
    size = gram.shape[0]
    eye = iota((size, size), 0) == iota((size, size), 1)
    unit = jnp.where(eye, 1.0, 0.0)
    power = jnp.sum(jnp.sum(jnp.where(eye, gram, 0.0), axis=1, keepdims=True), axis=0, keepdims=True)
    inverse = 1.0 / (jnp.sqrt(power) + NORM_FLOOR)
    current = gram * inverse * inverse
    result = None
    for step in range(NS_STEPS):
        square = dot_fine if step > 2 else dot_low
        poly = COEF_A * unit + COEF_B * current + COEF_C * square(current, current)
        result = poly if result is None else dot_low(poly, result)
        if step < NS_STEPS - 1:
            first = dot_fine if step < 2 else dot_low
            second = dot_fine if step < 1 else dot_low
            current = second(first(poly, current), poly)
    return result, inverse


def orthogonalize(owners, window, gram, poly, halves):
    is_row = False
    high, factor, parts = jnp.int32(0), jnp.float32(0), jnp.int32(0)
    low_half, high_half = jnp.int32(0), jnp.int32(0)
    for owner in owners:
        matrix, here = owner.matrix, owner.here
        if matrix["kind"] == "row":
            is_row = is_row | here
        high = jnp.where(here, matrix["lanes"][1], high)
        parts = jnp.where(here, -(-matrix["lanes"][1] // 512), parts)
        factor = jnp.where(here, MATRIX_RATE * matrix["scale"], factor)
        low_half = jnp.where(here, owner.first // 2, low_half)
        high_half = jnp.where(here, (owner.first + owner.shards) // 2, high_half)
    ins = {}
    for owner in owners:
        if owner.matrix["kind"] == "in":
            at = owner.matrix["lanes"][0]
            ins[at] = ins.get(at, False) | owner.here
    is_in = False
    for here in ins.values():
        is_in = is_in | here

    def part(k):
        lanes = pl.ds(pl.multiple_of(k * 512, 512), 512)
        values = window[:, :, lanes].reshape(GROUPED, 512)
        lane = iota((GROUPED, 512), 1) + k * 512
        return lanes, jnp.where(lane < high, values, jnp.zeros((), BF16))

    for at, here in ins.items():

        @pl.when(here)
        def _(at=at):
            valid = iota((GROUPED, 512), 1) < H
            for h in range(2):
                low = (at + H * h) // 128 * 128
                values = window[:, :, low : low + 512].reshape(GROUPED, 512).astype(F32)
                if (at + H * h) % 128:
                    values = pltpu.roll(values, 512 - (at + H * h) % 128, 1)
                halves[h] = jnp.where(valid, values, 0.0).astype(BF16)

    @pl.when(is_in)
    def _():
        gram[...] = dot_tn(halves[0], halves[0]) + dot_tn(halves[1], halves[1])

    @pl.when(is_row)
    def _():
        gram[...] = jnp.zeros(gram.shape, F32)

        def body(k, carry):
            values = part(k)[1]
            gram[:GROUPED, :GROUPED] += dot_nt(values, values)
            return carry

        lax.fori_loop(0, parts, body, 0)

    @pl.when(is_in | is_row)
    def _():
        result, inverse = polynomial_of(gram[...])
        poly[...] = (result * (inverse * factor)).astype(BF16)

    for at, here in ins.items():

        @pl.when(here)
        def _(at=at):
            window[:, :, :1024] = jnp.zeros((OWNERS, ROWS, 1024), BF16)

            def body(two_at, carry):
                two, served = pl.ds(2 * two_at, 2), pl.ds(pl.multiple_of(2 * ROWS * two_at, 2 * ROWS), 2 * ROWS)
                for h in range(2):
                    low = (at + H * h) // 128 * 128
                    step = dot_nt(halves[h, served], poly[...])
                    if (at + H * h) % 128:
                        step = pltpu.roll(step, (at + H * h) % 128, 1)
                    lanes = slice(low, low + 512)
                    window[two, :, lanes] = add_low(window[two, :, lanes], step.reshape(2, ROWS, 512))
                return carry

            lax.fori_loop(low_half, high_half, body, 0)

    @pl.when(is_row)
    def _():
        def body(k, carry):
            lanes, values = part(k)

            def half(two_at, carry):
                two, served = pl.ds(2 * two_at, 2), pl.ds(pl.multiple_of(2 * ROWS * two_at, 2 * ROWS), 2 * ROWS)
                step = dot(poly[served, :GROUPED], values)
                window[two, :, lanes] = step.astype(BF16).reshape(2, ROWS, 512)
                return carry

            lax.fori_loop(low_half, high_half, half, 0)
            return carry

        lax.fori_loop(0, parts, body, 0)


def norm_forward(src, width, gain, shift, act, unit, slope, spread, chunk=128):
    def body(k, carry):
        rows = pl.ds(pl.multiple_of(k * chunk, chunk), chunk)
        x = src[rows, :width].astype(F32)
        center = x - jnp.mean(x, axis=1, keepdims=True)
        scale = lax.rsqrt(jnp.mean(center * center, axis=1, keepdims=True) + EPSILON)
        xhat = center * scale
        a = xhat * gain + shift
        square = a * a
        half = 0.5 + 0.5 * jnp.tanh(a * (GELU_K + (GELU_K * GELU_C) * square))
        act[rows, :width] = (a * half).astype(BF16)
        unit[rows, :width] = xhat.astype(BF16)
        inner = GELU_K + (3.0 * GELU_K * GELU_C) * square
        slope[rows, :width] = (half + (2.0 * a * inner) * (half * (1.0 - half))).astype(BF16)
        spread[rows, :] = jnp.broadcast_to(scale, (chunk, 128))
        return carry

    lax.fori_loop(0, TOK // chunk, body, 0)


def fold_rows(values):
    total = values[0:8]
    for k in range(1, values.shape[0] // 8):
        total = total + values[8 * k : 8 * k + 8]
    return total


def norm_backward(grad, width, gain, unit, slope, spread, finish, chunk=128):
    def body(k, sums):
        rows = pl.ds(pl.multiple_of(k * chunk, chunk), chunk)
        da = grad[rows, :width] * slope[rows, :width].astype(F32)
        xhat = unit[rows, :width].astype(F32)
        product = da * xhat
        dxhat = da * gain
        mean_one = jnp.mean(dxhat, axis=1, keepdims=True)
        mean_two = jnp.mean(dxhat * xhat, axis=1, keepdims=True)
        dx = spread[rows, 0:1] * (dxhat - mean_one - xhat * mean_two)
        finish(rows, dx)
        return (sums[0] + fold_rows(product), sums[1] + fold_rows(da), sums[2] + fold_rows(dx))

    zero = jnp.zeros((8, width), F32)
    sums = lax.fori_loop(0, TOK // chunk, body, (zero, zero, zero))
    return tuple(jnp.sum(s, axis=0, keepdims=True) for s in sums)


def step_kernel(
    extra,
    dilation, lengths, tokens_hbm, cotangent_hbm,
    conv_hbm, in_hbm, out_hbm, wide_hbm, narrow_hbm,
    mom_conv_hbm, mom_in_hbm, mom_out_hbm, mom_wide_hbm, mom_narrow_hbm,
    *refs,
):
    results = refs[:12]
    refs = refs[12:]
    out, grad_tokens, moments, updates = refs[0], refs[1], refs[2:7], refs[7:12]
    refs = refs[2:]
    send, recv, own_send, own_recv, back_send, back_recv, local = refs[10:17]
    full, grads, parts = refs[17:22], refs[22:27], refs[27:32]
    rooms = refs[32:72]
    (
        window,
        tokens, cotangent, conv, in_shard, out_shard, wide_shard, narrow_shard,
        far, perm_h, vec_w, vec_n, w_in, x_one, wide_grad, tall,
        masks, act_d, act_h, act_g, act_t, e_all,
        unit_d, slope_d, spread_d, unit_h, slope_h, spread_h,
        gram, poly, halves,
    ) = refs[72:]
    place = Place(send, recv, extra)
    own = place.own
    owners = [Owner(place, k, owner) for k, matrix in enumerate(MATRICES) for owner in matrix["owners"]]
    conv_in, spare = gram.at[:TOK], gram.at[TOK:]
    hid = spare

    results = [
        pltpu.make_async_copy(source, target, local.at[12 + k])
        for k, (source, target) in enumerate(zip((out, grad_tokens) + moments + updates, results))
    ]

    sources = (conv_hbm, in_hbm, out_hbm, wide_hbm, narrow_hbm, tokens_hbm, cotangent_hbm)
    shard = (conv, in_shard, out_shard, wide_shard, narrow_shard)
    targets = shard + (tokens, cotangent)
    fetches = [pltpu.make_async_copy(s, t, local.at[k]) for k, (s, t) in enumerate(zip(sources, targets))]
    for fetch in fetches:
        fetch.start()
    barrier = pltpu.get_barrier_semaphore()
    for device in [place.core, place.near_x, place.near_y] + place.column + place.far:
        pl.semaphore_signal(barrier, inc=1, device_id=device, device_id_type=MESH)

    def pack(unit):
        full[unit][0] = jnp.zeros(full[unit].shape[1:], BF16)

        def put(low, rows, values, add):
            store(full[unit], unit, low, values.astype(BF16), lead=(0,), rows=rows, add=add)

        lay_out(unit, *shard, put)

    in_unit = WeightGather(place, full[IN0], 0, 128)
    conv_unit = WeightGather(place, full[CONV0], 0, 256)
    out_unit = WeightGather(place, full[OUT0], 0, 128)
    mid_unit = WeightGather(place, full[MID1], 0, 256)
    last_unit = WeightGather(place, full[OUT1], 0, 128)

    for k in (1, 3, 4):
        fetches[k].wait()
    pack(IN0)
    pl.semaphore_wait(barrier, 6 + len(extra))
    in_unit.cross()
    fetches[0].wait()
    pack(CONV0)
    conv_unit.cross()
    fetches[2].wait()
    for unit in (OUT0, MID1, OUT1):
        pack(unit)
    sources = (mom_conv_hbm, mom_in_hbm, mom_out_hbm, mom_wide_hbm, mom_narrow_hbm)
    moment_fetches = [pltpu.make_async_copy(s, t, local.at[7 + k]) for k, (s, t) in enumerate(zip(sources, shard))]
    for fetch in moment_fetches:
        fetch.start()

    row, col = iota((TOK, TOK), 0), iota((TOK, TOK), 1)
    seg_row, seg_col = jnp.zeros((TOK, TOK), jnp.int32), jnp.zeros((TOK, TOK), jnp.int32)
    end = jnp.int32(0)
    for k in range(8):
        end = end + lengths[0, k]
        seg_row = seg_row + jnp.where(row >= end, 1, 0)
        seg_col = seg_col + jnp.where(col >= end, 1, 0)
    far[...] = jnp.where(seg_row == seg_col, col - row, 4 * TOK)

    enc_shifts = [(j - K_ENC // 2) * dilation[0] for j in range(K_ENC)]
    dec_shifts = [j * dilation[1] for j in range(1 - K_DEC, K_DEC)]
    for k, shift in enumerate(enc_shifts + dec_shifts):
        masks[k] = one_hot(far[...] == shift)
    tap_masks = (
        [(j, K_ENC - 1 - j) for j in range(K_ENC)],
        [(K_ENC + K_DEC - 1 - j, K_ENC + K_DEC - 1 + j) for j in range(K_DEC)],
    )

    in_unit.first(out_unit)
    conv_unit.first(mid_unit)
    row, col = iota((H, GROUPED), 0), iota((H, GROUPED), 1)
    used = jnp.zeros((H, GROUPED), jnp.int32)
    for s in range(OWNERS):
        r = col - ROWS * s
        inside = (r >= 0) & (r < SHARD) & (row == r + SHARD * other_owner(own, s))
        used = used + jnp.where(inside, 1, 0)
    perm_h[...] = used.astype(F32).astype(BF16)
    in_unit.second()
    out_unit.first(last_unit)
    fetches[5].wait()
    x_one[...] = tokens[...].astype(F32).T
    conv_unit.second()
    in_unit.third()
    fetches[6].wait()
    wide_grad[...] = cotangent[...].astype(F32).T
    mid_unit.first()
    out_unit.second()
    conv_unit.third()
    in_unit.last()

    row_n, col_n = iota((128, H), 0), iota((128, H), 1)
    row_w, col_w = iota((128, D), 0), iota((128, D), 1)

    def put_narrow(s):
        return one_hot((col_n == row_n + SHARD * other_owner(own, s)) & (row_n < SHARD))

    def put_wide(s, h):
        return one_hot((col_w == row_w + SHARD * (2 * other_owner(own, s) + h)) & (row_w < SHARD))

    total_n, total_w = jnp.zeros((16, H), F32), jnp.zeros((16, D), F32)
    for s in range(OWNERS):
        vectors = load(full[IN0], IN0, VEC_AT, VEC_AT + 128, lead=(s,))
        total_n = total_n + dot(vectors[0:16], put_narrow(s))
        for h in range(2):
            total_w = total_w + dot(vectors[16 + 16 * h : 32 + 16 * h], put_wide(s, h))
    vec_n[...] = total_n
    vec_w[...] = total_w

    def narrow(b, k):
        return vec_n[6 * b + k : 6 * b + k + 1, :]

    def wide(b, k):
        return vec_w[3 * b + k : 3 * b + k + 1, :]

    def weights(unit, low, high):
        return load(full[unit], unit, low, high, lead=(slice(None),)).reshape(GROUPED, high - low)

    def weight_out(b):
        return weights(OUT_AT[b][0], 0, 896)[:, :D]

    def place_in(b):
        unit, at = IN_AT[b]
        for i in range(OWNERS):
            slot = other_owner(own, i)
            for h in range(2):
                low, high = lane_window(at + H * h, H)
                values = load(full[unit], unit, low, high, lead=(slot,)).astype(F32)[:SHARD]
                row_at = SHARD * (2 * i + h)
                tall[row_at : row_at + SHARD, :] = unshifted(values, at + H * h, H)
        w_in[b] = tall[...].astype(BF16)

    def taps(b):
        return [(H * j, forward, backward) for j, (forward, backward) in enumerate(tap_masks[b])]

    def forward_in(b):
        norm_forward(x_one, D, wide(b, 0), wide(b, 1), act_d.at[b], unit_d.at[b], slope_d.at[b], spread_d.at[b])
        place_in(b)
        hid[:, :H] = dot(act_d[b], w_in[b]) + narrow(b, 0)
        norm_forward(
            hid, H, narrow(b, 1), narrow(b, 2), act_h.at[0], unit_h.at[b, 0], slope_h.at[b, 0], spread_h.at[b, 0]
        )
        act_g[b, 0] = dot(act_h[0], perm_h[...]).astype(BF16)

    def forward_conv(b):
        for j, (at, mask, unused) in enumerate(taps(b)):
            moved = dot(masks[mask], act_g[b, 0]).astype(BF16)
            low = at - at % 128
            product = dot(moved, weights(CONV_AT[b][0], low, low + 512))
            if at % 128:
                product = pltpu.roll(product, 512 - at % 128, 1)
            if j == 0:
                conv_in[...] = product
            else:
                conv_in[...] += product
        conv_in[:, :H] += narrow(b, 3)

    def forward_out(b):
        norm_forward(
            conv_in, H, narrow(b, 4), narrow(b, 5), act_h.at[1], unit_h.at[b, 1], slope_h.at[b, 1], spread_h.at[b, 1]
        )
        act_g[b, 1] = dot(act_h[1], perm_h[...]).astype(BF16)
        return (x_one[...] + dot(act_g[b, 1], weight_out(b))) + wide(b, 2)

    forward_in(0)
    last_unit.first()
    mid_unit.second()
    out_unit.third()
    conv_unit.last()
    forward_conv(0)
    last_unit.second()
    mid_unit.third()
    out_unit.last()
    x_one[...] = forward_out(0)
    last_unit.third()

    for fetch in moment_fetches:
        fetch.wait()
    for unit in UNITS:
        moments[unit][...] = jnp.zeros(moments[unit].shape, BF16)

        def put_moment(low, rows, values, add, unit=unit):
            store(moments[unit], unit, low, (MOMENT_DECAY * values).astype(BF16), rows=rows, add=add)

        lay_out(unit, *shard, put_moment)
        parts[unit][...] = jnp.zeros(parts[unit].shape, BF16)

    mid_unit.last()
    forward_in(1)
    forward_conv(1)
    last_unit.last()
    out[...] = forward_out(1).T.astype(BF16)
    results[0].start()
    place.sent()
    gathers_used = place.used

    reduces = [Reduce(place, grads[k], moments[k], rooms[8 * k : 8 * k + 8]) for k in UNITS]
    grouped = (slice(None),)

    def put_grads(unit, low, values, add=False):
        store(grads[unit], unit, low, values.reshape(OWNERS, ROWS, values.shape[-1]), lead=grouped, add=add)

    rows_w, rows_n = [None] * 6, [None] * 12

    def keep_low(rows, dx):
        act_h[0, rows, :] = dx.astype(BF16)

    def backward_weight_out(b):
        rows_w[3 * b + 2] = jnp.sum(wide_grad[...], axis=0, keepdims=True)
        product = dot_tn(act_g[b, 1], wide_grad[...].astype(BF16)).astype(BF16)
        put_grads(OUT_AT[b][0], 0, jnp.concatenate([product, jnp.zeros((GROUPED, 1024 - D), BF16)], axis=1))

    def backward_out(b):
        back = dot_nt(wide_grad[...].astype(BF16), weight_out(b)).astype(BF16)
        spare[:, :H] = dot_nt(back, perm_h[...])
        sums = norm_backward(
            spare, H, narrow(b, 4), unit_h.at[b, 1], slope_h.at[b, 1], spread_h.at[b, 1], keep_low
        )
        rows_n[6 * b + 4], rows_n[6 * b + 5], rows_n[6 * b + 3] = sums

    def backward_conv(b):
        span = CONV_SPAN[b]
        e_all[:, :span] = jnp.zeros((TOK, span), BF16)
        for at, unused, mask in taps(b):
            moved = dot(masks[mask], act_h[0])
            moved = jnp.concatenate([moved, jnp.zeros((TOK, 512 - H), F32)], axis=1)
            if at % 128:
                moved = pltpu.roll(moved, at % 128, 1)
            low = at - at % 128
            e_all[:, low : low + 512] += moved.astype(BF16)
        act_t[...] = act_g[b, 0].T
        for low in range(0, span, 512):
            high = min(low + 512, span)
            put_grads(CONV_AT[b][0], low, dot(act_t[...], e_all[:, low:high]).astype(BF16))

    def backward_hidden(b):
        span = CONV_SPAN[b]
        back = None
        for low in range(0, span, 512):
            high = min(low + 512, span)
            part = dot_nt(e_all[:, low:high], weights(CONV_AT[b][0], low, high))
            back = part if back is None else back + part
        spare[:, :H] = dot_nt(back.astype(BF16), perm_h[...])
        sums = norm_backward(
            spare, H, narrow(b, 1), unit_h.at[b, 0], slope_h.at[b, 0], spread_h.at[b, 0], keep_low
        )
        rows_n[6 * b + 1], rows_n[6 * b + 2], rows_n[6 * b + 0] = sums

    def backward_weight_in(b):
        unit, at = IN_AT[b]
        tall[...] = dot_tn(act_d[b], act_h[0])
        low, high = lane_window(at, 2 * H)
        spare_rows = slice(SHARD, ROWS)
        if at % 128:
            rest = jnp.zeros((OWNERS, ROWS - SHARD, high - low - 128), BF16)
            store(grads[unit], unit, low + 128, rest, lead=grouped, rows=spare_rows)
        else:
            rest = jnp.zeros((OWNERS, ROWS - SHARD, high - low), BF16)
            store(grads[unit], unit, low, rest, lead=grouped, rows=spare_rows)
        for i in range(OWNERS):
            slot = other_owner(own, i)
            first = tall[2 * SHARD * i : 2 * SHARD * i + SHARD, :]
            second = tall[2 * SHARD * i + SHARD : 2 * SHARD * (i + 1), :]
            whole = shifted(first, at, low, high) + shifted(second, at + H, low, high)
            where = dict(lead=(slot,), rows=slice(0, SHARD))
            if at % 128:
                store(grads[unit], unit, low, whole[:, :128], add=True, **where)
                store(grads[unit], unit, low + 128, whole[:, 128:].astype(BF16), **where)
            else:
                store(grads[unit], unit, low, whole.astype(BF16), **where)

    def backward_in(b):
        x_one[...] = dot_nt(act_h[0], w_in[b])

        def add_up(rows, dx):
            wide_grad[rows, :] += dx

        sums = norm_backward(
            x_one, D, wide(b, 0), unit_d.at[b], slope_d.at[b], spread_d.at[b], add_up
        )
        rows_w[3 * b + 0], rows_w[3 * b + 1] = sums[0], sums[1]

    spread_moments = []

    def to_owners(unit):
        reduces[unit].finish()
        for k, owner in enumerate(owners):
            if owner.matrix["unit"] == unit:
                owner.gather(moments[unit], window, own_send, own_recv, k)
        spread_moments.append(Direct(place, moments[unit]))

    backward_weight_out(1)
    reduces[OUT1].core()
    backward_out(1)
    reduces[OUT1].plane()
    backward_conv(1)
    backward_hidden(1)
    reduces[OUT1].turn()
    backward_weight_in(1)
    reduces[MID1].core()
    backward_in(1)
    reduces[OUT1].cross()
    backward_weight_out(0)
    reduces[OUT0].core()
    reduces[MID1].plane()
    backward_out(0)
    backward_conv(0)
    reduces[CONV0].core()
    to_owners(OUT1)
    backward_hidden(0)
    reduces[MID1].turn()
    reduces[CONV0].plane()
    backward_weight_in(0)
    backward_in(0)
    reduces[OUT0].plane()
    for m in range(12):
        vec_n[m : m + 1, :] = rows_n[m]
    for m in range(6):
        vec_w[m : m + 1, :] = rows_w[m]
    low_n, low_w = vec_n[...].astype(BF16), vec_w[...].astype(BF16)
    for s in range(OWNERS):
        three = [dot_nt(low_n, put_narrow(s))] + [dot_nt(low_w, put_wide(s, h)) for h in range(2)]
        three.append(jnp.zeros((ROWS - 48, 128), F32))
        store(grads[IN0], IN0, VEC_AT, jnp.concatenate(three, axis=0).astype(BF16), lead=(s,))
    reduces[IN0].core()
    reduces[MID1].cross()
    reduces[CONV0].turn()
    reduces[IN0].plane()
    grad_tokens[...] = wide_grad[...].T
    results[1].start()
    to_owners(MID1)
    reduces[CONV0].cross()
    reduces[OUT0].turn()
    reduces[IN0].turn()
    to_owners(CONV0)
    reduces[OUT0].cross()
    reduces[IN0].cross()
    to_owners(OUT0)
    to_owners(IN0)
    for k, owner in enumerate(owners):
        owner.gather_sent(moments[owner.matrix["unit"]], window, own_send, own_recv, k)
    reduces_used, place.used = place.used, 0
    for gather in spread_moments:
        gather.first()
    for owner in owners:

        @pl.when(owner.here)
        def _(owner=owner):
            owner.gathered(window, own_recv)

    orthogonalize(owners, window, gram, poly, halves)
    for k, owner in enumerate(owners):

        @pl.when(owner.here)
        def _(owner=owner, k=k):
            owner.spread(window, parts[owner.matrix["unit"]], back_send, back_recv, owner.k)

    for gather in spread_moments:
        gather.second()
    spread_updates = []

    def take_updates(unit):
        for k, owner in enumerate(owners):
            if owner.matrix["unit"] == unit:
                owner.arrived(window, parts[unit], back_send, back_recv, owner.k)
        total = parts[unit][0]
        if unit == MID1:
            total = total + parts[unit][1]
        updates[unit][place.y, place.x, place.c] = total
        spread_updates.append(Direct(place, updates[unit]))
        spread_updates[-1].first()

    for unit in (OUT1, OUT0, IN0, MID1, CONV0):
        take_updates(unit)
    for gather in spread_moments:
        gather.last()
    for copy in results[2:7]:
        copy.start()
    for gather in spread_updates:
        gather.second()
    for k, unit in enumerate((OUT1, OUT0, IN0, MID1, CONV0)):
        spread_updates[k].last()
        results[7 + unit].start()
    assert place.used <= gathers_used
    place.sent()
    for copy in results:
        copy.wait()


def run_step(extra, dilation, lengths, params, tokens, cotangent, moments):
    in_smem = pl.BlockSpec(memory_space=pltpu.SMEM)
    anywhere = pl.BlockSpec(memory_space=pltpu.HBM)

    def dma(n):
        return pltpu.SemaphoreType.DMA((n,))

    def pieces(chunk, lead, dtype=BF16):
        return vmem(lead + (2, 2, 2, ROWS, WIDTH[chunk]), dtype)

    shared = [jax.ShapeDtypeStruct((2, 2, 2, ROWS, w), BF16) for w in WIDTH]
    results = [jax.ShapeDtypeStruct((D, TOK), BF16), jax.ShapeDtypeStruct((D, TOK), F32)] + shared + shared
    count = 8 * len(WIDTH) + (10 + len(extra)) * len(WIDTH)
    scratch = [vmem(a.shape, a.dtype) for a in results]
    scratch += [dma(count), dma(count), dma(2 * len(MATRICES)), dma(1), dma(1), dma(len(MATRICES)), dma(24)]
    scratch += [pieces(k, (OWNERS,)) for k in UNITS] * 2
    scratch += [vmem((2 if k == MID1 else 1, ROWS, w), BF16) for k, w in enumerate(WIDTH)]
    for unit in UNITS:
        scratch += reduce_room(unit, extra)
    scratch += [vmem((OWNERS, ROWS, WINDOW), BF16)]
    scratch += [vmem(a.shape, a.dtype) for a in (tokens, cotangent) + tuple(params)]
    scratch += [
        vmem((TOK, TOK), jnp.int32),
        vmem((H, GROUPED), BF16),
        vmem((16, D), F32),
        vmem((16, H), F32),
        vmem((2, D, H), BF16),
        vmem((TOK, D), F32),
        vmem((TOK, D), F32),
        vmem((D, H), F32),
        vmem((K_ENC + 2 * K_DEC - 1, TOK, TOK), BF16),
        vmem((2, TOK, D), BF16),
        vmem((2, TOK, H), BF16),
        vmem((2, 2, TOK, GROUPED), BF16),
        vmem((GROUPED, TOK), BF16),
        vmem((TOK, 2048), BF16),
        vmem((2, TOK, D), BF16),
        vmem((2, TOK, D), BF16),
        vmem((2, TOK, 128), F32),
        vmem((2, 2, TOK, H), BF16),
        vmem((2, 2, TOK, H), BF16),
        vmem((2, 2, TOK, 128), F32),
        vmem((512, 512), F32),
        vmem((512, 512), BF16),
        vmem((2, GROUPED, 512), BF16),
    ]
    return pl.pallas_call(
        functools.partial(step_kernel, extra),
        out_shape=tuple(results),
        in_specs=[in_smem] * 2 + [anywhere] * 12,
        out_specs=(anywhere,) * 12,
        scratch_shapes=scratch,
        compiler_params=pltpu.CompilerParams(
            collective_id=0, has_side_effects=True, vmem_limit_bytes=62 << 20
        ),
        name="step",
    )(dilation, lengths, tokens, cotangent, *params, *moments)


def finish_kernel(
    vector_step, *refs,
):
    in_hbm, out_to_hbm, ins, outs = refs[:17], refs[17:32], refs[32:49], refs[49:62]
    in_sems, out_sems = refs[62:]
    moments, updates = ins[2:7], ins[7:12]
    conv, w_in, w_out, wide, narrow = ins[12:]
    (
        mom_in, mom_conv, mom_out, mom_wide, mom_narrow,
        new_in, new_conv, new_out, new_wide, new_narrow, low_in, low_conv, low_out,
    ) = outs
    arrivals = [pltpu.make_async_copy(s, t, in_sems.at[k]) for k, (s, t) in enumerate(zip(in_hbm, ins))]
    sources = outs + ins[:2]
    targets = out_to_hbm[2:] + out_to_hbm[:2]
    departures = [pltpu.make_async_copy(s, t, out_sems.at[k]) for k, (s, t) in enumerate(zip(sources, targets))]
    arrivals = arrivals[2:] + arrivals[:2]
    for copy in arrivals:
        copy.start()
    rows = slice(0, SHARD)

    def conv_parts(refs):
        enc = load(refs[CONV0], CONV0, 0, 2048, rows=rows).astype(F32)
        dec = load(refs[MID1], MID1, 0, 1280, rows=rows).astype(F32)
        dec = pltpu.roll(dec, SPLIT % 128, 1)
        middle = jnp.where(iota((SHARD, 128), 1) < SPLIT % 128, enc[:, 1920:], dec[:, :128])
        return ((0, enc[:, :1920]), (1920, middle), (2048, dec[:, 128:]))

    def out_lanes(refs, b):
        return load(refs[OUT_AT[b][0]], OUT_AT[b][0], 0, 896, rows=rows).astype(F32)[:, :D]

    def in_lanes(refs, b, h):
        unit, at = IN_AT[b]
        low, high = lane_window(at + H * h, H)
        return unshifted(load(refs[unit], unit, low, high, rows=rows).astype(F32), at + H * h, H)

    for copy in arrivals[:5]:
        copy.wait()
    for low, values in conv_parts(moments):
        mom_conv[:, low : low + values.shape[1]] = values
    departures[1].start()
    for b in range(2):
        mom_out[:, b, :] = out_lanes(moments, b)
        for h in range(2):
            mom_in[b, h * SHARD : (h + 1) * SHARD, :] = in_lanes(moments, b, h)
    departures[0].start()
    departures[2].start()
    for copy in arrivals[15:]:
        copy.wait()
    for copy in departures[13:]:
        copy.start()
    for copy in arrivals[5:15]:
        copy.wait()
    for low, values in conv_parts(updates):
        lanes = slice(low, low + values.shape[1])
        value = conv[:, lanes] - values
        new_conv[:, lanes] = value
        low_conv[:, lanes] = value.astype(BF16)
    departures[6].start()
    departures[11].start()
    for b in range(2):
        value = w_out[:, b, :] - out_lanes(updates, b)
        new_out[:, b, :] = value
        for h in range(2):
            here = slice(h * SHARD, (h + 1) * SHARD)
            value = w_in[b, here, :] - in_lanes(updates, b, h)
            new_in[b, here, :] = value
            low_in[b, here, :] = value.astype(BF16)
    low_out[...] = new_out[...].astype(BF16)
    for k in (5, 7, 10, 12):
        departures[k].start()
    vectors = load(moments[IN0], IN0, VEC_AT, VEC_AT + 128).astype(F32)
    for b in range(2):
        for k in range(6):
            m = 6 * b + k
            value = vectors[m : m + 1, :SHARD]
            mom_narrow[k, b : b + 1, :] = value
            new_narrow[k, b : b + 1, :] = narrow[k, b : b + 1, :] - vector_step * value
        for k in range(3):
            for h in range(2):
                m = 16 + 16 * h + 3 * b + k
                lanes = slice(h * SHARD, (h + 1) * SHARD)
                value = vectors[m : m + 1, :SHARD]
                mom_wide[k, b : b + 1, lanes] = value
                new_wide[k, b : b + 1, lanes] = wide[k, b : b + 1, lanes] - vector_step * value
    for k in (3, 4, 8, 9):
        departures[k].start()
    for copy in departures:
        copy.wait()


def finish(vector_step, shared, params):
    in_hbm = pl.BlockSpec(memory_space=pltpu.HBM)
    conv, w_in, w_out, wide, narrow = params
    shapes = [w_in.shape, conv.shape, w_out.shape, wide.shape, narrow.shape]
    outs = [jax.ShapeDtypeStruct(a.shape, a.dtype) for a in shared[:2]]
    outs += [jax.ShapeDtypeStruct(s, F32) for s in shapes + shapes]
    outs += [jax.ShapeDtypeStruct(s, BF16) for s in shapes[:3]]
    ins = tuple(shared) + tuple(params)
    return pl.pallas_call(
        functools.partial(finish_kernel, vector_step),
        out_shape=tuple(outs),
        in_specs=[in_hbm] * len(ins),
        out_specs=(in_hbm,) * len(outs),
        scratch_shapes=[vmem(a.shape, a.dtype) for a in ins + tuple(outs[2:])]
        + [pltpu.SemaphoreType.DMA((17,)), pltpu.SemaphoreType.DMA((15,))],
        compiler_params=pltpu.CompilerParams(vmem_limit_bytes=62 << 20),
        name="finish",
    )(*ins)


def swap(array):
    return jnp.transpose(array, (1, 0, 2))


def shards(
    extra, vector_step, tokens, cotangent, lengths, dilation, proj_in, conv_weight, proj_out, vec_wide, vec_narrow,
    mom_in, mom_conv, mom_out, mom_wide, mom_narrow,
):
    params = (conv_weight, proj_in, swap(proj_out), swap(vec_wide), swap(vec_narrow))
    moments = (mom_conv, mom_in, swap(mom_out), swap(mom_wide), swap(mom_narrow))
    shared = run_step(extra, dilation, lengths, params, tokens.T, cotangent.T, moments)
    outs = list(finish(vector_step, shared, params))
    for k in (0, 1):
        outs[k] = outs[k].T
    for k in (4, 5, 6, 9, 10, 11, 14):
        outs[k] = swap(outs[k])
    return tuple(outs)


def solution(mesh):
    groups, owners = mesh.shape["dp"], mesh.shape["fsdp"]
    assert owners == OWNERS and groups % PIECES == 0
    extra, bit = [], PIECES
    while bit < groups:
        extra.append(bit)
        bit *= 2
    assert bit == groups
    vector_step = VECTOR_RATE / math.sqrt(TOK * groups * owners)
    tok, rep = P(("dp", "fsdp"), None), P()
    mid, first, final = P(None, "fsdp", None), P("fsdp", None), P(None, None, "fsdp")
    params = (mid, first, mid, final, final)
    return jax.shard_map(
        functools.partial(shards, tuple(extra), vector_step),
        mesh=mesh,
        in_specs=(tok, tok, tok, rep) + params + params,
        out_specs=(tok, tok) + params + params + (mid, first, mid),
        check_vma=False,
    )
```

```python
import functools
import math

import jax
import jax.numpy as jnp
from jax import lax
from jax.experimental import pallas as pl
from jax.experimental.pallas import tpu as pltpu
from jax.sharding import PartitionSpec as P

D = 800
H = 400
K_ENC = 5
K_DEC = 3
NS_STEPS = 5
EPSILON = 1e-05
NORM_FLOOR = 1e-07
COEF_A = 3.4445
COEF_B = -4.775
COEF_C = 2.0315
MOMENT_DECAY = 0.5
MATRIX_RATE = 0.5
VECTOR_RATE = 0.1

F32 = jnp.float32
BF16 = jnp.bfloat16
MESH = pl.DeviceIdType.MESH

OWNERS = 4
PIECES = 8
SHARD = 100
ROWS = 112
IN0, CONV0, OUT0, MID1, OUT1 = range(5)
WIDTH = (128, 256, 128, 256, 128)
UNITS = range(len(WIDTH))
IN_AT = ((IN0, 0), (MID1, 1200))
OUT_AT = ((OUT0, 0), (OUT1, 0))
CONV_AT = ((CONV0, 0), (MID1, 0))
CONV_SPAN = (2048, 1280)
VEC_AT = 896
SPLIT = K_ENC * H
TOK = 256
GROUPED = OWNERS * ROWS
WINDOW = 2048

GELU_K = math.sqrt(2.0 / math.pi)
GELU_C = 0.044715


def vmem(shape, dtype):
    return pltpu.VMEM(shape, dtype)


def dot(a, b):
    return lax.dot_general(a, b, (((1,), (0,)), ((), ())), preferred_element_type=F32)


def dot_nt(a, b):
    return lax.dot_general(a, b, (((1,), (1,)), ((), ())), preferred_element_type=F32)


def dot_tn(a, b):
    return lax.dot_general(a, b, (((0,), (0,)), ((), ())), preferred_element_type=F32)


def one_hot(mask):
    return jnp.where(mask, 1.0, 0.0).astype(BF16)


def iota(shape, dim):
    return lax.broadcasted_iota(jnp.int32, shape, dim)


def add_low(*parts):
    total = parts[0].astype(F32)
    for part in parts[1:]:
        total = total + part.astype(F32)
    return total.astype(BF16)


def spans(chunk, low, high):
    width = WIDTH[chunk]
    for q in range(low // width, -(-high // width)):
        yield q, max(low - q * width, 0), min(high - q * width, width)


def load(ref, chunk, low, high, lead=(), rows=slice(None)):
    parts = []
    for q, start, stop in spans(chunk, low, high):
        parts.append(ref[lead + (q // 4, q // 2 % 2, q % 2, rows, slice(start, stop))])
    return parts[0] if len(parts) == 1 else jnp.concatenate(parts, axis=-1)


def store(ref, chunk, low, value, lead=(), rows=slice(None), add=False):
    at = 0
    for q, start, stop in spans(chunk, low, low + value.shape[-1]):
        index = lead + (q // 4, q // 2 % 2, q % 2, rows, slice(start, stop))
        part = value[..., at : at + stop - start]
        ref[index] = add_low(ref[index], part) if add else part
        at += stop - start


def shifted(values, at, low, high):
    rows, count = values.shape
    base = at - at % 128
    width = -(-(at % 128 + count) // 128) * 128
    parts = []
    if base > low:
        parts.append(jnp.zeros((rows, base - low), F32))
    if width > count:
        values = jnp.concatenate([values, jnp.zeros((rows, width - count), F32)], axis=1)
    parts.append(pltpu.roll(values, at % 128, 1) if at % 128 else values)
    if high > base + width:
        parts.append(jnp.zeros((rows, high - base - width), F32))
    return parts[0] if len(parts) == 1 else jnp.concatenate(parts, axis=1)


def lane_window(at, count):
    return at - at % 128, -(-(at + count) // 128) * 128


def unshifted(values, at, count):
    if at % 128:
        values = pltpu.roll(values, values.shape[1] - at % 128, 1)
    return values[:, :count]


def lay_out(unit, conv, w_in, w_out, wide, narrow, put):
    rows = slice(0, SHARD)
    for b in range(2):
        if unit == CONV_AT[b][0]:
            low, high = (0, SPLIT) if b == 0 else (SPLIT, SPLIT + K_DEC * H)
            start, stop = lane_window(low, high - low)
            stop = min(stop, 3200)
            values = unshifted(conv[:, start:stop], low, high - low)
            put(0, rows, values, False)
        if unit == OUT_AT[b][0]:
            put(0, rows, w_out[:, b, :], False)
        if unit == IN_AT[b][0]:
            at = IN_AT[b][1]
            low, high = lane_window(at, 2 * H)
            values = shifted(w_in[b, :SHARD, :], at, low, high) + shifted(w_in[b, SHARD:, :], at + H, low, high)
            put(low, rows, values, True)
    if unit == IN0:
        for b in range(2):
            for k in range(6):
                m = 6 * b + k
                put(VEC_AT, slice(m, m + 1), narrow[k, b : b + 1, :], False)
            for k in range(3):
                for h in range(2):
                    m = 16 + 16 * h + 3 * b + k
                    put(VEC_AT, slice(m, m + 1), wide[k, b : b + 1, h * SHARD : (h + 1) * SHARD], False)


def flip(value, bit):
    return value + bit - 2 * bit * ((value // bit) % 2)


def other_owner(own, step):
    if step == 0:
        return own
    if step == 3:
        return 3 - own
    return flip(own, step)


def remote(src, dst, send, recv, device):
    return pltpu.make_async_remote_copy(
        src_ref=src,
        dst_ref=dst,
        send_sem=send,
        recv_sem=recv,
        device_id=device,
        device_id_type=MESH,
    )


class Place:
    def __init__(self, send, recv, extra):
        at = lax.axis_index("dp")
        self.piece = at % PIECES
        self.base = at - self.piece
        self.me = at
        self.own = lax.axis_index("fsdp")
        self.y, self.x, self.c = self.piece // 4, self.piece // 2 % 2, self.piece % 2
        self.core, self.near_x, self.near_y = [
            (self.base + flip(self.piece, bit), self.own) for bit in (1, 2, 4)
        ]
        self.near_xy = (self.base + flip(flip(self.piece, 2), 4), self.own)
        self.column = [(at, other_owner(self.own, step)) for step in (1, 2, 3)]
        self.far = [(flip(at, bit), self.own) for bit in extra]
        self.send, self.recv, self.used = send, recv, 0
        self.started = []

    def take(self, count):
        first = self.used
        self.used += count
        return first

    def start(self, src, dst, device):
        k = self.take(1)
        copy = remote(src, dst, self.send.at[k], self.recv.at[k], device)
        copy.start()
        self.started.append(copy)
        return copy

    def sent(self):
        for copy in self.started:
            copy.wait_send()
        self.started = []


class Direct:
    ALL = slice(None)

    def __init__(self, place, ref):
        self.place, self.ref = place, ref

    def first(self):
        p = self.place
        mine = self.ref.at[p.y, p.x, p.c]
        self.copies = [p.start(mine, mine, device) for device in (p.near_x, p.near_y, p.near_xy)]

    def second(self):
        p = self.place
        for copy in self.copies:
            copy.wait_recv()
        pieces = self.ref.at[self.ALL, self.ALL, p.c]
        self.copies = [p.start(pieces, pieces, p.core)]

    def last(self):
        self.copies[0].wait_recv()


class Gather:
    LOW, HIGH, ALL = pl.ds(0, 64), pl.ds(64, 48), slice(None)

    def __init__(self, place, view):
        self.place, self.view = place, view

    def move(self, device, *index):
        ref = self.view(*index)
        return self.place.start(ref, ref, device)

    def first(self):
        p = self.place
        self.a = self.move(p.near_y, p.y, p.x, p.c, self.LOW)
        self.b = self.move(p.near_x, p.y, p.x, p.c, self.HIGH)

    def second(self):
        p = self.place
        self.a.wait_recv()
        self.a = self.move(p.near_x, self.ALL, p.x, p.c, self.LOW)
        self.b.wait_recv()
        self.b = self.move(p.near_y, p.y, self.ALL, p.c, self.HIGH)

    def third(self):
        p = self.place
        self.a.wait_recv()
        self.b.wait_recv()
        self.a = self.move(p.core, self.ALL, self.ALL, p.c, self.ALL)

    def last(self):
        self.a.wait_recv()


class WeightGather(Gather):
    def __init__(self, place, ref, low, width):
        lanes = pl.ds(low, width)

        def view(y, x, c, rows):
            return ref.at[pl.ds(1, 3), y, x, c, rows, lanes]

        super().__init__(place, view)
        self.ref, self.lanes = ref, lanes

    def cross(self):
        p = self.place
        index = (p.y, p.x, p.c, self.ALL, self.lanes)
        mine = self.ref.at[(0,) + index]
        self.crossing = [
            p.start(mine, self.ref.at[(step,) + index], p.column[step - 1]) for step in (1, 2, 3)
        ]

    def first(self, follower=None):
        for copy in self.crossing:
            copy.wait_recv()
        if follower is not None:
            follower.cross()
        super().first()


class Reduce:
    def __init__(self, place, grads, moment, room):
        self.place, self.grads, self.moment = place, grads, moment
        self.from_core, self.sums, self.from_x, self.from_y = room[:4]
        self.last_x, self.last_y, self.from_z, self.from_far = room[4:]

    def core(self):
        p = self.place
        self.halves = []
        for y in (1 - p.y, p.y):
            src = self.grads.at[:, y, :, 1 - p.c]
            self.halves.append((y, p.start(src, self.from_core.at[:, y], p.core)))

    def plane(self):
        p = self.place
        self.a = []
        for k, (y, copy) in enumerate(self.halves):
            copy.wait_recv()
            self.sums[:, y] = add_low(self.grads[:, y, :, p.c], self.from_core[:, y])
            self.a.append(
                p.start(self.sums.at[0:2, y, 1 - p.x], self.from_x.at[:, y], p.near_x)
            )
            if k == 0:
                self.b = p.start(self.sums.at[2:4, y], self.from_y, p.near_y)

    def turn(self):
        p = self.place
        y, x = 1 - p.y, 1 - p.x
        self.a[0].wait_recv()
        self.sums[0:2, y, p.x] = add_low(self.sums[0:2, y, p.x], self.from_x[:, y])
        self.y_last = p.start(self.sums.at[0:2, y, p.x], self.last_y, p.near_y)
        self.b.wait_recv()
        self.sums[2:4, p.y, x] = add_low(self.sums[2:4, p.y, x], self.from_y[:, x])
        self.x_last = p.start(self.sums.at[2:4, p.y, x], self.last_x, p.near_x)

    def cross(self):
        p = self.place
        y, x = p.y, p.x
        self.a[1].wait_recv()
        self.y_last.wait_recv()
        self.sums[0:2, y, x] = add_low(self.sums[0:2, y, x], self.from_x[:, y], self.last_y[...])
        self.x_last.wait_recv()
        self.sums[2:4, y, x] = add_low(self.sums[2:4, y, x], self.from_y[:, x], self.last_x[...])
        for k, device in enumerate(p.far):
            p.start(self.sums.at[:, y, x], self.from_far.at[k], device).wait_recv()
            p.started.pop().wait_send()
            self.sums[:, y, x] = add_low(self.sums[:, y, x], self.from_far[k])
        self.crossing = [
            p.start(self.sums.at[step, y, x], self.from_z.at[step - 1], p.column[step - 1])
            for step in (1, 2, 3)
        ]

    def finish(self):
        p = self.place
        for copy in self.crossing:
            copy.wait_recv()
        parts = [self.sums[0, p.y, p.x]] + [self.from_z[k] for k in range(3)]
        self.moment[p.y, p.x, p.c] = add_low(self.moment[p.y, p.x, p.c], *parts)


def reduce_room(chunk, extra):
    width = WIDTH[chunk]
    shapes = (
        (OWNERS, 2, 2), (OWNERS, 2, 2), (2, 2), (2, 2), (2,), (2,), (3,), (max(len(extra), 1), OWNERS),
    )
    return [vmem(shape + (ROWS, width), BF16) for shape in shapes]


MATRICES = (
    dict(
        kind="row", unit=OUT1, first=0, last=6, piece=5, lanes=(0, D), slot=0, scale=math.sqrt(D / H),
        owners=((0, 0, 2), (3, 2, 2)),
    ),
    dict(
        kind="row", unit=MID1, first=0, last=4, piece=2, lanes=(0, K_DEC * H), slot=0, scale=1.0,
        owners=((0, 0, 2), (3, 2, 2)),
    ),
    dict(
        kind="in", unit=MID1, first=4, last=7, piece=4, lanes=(176, 976), slot=1, scale=1.0,
        owners=((0, 0, 2), (3, 2, 2)),
    ),
    dict(
        kind="row", unit=OUT0, first=0, last=6, piece=3, lanes=(0, D), slot=0, scale=math.sqrt(D / H),
        owners=((1, 0, 2), (2, 2, 2)),
    ),
    dict(
        kind="row", unit=CONV0, first=0, last=7, piece=0, lanes=(0, SPLIT), slot=0, scale=1.0,
        owners=((1, 0, 2), (2, 2, 2)),
    ),
    dict(
        kind="in", unit=IN0, first=0, last=6, piece=6, lanes=(0, D), slot=0, scale=1.0,
        owners=((1, 0, 2), (2, 2, 2)),
    ),
)


class Owner:
    def __init__(self, place, k, owner):
        self.place, self.k = place, k
        matrix = self.matrix = MATRICES[k]
        at, self.first, self.shards = owner
        self.at = at
        self.width = WIDTH[matrix["unit"]]
        self.count = OWNERS * (matrix["last"] - matrix["first"] + 1)
        p = place
        self.here = (p.piece == matrix["piece"]) & (p.own == at)
        self.away = (p.piece != matrix["piece"]) | (p.own != at)
        self.holds = (p.piece >= matrix["first"]) & (p.piece <= matrix["last"])
        self.served = (p.own >= self.first) & (p.own < self.first + self.shards)
        self.device = (p.base + matrix["piece"], at)
    def each_served(self, act):
        def body(k, carry):
            piece = self.matrix["first"] + k // self.shards
            own = self.first + k % self.shards

            @pl.when((piece != self.matrix["piece"]) | (own != self.at))
            def _():
                act(k // self.shards, own, (self.place.base + piece, own))

            return carry

        lax.fori_loop(0, self.count // OWNERS * self.shards, body, 0)

    def lanes(self, k):
        return pl.ds(pl.multiple_of(k * self.width, 128), self.width)

    def to_owner(self, moment, window, send, recv, k):
        p = self.place
        at = p.piece - self.matrix["first"]
        src = moment.at[p.y, p.x, p.c]
        dst = window.at[p.own, :, self.lanes(at)]
        return remote(src, dst, send.at[k], recv.at[0], self.device)

    def gather(self, moment, window, send, recv, k):
        @pl.when(self.holds & self.away)
        def _():
            self.to_owner(moment, window, send, recv, k).start()

        @pl.when(self.here)
        def _():
            p = self.place
            at = p.piece - self.matrix["first"]
            pltpu.make_async_copy(
                moment.at[p.y, p.x, p.c], window.at[p.own, :, self.lanes(at)], recv.at[0]
            ).start()

    def gather_sent(self, moment, window, send, recv, k):
        @pl.when(self.holds & self.away)
        def _():
            self.to_owner(moment, window, send, recv, k).wait_send()

    def whole(self, window, slots, sem):
        values = window.at[slots, :, pl.ds(0, self.count // OWNERS * self.width)]
        return pltpu.make_async_copy(values, values, sem.at[0])

    def gathered(self, window, recv):
        self.whole(window, pl.ds(0, OWNERS), recv).wait()

    def spread(self, window, parts, send, recv, k):
        p = self.place
        slot = parts.at[self.matrix["slot"]]

        def act(at, own, device):
            remote(window.at[own, :, self.lanes(at)], slot, send.at[0], recv.at[k], device).start()

        self.each_served(act)
        if self.first <= self.at < self.first + self.shards:
            at = p.piece - self.matrix["first"]
            pltpu.make_async_copy(window.at[p.own, :, self.lanes(at)], slot, send.at[0]).start()

    def arrived(self, window, parts, send, recv, k):
        @pl.when(self.here)
        def _():
            self.whole(window, pl.ds(self.first, self.shards), send).wait()

        @pl.when(self.holds & self.served & self.away)
        def _():
            src = window.at[0, :, self.lanes(0)]
            dst = parts.at[self.matrix["slot"]]
            remote(src, dst, send.at[0], recv.at[k], self.device).wait_recv()


def split(a):
    high = a.astype(BF16)
    return high, (a - high.astype(F32)).astype(BF16)


def dot_fine(a, b):
    a_high, a_low = split(a)
    b_high, b_low = split(b)
    return dot(a_high, b_high) + (dot(a_high, b_low) + dot(a_low, b_high))


def dot_low(a, b):
    return dot(a.astype(BF16), b.astype(BF16))


def polynomial_of(gram):
    size = gram.shape[0]
    eye = iota((size, size), 0) == iota((size, size), 1)
    unit = jnp.where(eye, 1.0, 0.0)
    power = jnp.sum(jnp.sum(jnp.where(eye, gram, 0.0), axis=1, keepdims=True), axis=0, keepdims=True)
    inverse = 1.0 / (jnp.sqrt(power) + NORM_FLOOR)
    current = gram * inverse * inverse
    result = None
    for step in range(NS_STEPS):
        square = dot_fine if step > 2 else dot_low
        poly = COEF_A * unit + COEF_B * current + COEF_C * square(current, current)
        result = poly if result is None else dot_low(poly, result)
        if step < NS_STEPS - 1:
            first = dot_fine if step < 2 else dot_low
            second = dot_fine if step < 1 else dot_low
            current = second(first(poly, current), poly)
    return result, inverse


def orthogonalize(owners, window, gram, poly, halves):
    is_row = False
    high, factor, parts = jnp.int32(0), jnp.float32(0), jnp.int32(0)
    low_half, high_half = jnp.int32(0), jnp.int32(0)
    for owner in owners:
        matrix, here = owner.matrix, owner.here
        if matrix["kind"] == "row":
            is_row = is_row | here
        high = jnp.where(here, matrix["lanes"][1], high)
        parts = jnp.where(here, -(-matrix["lanes"][1] // 512), parts)
        factor = jnp.where(here, MATRIX_RATE * matrix["scale"], factor)
        low_half = jnp.where(here, owner.first // 2, low_half)
        high_half = jnp.where(here, (owner.first + owner.shards) // 2, high_half)
    ins = {}
    for owner in owners:
        if owner.matrix["kind"] == "in":
            at = owner.matrix["lanes"][0]
            ins[at] = ins.get(at, False) | owner.here
    is_in = False
    for here in ins.values():
        is_in = is_in | here

    def part(k):
        lanes = pl.ds(pl.multiple_of(k * 512, 512), 512)
        values = window[:, :, lanes].reshape(GROUPED, 512)
        lane = iota((GROUPED, 512), 1) + k * 512
        return lanes, jnp.where(lane < high, values, jnp.zeros((), BF16))

    for at, here in ins.items():

        @pl.when(here)
        def _(at=at):
            valid = iota((GROUPED, 512), 1) < H
            for h in range(2):
                low = (at + H * h) // 128 * 128
                values = window[:, :, low : low + 512].reshape(GROUPED, 512).astype(F32)
                if (at + H * h) % 128:
                    values = pltpu.roll(values, 512 - (at + H * h) % 128, 1)
                halves[h] = jnp.where(valid, values, 0.0).astype(BF16)

    @pl.when(is_in)
    def _():
        gram[...] = dot_tn(halves[0], halves[0]) + dot_tn(halves[1], halves[1])

    @pl.when(is_row)
    def _():
        gram[...] = jnp.zeros(gram.shape, F32)

        def body(k, carry):
            values = part(k)[1]
            gram[:GROUPED, :GROUPED] += dot_nt(values, values)
            return carry

        lax.fori_loop(0, parts, body, 0)

    @pl.when(is_in | is_row)
    def _():
        result, inverse = polynomial_of(gram[...])
        poly[...] = (result * (inverse * factor)).astype(BF16)

    for at, here in ins.items():

        @pl.when(here)
        def _(at=at):
            window[:, :, :1024] = jnp.zeros((OWNERS, ROWS, 1024), BF16)

            def body(two_at, carry):
                two, served = pl.ds(2 * two_at, 2), pl.ds(pl.multiple_of(2 * ROWS * two_at, 2 * ROWS), 2 * ROWS)
                for h in range(2):
                    low = (at + H * h) // 128 * 128
                    step = dot_nt(halves[h, served], poly[...])
                    if (at + H * h) % 128:
                        step = pltpu.roll(step, (at + H * h) % 128, 1)
                    lanes = slice(low, low + 512)
                    window[two, :, lanes] = add_low(window[two, :, lanes], step.reshape(2, ROWS, 512))
                return carry

            lax.fori_loop(low_half, high_half, body, 0)

    @pl.when(is_row)
    def _():
        def body(k, carry):
            lanes, values = part(k)

            def half(two_at, carry):
                two, served = pl.ds(2 * two_at, 2), pl.ds(pl.multiple_of(2 * ROWS * two_at, 2 * ROWS), 2 * ROWS)
                step = dot(poly[served, :GROUPED], values)
                window[two, :, lanes] = step.astype(BF16).reshape(2, ROWS, 512)
                return carry

            lax.fori_loop(low_half, high_half, half, 0)
            return carry

        lax.fori_loop(0, parts, body, 0)


def norm_forward(src, width, gain, shift, act, unit, slope, spread, chunk=256):
    def body(k, carry):
        rows = pl.ds(pl.multiple_of(k * chunk, chunk), chunk)
        x = src[rows, :width].astype(F32)
        center = x - jnp.mean(x, axis=1, keepdims=True)
        scale = lax.rsqrt(jnp.mean(center * center, axis=1, keepdims=True) + EPSILON)
        xhat = center * scale
        a = xhat * gain + shift
        square = a * a
        half = 0.5 + 0.5 * jnp.tanh(a * (GELU_K + (GELU_K * GELU_C) * square))
        act[rows, :width] = (a * half).astype(BF16)
        unit[rows, :width] = xhat.astype(BF16)
        inner = GELU_K + (3.0 * GELU_K * GELU_C) * square
        slope[rows, :width] = (half + (2.0 * a * inner) * (half * (1.0 - half))).astype(BF16)
        spread[rows, :] = jnp.broadcast_to(scale, (chunk, 128))
        return carry

    lax.fori_loop(0, TOK // chunk, body, 0)


def fold_rows(values):
    total = values[0:8]
    for k in range(1, values.shape[0] // 8):
        total = total + values[8 * k : 8 * k + 8]
    return total


def norm_backward(grad, width, gain, unit, slope, spread, finish, chunk=256):
    def body(k, sums):
        rows = pl.ds(pl.multiple_of(k * chunk, chunk), chunk)
        da = grad[rows, :width] * slope[rows, :width].astype(F32)
        xhat = unit[rows, :width].astype(F32)
        product = da * xhat
        dxhat = da * gain
        mean_one = jnp.mean(dxhat, axis=1, keepdims=True)
        mean_two = jnp.mean(dxhat * xhat, axis=1, keepdims=True)
        dx = spread[rows, 0:1] * (dxhat - mean_one - xhat * mean_two)
        finish(rows, dx)
        return (sums[0] + fold_rows(product), sums[1] + fold_rows(da), sums[2] + fold_rows(dx))

    zero = jnp.zeros((8, width), F32)
    sums = lax.fori_loop(0, TOK // chunk, body, (zero, zero, zero))
    return tuple(jnp.sum(s, axis=0, keepdims=True) for s in sums)


def step_kernel(
    extra,
    dilation, lengths, tokens_hbm, cotangent_hbm,
    conv_hbm, in_hbm, out_hbm, wide_hbm, narrow_hbm,
    mom_conv_hbm, mom_in_hbm, mom_out_hbm, mom_wide_hbm, mom_narrow_hbm,
    *refs,
):
    results = refs[:12]
    refs = refs[12:]
    out, grad_tokens, moments, updates = refs[0], refs[1], refs[2:7], refs[7:12]
    refs = refs[2:]
    send, recv, own_send, own_recv, back_send, back_recv, local = refs[10:17]
    full, grads, parts = refs[17:22], refs[22:27], refs[27:32]
    rooms = refs[32:72]
    (
        window,
        tokens, cotangent, conv, in_shard, out_shard, wide_shard, narrow_shard,
        far, perm_h, vec_w, vec_n, w_in, x_one, wide_grad, tall,
        masks, act_d, act_h, act_g, act_t, e_all,
        unit_d, slope_d, spread_d, unit_h, slope_h, spread_h,
        gram, poly, halves,
    ) = refs[72:]
    place = Place(send, recv, extra)
    own = place.own
    owners = [Owner(place, k, owner) for k, matrix in enumerate(MATRICES) for owner in matrix["owners"]]
    conv_in, spare = gram.at[:TOK], gram.at[TOK:]
    hid = spare

    results = [
        pltpu.make_async_copy(source, target, local.at[12 + k])
        for k, (source, target) in enumerate(zip((out, grad_tokens) + moments + updates, results))
    ]

    sources = (conv_hbm, in_hbm, out_hbm, wide_hbm, narrow_hbm, tokens_hbm, cotangent_hbm)
    shard = (conv, in_shard, out_shard, wide_shard, narrow_shard)
    targets = shard + (tokens, cotangent)
    fetches = [pltpu.make_async_copy(s, t, local.at[k]) for k, (s, t) in enumerate(zip(sources, targets))]
    for fetch in fetches:
        fetch.start()
    barrier = pltpu.get_barrier_semaphore()
    for device in [place.core, place.near_x, place.near_y] + place.column + place.far:
        pl.semaphore_signal(barrier, inc=1, device_id=device, device_id_type=MESH)

    def pack(unit):
        full[unit][0] = jnp.zeros(full[unit].shape[1:], BF16)

        def put(low, rows, values, add):
            store(full[unit], unit, low, values.astype(BF16), lead=(0,), rows=rows, add=add)

        lay_out(unit, *shard, put)

    in_unit = WeightGather(place, full[IN0], 0, 128)
    conv_unit = WeightGather(place, full[CONV0], 0, 256)
    out_unit = WeightGather(place, full[OUT0], 0, 128)
    mid_unit = WeightGather(place, full[MID1], 0, 256)
    last_unit = WeightGather(place, full[OUT1], 0, 128)

    for k in (1, 3, 4):
        fetches[k].wait()
    pack(IN0)
    pl.semaphore_wait(barrier, 6 + len(extra))
    in_unit.cross()
    fetches[0].wait()
    pack(CONV0)
    conv_unit.cross()
    fetches[2].wait()
    for unit in (OUT0, MID1, OUT1):
        pack(unit)
    sources = (mom_conv_hbm, mom_in_hbm, mom_out_hbm, mom_wide_hbm, mom_narrow_hbm)
    moment_fetches = [pltpu.make_async_copy(s, t, local.at[7 + k]) for k, (s, t) in enumerate(zip(sources, shard))]
    for fetch in moment_fetches:
        fetch.start()

    row, col = iota((TOK, TOK), 0), iota((TOK, TOK), 1)
    seg_row, seg_col = jnp.zeros((TOK, TOK), jnp.int32), jnp.zeros((TOK, TOK), jnp.int32)
    end = jnp.int32(0)
    for k in range(8):
        end = end + lengths[0, k]
        seg_row = seg_row + jnp.where(row >= end, 1, 0)
        seg_col = seg_col + jnp.where(col >= end, 1, 0)
    far[...] = jnp.where(seg_row == seg_col, col - row, 4 * TOK)

    enc_shifts = [(j - K_ENC // 2) * dilation[0] for j in range(K_ENC)]
    dec_shifts = [j * dilation[1] for j in range(1 - K_DEC, K_DEC)]
    for k, shift in enumerate(enc_shifts + dec_shifts):
        masks[k] = one_hot(far[...] == shift)
    tap_masks = (
        [(j, K_ENC - 1 - j) for j in range(K_ENC)],
        [(K_ENC + K_DEC - 1 - j, K_ENC + K_DEC - 1 + j) for j in range(K_DEC)],
    )

    for fetch in moment_fetches:
        fetch.wait()
    for unit in UNITS:
        moments[unit][...] = jnp.zeros(moments[unit].shape, BF16)

        def put_moment(low, rows, values, add, unit=unit):
            store(moments[unit], unit, low, (MOMENT_DECAY * values).astype(BF16), rows=rows, add=add)

        lay_out(unit, *shard, put_moment)
        parts[unit][...] = jnp.zeros(parts[unit].shape, BF16)

    in_unit.first(out_unit)
    conv_unit.first(mid_unit)
    row, col = iota((H, GROUPED), 0), iota((H, GROUPED), 1)
    used = jnp.zeros((H, GROUPED), jnp.int32)
    for s in range(OWNERS):
        r = col - ROWS * s
        inside = (r >= 0) & (r < SHARD) & (row == r + SHARD * other_owner(own, s))
        used = used + jnp.where(inside, 1, 0)
    perm_h[...] = used.astype(F32).astype(BF16)
    in_unit.second()
    out_unit.first(last_unit)
    fetches[5].wait()
    x_one[...] = tokens[...].astype(F32).T
    conv_unit.second()
    in_unit.third()
    fetches[6].wait()
    wide_grad[...] = cotangent[...].astype(F32).T
    mid_unit.first()
    out_unit.second()
    conv_unit.third()
    in_unit.last()

    row_n, col_n = iota((128, H), 0), iota((128, H), 1)
    row_w, col_w = iota((128, D), 0), iota((128, D), 1)

    def put_narrow(s):
        return one_hot((col_n == row_n + SHARD * other_owner(own, s)) & (row_n < SHARD))

    def put_wide(s, h):
        return one_hot((col_w == row_w + SHARD * (2 * other_owner(own, s) + h)) & (row_w < SHARD))

    total_n, total_w = jnp.zeros((16, H), F32), jnp.zeros((16, D), F32)
    for s in range(OWNERS):
        vectors = load(full[IN0], IN0, VEC_AT, VEC_AT + 128, lead=(s,))
        total_n = total_n + dot(vectors[0:16], put_narrow(s))
        for h in range(2):
            total_w = total_w + dot(vectors[16 + 16 * h : 32 + 16 * h], put_wide(s, h))
    vec_n[...] = total_n
    vec_w[...] = total_w

    def narrow(b, k):
        return vec_n[6 * b + k : 6 * b + k + 1, :]

    def wide(b, k):
        return vec_w[3 * b + k : 3 * b + k + 1, :]

    def weights(unit, low, high):
        return load(full[unit], unit, low, high, lead=(slice(None),)).reshape(GROUPED, high - low)

    def weight_out(b):
        return weights(OUT_AT[b][0], 0, 896)[:, :D]

    def place_in(b):
        unit, at = IN_AT[b]
        for i in range(OWNERS):
            slot = other_owner(own, i)
            for h in range(2):
                low, high = lane_window(at + H * h, H)
                values = load(full[unit], unit, low, high, lead=(slot,)).astype(F32)[:SHARD]
                row_at = SHARD * (2 * i + h)
                tall[row_at : row_at + SHARD, :] = unshifted(values, at + H * h, H)
        w_in[b] = tall[...].astype(BF16)

    def taps(b):
        return [(H * j, forward, backward) for j, (forward, backward) in enumerate(tap_masks[b])]

    def forward_in(b):
        norm_forward(x_one, D, wide(b, 0), wide(b, 1), act_d.at[b], unit_d.at[b], slope_d.at[b], spread_d.at[b])
        place_in(b)
        hid[:, :H] = dot(act_d[b], w_in[b]) + narrow(b, 0)
        norm_forward(
            hid, H, narrow(b, 1), narrow(b, 2), act_h.at[0], unit_h.at[b, 0], slope_h.at[b, 0], spread_h.at[b, 0]
        )
        act_g[b, 0] = dot(act_h[0], perm_h[...]).astype(BF16)

    def forward_conv(b):
        for j, (at, mask, unused) in enumerate(taps(b)):
            moved = dot(masks[mask], act_g[b, 0]).astype(BF16)
            low = at - at % 128
            product = dot(moved, weights(CONV_AT[b][0], low, low + 512))
            if at % 128:
                product = pltpu.roll(product, 512 - at % 128, 1)
            if j == 0:
                conv_in[...] = product
            else:
                conv_in[...] += product
        conv_in[:, :H] += narrow(b, 3)

    def forward_out(b):
        norm_forward(
            conv_in, H, narrow(b, 4), narrow(b, 5), act_h.at[1], unit_h.at[b, 1], slope_h.at[b, 1], spread_h.at[b, 1]
        )
        act_g[b, 1] = dot(act_h[1], perm_h[...]).astype(BF16)
        return (x_one[...] + dot(act_g[b, 1], weight_out(b))) + wide(b, 2)

    forward_in(0)
    last_unit.first()
    mid_unit.second()
    out_unit.third()
    conv_unit.last()
    forward_conv(0)
    last_unit.second()
    mid_unit.third()
    out_unit.last()
    x_one[...] = forward_out(0)
    last_unit.third()

    mid_unit.last()
    forward_in(1)
    forward_conv(1)
    last_unit.last()
    out[...] = forward_out(1).T.astype(BF16)
    results[0].start()
    place.sent()
    gathers_used = place.used

    reduces = [Reduce(place, grads[k], moments[k], rooms[8 * k : 8 * k + 8]) for k in UNITS]
    grouped = (slice(None),)

    def put_grads(unit, low, values, add=False):
        store(grads[unit], unit, low, values.reshape(OWNERS, ROWS, values.shape[-1]), lead=grouped, add=add)

    rows_w, rows_n = [None] * 6, [None] * 12

    def keep_low(rows, dx):
        act_h[0, rows, :] = dx.astype(BF16)

    def backward_weight_out(b):
        rows_w[3 * b + 2] = jnp.sum(wide_grad[...], axis=0, keepdims=True)
        product = dot_tn(act_g[b, 1], wide_grad[...].astype(BF16)).astype(BF16)
        put_grads(OUT_AT[b][0], 0, jnp.concatenate([product, jnp.zeros((GROUPED, 1024 - D), BF16)], axis=1))

    def backward_out(b):
        back = dot_nt(wide_grad[...].astype(BF16), weight_out(b)).astype(BF16)
        spare[:, :H] = dot_nt(back, perm_h[...])
        sums = norm_backward(
            spare, H, narrow(b, 4), unit_h.at[b, 1], slope_h.at[b, 1], spread_h.at[b, 1], keep_low
        )
        rows_n[6 * b + 4], rows_n[6 * b + 5], rows_n[6 * b + 3] = sums

    def backward_conv(b):
        span = CONV_SPAN[b]
        e_all[:, :span] = jnp.zeros((TOK, span), BF16)
        for at, unused, mask in taps(b):
            moved = dot(masks[mask], act_h[0])
            moved = jnp.concatenate([moved, jnp.zeros((TOK, 512 - H), F32)], axis=1)
            if at % 128:
                moved = pltpu.roll(moved, at % 128, 1)
            low = at - at % 128
            e_all[:, low : low + 512] += moved.astype(BF16)
        act_t[...] = act_g[b, 0].T
        for low in range(0, span, 512):
            high = min(low + 512, span)
            put_grads(CONV_AT[b][0], low, dot(act_t[...], e_all[:, low:high]).astype(BF16))

    def backward_hidden(b):
        span = CONV_SPAN[b]
        back = None
        for low in range(0, span, 512):
            high = min(low + 512, span)
            part = dot_nt(e_all[:, low:high], weights(CONV_AT[b][0], low, high))
            back = part if back is None else back + part
        spare[:, :H] = dot_nt(back.astype(BF16), perm_h[...])
        sums = norm_backward(
            spare, H, narrow(b, 1), unit_h.at[b, 0], slope_h.at[b, 0], spread_h.at[b, 0], keep_low
        )
        rows_n[6 * b + 1], rows_n[6 * b + 2], rows_n[6 * b + 0] = sums

    def backward_weight_in(b):
        unit, at = IN_AT[b]
        tall[...] = dot_tn(act_d[b], act_h[0])
        low, high = lane_window(at, 2 * H)
        spare_rows = slice(SHARD, ROWS)
        if at % 128:
            rest = jnp.zeros((OWNERS, ROWS - SHARD, high - low - 128), BF16)
            store(grads[unit], unit, low + 128, rest, lead=grouped, rows=spare_rows)
        else:
            rest = jnp.zeros((OWNERS, ROWS - SHARD, high - low), BF16)
            store(grads[unit], unit, low, rest, lead=grouped, rows=spare_rows)
        for i in range(OWNERS):
            slot = other_owner(own, i)
            first = tall[2 * SHARD * i : 2 * SHARD * i + SHARD, :]
            second = tall[2 * SHARD * i + SHARD : 2 * SHARD * (i + 1), :]
            whole = shifted(first, at, low, high) + shifted(second, at + H, low, high)
            where = dict(lead=(slot,), rows=slice(0, SHARD))
            if at % 128:
                store(grads[unit], unit, low, whole[:, :128], add=True, **where)
                store(grads[unit], unit, low + 128, whole[:, 128:].astype(BF16), **where)
            else:
                store(grads[unit], unit, low, whole.astype(BF16), **where)

    def backward_in(b):
        x_one[...] = dot_nt(act_h[0], w_in[b])

        def add_up(rows, dx):
            wide_grad[rows, :] += dx

        sums = norm_backward(
            x_one, D, wide(b, 0), unit_d.at[b], slope_d.at[b], spread_d.at[b], add_up
        )
        rows_w[3 * b + 0], rows_w[3 * b + 1] = sums[0], sums[1]

    spread_moments = []

    def to_owners(unit):
        reduces[unit].finish()
        for k, owner in enumerate(owners):
            if owner.matrix["unit"] == unit:
                owner.gather(moments[unit], window, own_send, own_recv, k)
        spread_moments.append(Direct(place, moments[unit]))

    backward_weight_out(1)
    reduces[OUT1].core()
    backward_out(1)
    reduces[OUT1].plane()
    backward_conv(1)
    backward_hidden(1)
    reduces[OUT1].turn()
    backward_weight_in(1)
    reduces[MID1].core()
    backward_in(1)
    reduces[OUT1].cross()
    backward_weight_out(0)
    reduces[OUT0].core()
    reduces[MID1].plane()
    backward_out(0)
    backward_conv(0)
    reduces[CONV0].core()
    backward_hidden(0)
    reduces[MID1].turn()
    reduces[CONV0].plane()
    backward_weight_in(0)
    backward_in(0)
    reduces[OUT0].plane()
    for m in range(12):
        vec_n[m : m + 1, :] = rows_n[m]
    for m in range(6):
        vec_w[m : m + 1, :] = rows_w[m]
    low_n, low_w = vec_n[...].astype(BF16), vec_w[...].astype(BF16)
    for s in range(OWNERS):
        three = [dot_nt(low_n, put_narrow(s))] + [dot_nt(low_w, put_wide(s, h)) for h in range(2)]
        three.append(jnp.zeros((ROWS - 48, 128), F32))
        store(grads[IN0], IN0, VEC_AT, jnp.concatenate(three, axis=0).astype(BF16), lead=(s,))
    reduces[IN0].core()
    to_owners(OUT1)
    reduces[MID1].cross()
    reduces[CONV0].turn()
    reduces[IN0].plane()
    grad_tokens[...] = wide_grad[...].T
    results[1].start()
    to_owners(MID1)
    reduces[CONV0].cross()
    reduces[OUT0].turn()
    reduces[IN0].turn()
    reduces[OUT0].cross()
    to_owners(CONV0)
    reduces[IN0].cross()
    to_owners(OUT0)
    to_owners(IN0)
    for k, owner in enumerate(owners):
        owner.gather_sent(moments[owner.matrix["unit"]], window, own_send, own_recv, k)
    reduces_used, place.used = place.used, 0
    for gather in spread_moments:
        gather.first()
    for owner in owners:

        @pl.when(owner.here)
        def _(owner=owner):
            owner.gathered(window, own_recv)

    orthogonalize(owners, window, gram, poly, halves)
    for k, owner in enumerate(owners):

        @pl.when(owner.here)
        def _(owner=owner, k=k):
            owner.spread(window, parts[owner.matrix["unit"]], back_send, back_recv, owner.k)

    for gather in spread_moments:
        gather.second()
    spread_updates = []

    def take_updates(unit):
        for k, owner in enumerate(owners):
            if owner.matrix["unit"] == unit:
                owner.arrived(window, parts[unit], back_send, back_recv, owner.k)
        total = parts[unit][0]
        if unit == MID1:
            total = total + parts[unit][1]
        updates[unit][place.y, place.x, place.c] = total
        spread_updates.append(Direct(place, updates[unit]))
        spread_updates[-1].first()

    for unit in (OUT1, OUT0, IN0, MID1, CONV0):
        take_updates(unit)
    for gather in spread_moments:
        gather.last()
    for copy in results[2:7]:
        copy.start()
    for gather in spread_updates:
        gather.second()
    for k, unit in enumerate((OUT1, OUT0, IN0, MID1, CONV0)):
        spread_updates[k].last()
        results[7 + unit].start()
    assert place.used <= gathers_used
    place.sent()
    for copy in results:
        copy.wait()


def run_step(extra, dilation, lengths, params, tokens, cotangent, moments):
    in_smem = pl.BlockSpec(memory_space=pltpu.SMEM)
    anywhere = pl.BlockSpec(memory_space=pltpu.HBM)

    def dma(n):
        return pltpu.SemaphoreType.DMA((n,))

    def pieces(chunk, lead, dtype=BF16):
        return vmem(lead + (2, 2, 2, ROWS, WIDTH[chunk]), dtype)

    shared = [jax.ShapeDtypeStruct((2, 2, 2, ROWS, w), BF16) for w in WIDTH]
    results = [jax.ShapeDtypeStruct((D, TOK), BF16), jax.ShapeDtypeStruct((D, TOK), F32)] + shared + shared
    count = 8 * len(WIDTH) + (10 + len(extra)) * len(WIDTH)
    scratch = [vmem(a.shape, a.dtype) for a in results]
    scratch += [dma(count), dma(count), dma(2 * len(MATRICES)), dma(1), dma(1), dma(len(MATRICES)), dma(24)]
    scratch += [pieces(k, (OWNERS,)) for k in UNITS] * 2
    scratch += [vmem((2 if k == MID1 else 1, ROWS, w), BF16) for k, w in enumerate(WIDTH)]
    for unit in UNITS:
        scratch += reduce_room(unit, extra)
    scratch += [vmem((OWNERS, ROWS, WINDOW), BF16)]
    scratch += [vmem(a.shape, a.dtype) for a in (tokens, cotangent) + tuple(params)]
    scratch += [
        vmem((TOK, TOK), jnp.int32),
        vmem((H, GROUPED), BF16),
        vmem((16, D), F32),
        vmem((16, H), F32),
        vmem((2, D, H), BF16),
        vmem((TOK, D), F32),
        vmem((TOK, D), F32),
        vmem((D, H), F32),
        vmem((K_ENC + 2 * K_DEC - 1, TOK, TOK), BF16),
        vmem((2, TOK, D), BF16),
        vmem((2, TOK, H), BF16),
        vmem((2, 2, TOK, GROUPED), BF16),
        vmem((GROUPED, TOK), BF16),
        vmem((TOK, 2048), BF16),
        vmem((2, TOK, D), BF16),
        vmem((2, TOK, D), BF16),
        vmem((2, TOK, 128), F32),
        vmem((2, 2, TOK, H), BF16),
        vmem((2, 2, TOK, H), BF16),
        vmem((2, 2, TOK, 128), F32),
        vmem((512, 512), F32),
        vmem((512, 512), BF16),
        vmem((2, GROUPED, 512), BF16),
    ]
    return pl.pallas_call(
        functools.partial(step_kernel, extra),
        out_shape=tuple(results),
        in_specs=[in_smem] * 2 + [anywhere] * 12,
        out_specs=(anywhere,) * 12,
        scratch_shapes=scratch,
        compiler_params=pltpu.CompilerParams(
            collective_id=0, has_side_effects=True, vmem_limit_bytes=62 << 20
        ),
        name="step",
    )(dilation, lengths, tokens, cotangent, *params, *moments)


def finish_kernel(
    vector_step, *refs,
):
    in_hbm, out_to_hbm, ins, outs = refs[:17], refs[17:32], refs[32:49], refs[49:62]
    in_sems, out_sems = refs[62:]
    moments, updates = ins[2:7], ins[7:12]
    conv, w_in, w_out, wide, narrow = ins[12:]
    (
        mom_in, mom_conv, mom_out, mom_wide, mom_narrow,
        new_in, new_conv, new_out, new_wide, new_narrow, low_in, low_conv, low_out,
    ) = outs
    arrivals = [pltpu.make_async_copy(s, t, in_sems.at[k]) for k, (s, t) in enumerate(zip(in_hbm, ins))]
    sources = outs + ins[:2]
    targets = out_to_hbm[2:] + out_to_hbm[:2]
    departures = [pltpu.make_async_copy(s, t, out_sems.at[k]) for k, (s, t) in enumerate(zip(sources, targets))]
    arrivals = arrivals[2:] + arrivals[:2]
    for copy in arrivals:
        copy.start()
    rows = slice(0, SHARD)

    def conv_parts(refs):
        enc = load(refs[CONV0], CONV0, 0, 2048, rows=rows).astype(F32)
        dec = load(refs[MID1], MID1, 0, 1280, rows=rows).astype(F32)
        dec = pltpu.roll(dec, SPLIT % 128, 1)
        middle = jnp.where(iota((SHARD, 128), 1) < SPLIT % 128, enc[:, 1920:], dec[:, :128])
        return ((0, enc[:, :1920]), (1920, middle), (2048, dec[:, 128:]))

    def out_lanes(refs, b):
        return load(refs[OUT_AT[b][0]], OUT_AT[b][0], 0, 896, rows=rows).astype(F32)[:, :D]

    def in_lanes(refs, b, h):
        unit, at = IN_AT[b]
        low, high = lane_window(at + H * h, H)
        return unshifted(load(refs[unit], unit, low, high, rows=rows).astype(F32), at + H * h, H)

    for copy in arrivals[:5]:
        copy.wait()
    for low, values in conv_parts(moments):
        mom_conv[:, low : low + values.shape[1]] = values
    departures[1].start()
    for b in range(2):
        mom_out[:, b, :] = out_lanes(moments, b)
        for h in range(2):
            mom_in[b, h * SHARD : (h + 1) * SHARD, :] = in_lanes(moments, b, h)
    departures[0].start()
    departures[2].start()
    for copy in arrivals[15:]:
        copy.wait()
    for copy in departures[13:]:
        copy.start()
    for copy in arrivals[5:15]:
        copy.wait()
    for low, values in conv_parts(updates):
        lanes = slice(low, low + values.shape[1])
        value = conv[:, lanes] - values
        new_conv[:, lanes] = value
        low_conv[:, lanes] = value.astype(BF16)
    departures[6].start()
    departures[11].start()
    for b in range(2):
        value = w_out[:, b, :] - out_lanes(updates, b)
        new_out[:, b, :] = value
        for h in range(2):
            here = slice(h * SHARD, (h + 1) * SHARD)
            value = w_in[b, here, :] - in_lanes(updates, b, h)
            new_in[b, here, :] = value
            low_in[b, here, :] = value.astype(BF16)
    low_out[...] = new_out[...].astype(BF16)
    for k in (5, 7, 10, 12):
        departures[k].start()
    vectors = load(moments[IN0], IN0, VEC_AT, VEC_AT + 128).astype(F32)
    for b in range(2):
        for k in range(6):
            m = 6 * b + k
            value = vectors[m : m + 1, :SHARD]
            mom_narrow[k, b : b + 1, :] = value
            new_narrow[k, b : b + 1, :] = narrow[k, b : b + 1, :] - vector_step * value
        for k in range(3):
            for h in range(2):
                m = 16 + 16 * h + 3 * b + k
                lanes = slice(h * SHARD, (h + 1) * SHARD)
                value = vectors[m : m + 1, :SHARD]
                mom_wide[k, b : b + 1, lanes] = value
                new_wide[k, b : b + 1, lanes] = wide[k, b : b + 1, lanes] - vector_step * value
    for k in (3, 4, 8, 9):
        departures[k].start()
    for copy in departures:
        copy.wait()


def finish(vector_step, shared, params):
    in_hbm = pl.BlockSpec(memory_space=pltpu.HBM)
    conv, w_in, w_out, wide, narrow = params
    shapes = [w_in.shape, conv.shape, w_out.shape, wide.shape, narrow.shape]
    outs = [jax.ShapeDtypeStruct(a.shape, a.dtype) for a in shared[:2]]
    outs += [jax.ShapeDtypeStruct(s, F32) for s in shapes + shapes]
    outs += [jax.ShapeDtypeStruct(s, BF16) for s in shapes[:3]]
    ins = tuple(shared) + tuple(params)
    return pl.pallas_call(
        functools.partial(finish_kernel, vector_step),
        out_shape=tuple(outs),
        in_specs=[in_hbm] * len(ins),
        out_specs=(in_hbm,) * len(outs),
        scratch_shapes=[vmem(a.shape, a.dtype) for a in ins + tuple(outs[2:])]
        + [pltpu.SemaphoreType.DMA((17,)), pltpu.SemaphoreType.DMA((15,))],
        compiler_params=pltpu.CompilerParams(vmem_limit_bytes=62 << 20),
        name="finish",
    )(*ins)


def swap(array):
    return jnp.transpose(array, (1, 0, 2))


def shards(
    extra, vector_step, tokens, cotangent, lengths, dilation, proj_in, conv_weight, proj_out, vec_wide, vec_narrow,
    mom_in, mom_conv, mom_out, mom_wide, mom_narrow,
):
    params = (conv_weight, proj_in, swap(proj_out), swap(vec_wide), swap(vec_narrow))
    moments = (mom_conv, mom_in, swap(mom_out), swap(mom_wide), swap(mom_narrow))
    shared = run_step(extra, dilation, lengths, params, tokens.T, cotangent.T, moments)
    outs = list(finish(vector_step, shared, params))
    for k in (0, 1):
        outs[k] = outs[k].T
    for k in (4, 5, 6, 9, 10, 11, 14):
        outs[k] = swap(outs[k])
    return tuple(outs)


def solution(mesh):
    groups, owners = mesh.shape["dp"], mesh.shape["fsdp"]
    assert owners == OWNERS and groups % PIECES == 0
    extra, bit = [], PIECES
    while bit < groups:
        extra.append(bit)
        bit *= 2
    assert bit == groups
    vector_step = VECTOR_RATE / math.sqrt(TOK * groups * owners)
    tok, rep = P(("dp", "fsdp"), None), P()
    mid, first, final = P(None, "fsdp", None), P("fsdp", None), P(None, None, "fsdp")
    params = (mid, first, mid, final, final)
    return jax.shard_map(
        functools.partial(shards, tuple(extra), vector_step),
        mesh=mesh,
        in_specs=(tok, tok, tok, rep) + params + params,
        out_specs=(tok, tok) + params + params + (mid, first, mid),
        check_vma=False,
    )
```

```python
import functools
import math

import jax
import jax.numpy as jnp
from jax import lax
from jax.experimental import pallas as pl
from jax.experimental.pallas import tpu as pltpu
from jax.sharding import PartitionSpec as P

D = 800
H = 400
K_ENC = 5
K_DEC = 3
NS_STEPS = 5
EPSILON = 1e-05
NORM_FLOOR = 1e-07
COEF_A = 3.4445
COEF_B = -4.775
COEF_C = 2.0315
MOMENT_DECAY = 0.5
MATRIX_RATE = 0.5
VECTOR_RATE = 0.1

F32 = jnp.float32
BF16 = jnp.bfloat16
MESH = pl.DeviceIdType.MESH

OWNERS = 4
PIECES = 8
SHARD = 100
ROWS = 112
IN0, CONV0, OUT0, MID1, OUT1 = range(5)
WIDTH = (128, 256, 128, 256, 128)
UNITS = range(len(WIDTH))
IN_AT = ((IN0, 0), (MID1, 1200))
OUT_AT = ((OUT0, 0), (OUT1, 0))
CONV_AT = ((CONV0, 0), (MID1, 0))
CONV_SPAN = (2048, 1280)
VEC_AT = 896
SPLIT = K_ENC * H
TOK = 256
GROUPED = OWNERS * ROWS
WINDOW = 2048

GELU_K = math.sqrt(2.0 / math.pi)
GELU_C = 0.044715


def vmem(shape, dtype):
    return pltpu.VMEM(shape, dtype)


def dot(a, b):
    return lax.dot_general(a, b, (((1,), (0,)), ((), ())), preferred_element_type=F32)


def dot_nt(a, b):
    return lax.dot_general(a, b, (((1,), (1,)), ((), ())), preferred_element_type=F32)


def dot_tn(a, b):
    return lax.dot_general(a, b, (((0,), (0,)), ((), ())), preferred_element_type=F32)


def one_hot(mask):
    return jnp.where(mask, 1.0, 0.0).astype(BF16)


def iota(shape, dim):
    return lax.broadcasted_iota(jnp.int32, shape, dim)


def add_low(*parts):
    total = parts[0].astype(F32)
    for part in parts[1:]:
        total = total + part.astype(F32)
    return total.astype(BF16)


def spans(chunk, low, high):
    width = WIDTH[chunk]
    for q in range(low // width, -(-high // width)):
        yield q, max(low - q * width, 0), min(high - q * width, width)


def load(ref, chunk, low, high, lead=(), rows=slice(None)):
    parts = []
    for q, start, stop in spans(chunk, low, high):
        parts.append(ref[lead + (q // 4, q // 2 % 2, q % 2, rows, slice(start, stop))])
    return parts[0] if len(parts) == 1 else jnp.concatenate(parts, axis=-1)


def store(ref, chunk, low, value, lead=(), rows=slice(None), add=False):
    at = 0
    for q, start, stop in spans(chunk, low, low + value.shape[-1]):
        index = lead + (q // 4, q // 2 % 2, q % 2, rows, slice(start, stop))
        part = value[..., at : at + stop - start]
        ref[index] = add_low(ref[index], part) if add else part
        at += stop - start


def shifted(values, at, low, high):
    rows, count = values.shape
    base = at - at % 128
    width = -(-(at % 128 + count) // 128) * 128
    parts = []
    if base > low:
        parts.append(jnp.zeros((rows, base - low), F32))
    if width > count:
        values = jnp.concatenate([values, jnp.zeros((rows, width - count), F32)], axis=1)
    parts.append(pltpu.roll(values, at % 128, 1) if at % 128 else values)
    if high > base + width:
        parts.append(jnp.zeros((rows, high - base - width), F32))
    return parts[0] if len(parts) == 1 else jnp.concatenate(parts, axis=1)


def lane_window(at, count):
    return at - at % 128, -(-(at + count) // 128) * 128


def unshifted(values, at, count):
    if at % 128:
        values = pltpu.roll(values, values.shape[1] - at % 128, 1)
    return values[:, :count]


def lay_out(unit, conv, w_in, w_out, wide, narrow, put):
    rows = slice(0, SHARD)
    for b in range(2):
        if unit == CONV_AT[b][0]:
            low, high = (0, SPLIT) if b == 0 else (SPLIT, SPLIT + K_DEC * H)
            start, stop = lane_window(low, high - low)
            stop = min(stop, 3200)
            values = unshifted(conv[:, start:stop], low, high - low)
            put(0, rows, values, False)
        if unit == OUT_AT[b][0]:
            put(0, rows, w_out[:, b, :], False)
        if unit == IN_AT[b][0]:
            at = IN_AT[b][1]
            low, high = lane_window(at, 2 * H)
            values = shifted(w_in[b, :SHARD, :], at, low, high) + shifted(w_in[b, SHARD:, :], at + H, low, high)
            put(low, rows, values, True)
    if unit == IN0:
        for b in range(2):
            for k in range(6):
                m = 6 * b + k
                put(VEC_AT, slice(m, m + 1), narrow[k, b : b + 1, :], False)
            for k in range(3):
                for h in range(2):
                    m = 16 + 16 * h + 3 * b + k
                    put(VEC_AT, slice(m, m + 1), wide[k, b : b + 1, h * SHARD : (h + 1) * SHARD], False)


def flip(value, bit):
    return value + bit - 2 * bit * ((value // bit) % 2)


def other_owner(own, step):
    if step == 0:
        return own
    if step == 3:
        return 3 - own
    return flip(own, step)


def remote(src, dst, send, recv, device):
    return pltpu.make_async_remote_copy(
        src_ref=src,
        dst_ref=dst,
        send_sem=send,
        recv_sem=recv,
        device_id=device,
        device_id_type=MESH,
    )


class Place:
    def __init__(self, send, recv, extra):
        at = lax.axis_index("dp")
        self.piece = at % PIECES
        self.base = at - self.piece
        self.me = at
        self.own = lax.axis_index("fsdp")
        self.y, self.x, self.c = self.piece // 4, self.piece // 2 % 2, self.piece % 2
        self.core, self.near_x, self.near_y = [
            (self.base + flip(self.piece, bit), self.own) for bit in (1, 2, 4)
        ]
        self.near_xy = (self.base + flip(flip(self.piece, 2), 4), self.own)
        self.column = [(at, other_owner(self.own, step)) for step in (1, 2, 3)]
        self.far = [(flip(at, bit), self.own) for bit in extra]
        self.send, self.recv, self.used = send, recv, 0
        self.started = []

    def take(self, count):
        first = self.used
        self.used += count
        return first

    def start(self, src, dst, device):
        k = self.take(1)
        copy = remote(src, dst, self.send.at[k], self.recv.at[k], device)
        copy.start()
        self.started.append(copy)
        return copy

    def sent(self):
        for copy in self.started:
            copy.wait_send()
        self.started = []


class Direct:
    ALL = slice(None)

    def __init__(self, place, ref):
        self.place, self.ref = place, ref

    def first(self):
        p = self.place
        mine = self.ref.at[p.y, p.x, p.c]
        self.copies = [p.start(mine, mine, device) for device in (p.near_x, p.near_y, p.near_xy)]

    def second(self):
        p = self.place
        for copy in self.copies:
            copy.wait_recv()
        pieces = self.ref.at[self.ALL, self.ALL, p.c]
        self.copies = [p.start(pieces, pieces, p.core)]

    def last(self):
        self.copies[0].wait_recv()


class Gather:
    LOW, HIGH, ALL = pl.ds(0, 64), pl.ds(64, 48), slice(None)

    def __init__(self, place, view):
        self.place, self.view = place, view

    def move(self, device, *index):
        ref = self.view(*index)
        return self.place.start(ref, ref, device)

    def first(self):
        p = self.place
        self.a = self.move(p.near_y, p.y, p.x, p.c, self.LOW)
        self.b = self.move(p.near_x, p.y, p.x, p.c, self.HIGH)

    def second(self):
        p = self.place
        self.a.wait_recv()
        self.a = self.move(p.near_x, self.ALL, p.x, p.c, self.LOW)
        self.b.wait_recv()
        self.b = self.move(p.near_y, p.y, self.ALL, p.c, self.HIGH)

    def third(self):
        p = self.place
        self.a.wait_recv()
        self.b.wait_recv()
        self.a = self.move(p.core, self.ALL, self.ALL, p.c, self.ALL)

    def last(self):
        self.a.wait_recv()


class WeightGather(Gather):
    def __init__(self, place, ref, low, width):
        lanes = pl.ds(low, width)

        def view(y, x, c, rows):
            return ref.at[pl.ds(1, 3), y, x, c, rows, lanes]

        super().__init__(place, view)
        self.ref, self.lanes = ref, lanes

    def cross(self):
        p = self.place
        index = (p.y, p.x, p.c, self.ALL, self.lanes)
        mine = self.ref.at[(0,) + index]
        self.crossing = [
            p.start(mine, self.ref.at[(step,) + index], p.column[step - 1]) for step in (1, 2, 3)
        ]

    def first(self, follower=None):
        for copy in self.crossing:
            copy.wait_recv()
        if follower is not None:
            follower.cross()
        super().first()


class Reduce:
    def __init__(self, place, grads, moment, room):
        self.place, self.grads, self.moment = place, grads, moment
        self.from_core, self.sums, self.from_x, self.from_y = room[:4]
        self.last_x, self.last_y, self.from_z, self.from_far = room[4:]

    def core(self):
        p = self.place
        self.halves = []
        for y in (1 - p.y, p.y):
            src = self.grads.at[:, y, :, 1 - p.c]
            self.halves.append((y, p.start(src, self.from_core.at[:, y], p.core)))

    def plane(self):
        p = self.place
        self.a = []
        for k, (y, copy) in enumerate(self.halves):
            copy.wait_recv()
            self.sums[:, y] = add_low(self.grads[:, y, :, p.c], self.from_core[:, y])
            self.a.append(
                p.start(self.sums.at[0:2, y, 1 - p.x], self.from_x.at[:, y], p.near_x)
            )
            if k == 0:
                self.b = p.start(self.sums.at[2:4, y], self.from_y, p.near_y)

    def turn(self):
        p = self.place
        y, x = 1 - p.y, 1 - p.x
        self.a[0].wait_recv()
        self.sums[0:2, y, p.x] = add_low(self.sums[0:2, y, p.x], self.from_x[:, y])
        self.y_last = p.start(self.sums.at[0:2, y, p.x], self.last_y, p.near_y)
        self.b.wait_recv()
        self.sums[2:4, p.y, x] = add_low(self.sums[2:4, p.y, x], self.from_y[:, x])
        self.x_last = p.start(self.sums.at[2:4, p.y, x], self.last_x, p.near_x)

    def cross(self):
        p = self.place
        y, x = p.y, p.x
        self.a[1].wait_recv()
        self.y_last.wait_recv()
        self.sums[0:2, y, x] = add_low(self.sums[0:2, y, x], self.from_x[:, y], self.last_y[...])
        self.x_last.wait_recv()
        self.sums[2:4, y, x] = add_low(self.sums[2:4, y, x], self.from_y[:, x], self.last_x[...])
        for k, device in enumerate(p.far):
            p.start(self.sums.at[:, y, x], self.from_far.at[k], device).wait_recv()
            p.started.pop().wait_send()
            self.sums[:, y, x] = add_low(self.sums[:, y, x], self.from_far[k])
        self.crossing = [
            p.start(self.sums.at[step, y, x], self.from_z.at[step - 1], p.column[step - 1])
            for step in (1, 2, 3)
        ]

    def finish(self):
        p = self.place
        for copy in self.crossing:
            copy.wait_recv()
        parts = [self.sums[0, p.y, p.x]] + [self.from_z[k] for k in range(3)]
        self.moment[p.y, p.x, p.c] = add_low(self.moment[p.y, p.x, p.c], *parts)


def reduce_room(chunk, extra):
    width = WIDTH[chunk]
    shapes = (
        (OWNERS, 2, 2), (OWNERS, 2, 2), (2, 2), (2, 2), (2,), (2,), (3,), (max(len(extra), 1), OWNERS),
    )
    return [vmem(shape + (ROWS, width), BF16) for shape in shapes]


MATRICES = (
    dict(
        kind="row", unit=OUT1, first=0, last=6, piece=5, lanes=(0, D), slot=0, scale=math.sqrt(D / H),
        owners=((0, 0, 2), (3, 2, 2)),
    ),
    dict(
        kind="row", unit=MID1, first=0, last=4, piece=2, lanes=(0, K_DEC * H), slot=0, scale=1.0,
        owners=((0, 0, 2), (3, 2, 2)),
    ),
    dict(
        kind="in", unit=MID1, first=4, last=7, piece=4, lanes=(176, 976), slot=1, scale=1.0,
        owners=((0, 0, 2), (3, 2, 2)),
    ),
    dict(
        kind="row", unit=OUT0, first=0, last=6, piece=3, lanes=(0, D), slot=0, scale=math.sqrt(D / H),
        owners=((1, 0, 2), (2, 2, 2)),
    ),
    dict(
        kind="row", unit=CONV0, first=0, last=7, piece=0, lanes=(0, SPLIT), slot=0, scale=1.0,
        owners=((1, 0, 2), (2, 2, 2)),
    ),
    dict(
        kind="in", unit=IN0, first=0, last=6, piece=6, lanes=(0, D), slot=0, scale=1.0,
        owners=((1, 0, 2), (2, 2, 2)),
    ),
)


class Owner:
    def __init__(self, place, k, owner):
        self.place, self.k = place, k
        matrix = self.matrix = MATRICES[k]
        at, self.first, self.shards = owner
        self.at = at
        self.width = WIDTH[matrix["unit"]]
        self.count = OWNERS * (matrix["last"] - matrix["first"] + 1)
        p = place
        self.here = (p.piece == matrix["piece"]) & (p.own == at)
        self.away = (p.piece != matrix["piece"]) | (p.own != at)
        self.holds = (p.piece >= matrix["first"]) & (p.piece <= matrix["last"])
        self.served = (p.own >= self.first) & (p.own < self.first + self.shards)
        self.device = (p.base + matrix["piece"], at)
    def each_served(self, act):
        def body(k, carry):
            piece = self.matrix["first"] + k // self.shards
            own = self.first + k % self.shards

            @pl.when((piece != self.matrix["piece"]) | (own != self.at))
            def _():
                act(k // self.shards, own, (self.place.base + piece, own))

            return carry

        lax.fori_loop(0, self.count // OWNERS * self.shards, body, 0)

    def lanes(self, k):
        return pl.ds(pl.multiple_of(k * self.width, 128), self.width)

    def to_owner(self, moment, window, send, recv, k):
        p = self.place
        at = p.piece - self.matrix["first"]
        src = moment.at[p.y, p.x, p.c]
        dst = window.at[p.own, :, self.lanes(at)]
        return remote(src, dst, send.at[k], recv.at[0], self.device)

    def gather(self, moment, window, send, recv, k):
        @pl.when(self.holds & self.away)
        def _():
            self.to_owner(moment, window, send, recv, k).start()

        @pl.when(self.here)
        def _():
            p = self.place
            at = p.piece - self.matrix["first"]
            pltpu.make_async_copy(
                moment.at[p.y, p.x, p.c], window.at[p.own, :, self.lanes(at)], recv.at[0]
            ).start()

    def gather_sent(self, moment, window, send, recv, k):
        @pl.when(self.holds & self.away)
        def _():
            self.to_owner(moment, window, send, recv, k).wait_send()

    def whole(self, window, slots, sem):
        values = window.at[slots, :, pl.ds(0, self.count // OWNERS * self.width)]
        return pltpu.make_async_copy(values, values, sem.at[0])

    def gathered(self, window, recv):
        self.whole(window, pl.ds(0, OWNERS), recv).wait()

    def spread(self, window, parts, send, recv, k):
        p = self.place
        slot = parts.at[self.matrix["slot"]]

        def act(at, own, device):
            remote(window.at[own, :, self.lanes(at)], slot, send.at[0], recv.at[k], device).start()

        self.each_served(act)
        if self.first <= self.at < self.first + self.shards:
            at = p.piece - self.matrix["first"]
            pltpu.make_async_copy(window.at[p.own, :, self.lanes(at)], slot, send.at[0]).start()

    def arrived(self, window, parts, send, recv, k):
        @pl.when(self.here)
        def _():
            self.whole(window, pl.ds(self.first, self.shards), send).wait()

        @pl.when(self.holds & self.served & self.away)
        def _():
            src = window.at[0, :, self.lanes(0)]
            dst = parts.at[self.matrix["slot"]]
            remote(src, dst, send.at[0], recv.at[k], self.device).wait_recv()


def split(a):
    high = a.astype(BF16)
    return high, (a - high.astype(F32)).astype(BF16)


def dot_fine(a, b):
    a_high, a_low = split(a)
    b_high, b_low = split(b)
    return dot(a_high, b_high) + (dot(a_high, b_low) + dot(a_low, b_high))


def dot_low(a, b):
    return dot(a.astype(BF16), b.astype(BF16))


def polynomial_of(gram):
    size = gram.shape[0]
    eye = iota((size, size), 0) == iota((size, size), 1)
    unit = jnp.where(eye, 1.0, 0.0)
    power = jnp.sum(jnp.sum(jnp.where(eye, gram, 0.0), axis=1, keepdims=True), axis=0, keepdims=True)
    inverse = 1.0 / (jnp.sqrt(power) + NORM_FLOOR)
    current = gram * inverse * inverse
    result = None
    for step in range(NS_STEPS):
        square = dot_fine if step == 3 else dot_low
        poly = COEF_A * unit + COEF_B * current + COEF_C * square(current, current)
        result = poly if result is None else dot_low(poly, result)
        if step < NS_STEPS - 1:
            first = dot_fine if step < 2 else dot_low
            second = dot_fine if step < 1 else dot_low
            current = second(first(poly, current), poly)
    return result, inverse


def orthogonalize(owners, window, gram, poly, halves):
    is_row = False
    high, factor, parts = jnp.int32(0), jnp.float32(0), jnp.int32(0)
    low_half, high_half = jnp.int32(0), jnp.int32(0)
    for owner in owners:
        matrix, here = owner.matrix, owner.here
        if matrix["kind"] == "row":
            is_row = is_row | here
        high = jnp.where(here, matrix["lanes"][1], high)
        parts = jnp.where(here, -(-matrix["lanes"][1] // 512), parts)
        factor = jnp.where(here, MATRIX_RATE * matrix["scale"], factor)
        low_half = jnp.where(here, owner.first // 2, low_half)
        high_half = jnp.where(here, (owner.first + owner.shards) // 2, high_half)
    ins = {}
    for owner in owners:
        if owner.matrix["kind"] == "in":
            at = owner.matrix["lanes"][0]
            ins[at] = ins.get(at, False) | owner.here
    is_in = False
    for here in ins.values():
        is_in = is_in | here

    def part(k):
        lanes = pl.ds(pl.multiple_of(k * 512, 512), 512)
        values = window[:, :, lanes].reshape(GROUPED, 512)
        lane = iota((GROUPED, 512), 1) + k * 512
        return lanes, jnp.where(lane < high, values, jnp.zeros((), BF16))

    for at, here in ins.items():

        @pl.when(here)
        def _(at=at):
            valid = iota((GROUPED, 512), 1) < H
            for h in range(2):
                low = (at + H * h) // 128 * 128
                values = window[:, :, low : low + 512].reshape(GROUPED, 512).astype(F32)
                if (at + H * h) % 128:
                    values = pltpu.roll(values, 512 - (at + H * h) % 128, 1)
                halves[h] = jnp.where(valid, values, 0.0).astype(BF16)

    @pl.when(is_in)
    def _():
        gram[...] = dot_tn(halves[0], halves[0]) + dot_tn(halves[1], halves[1])

    @pl.when(is_row)
    def _():
        gram[...] = jnp.zeros(gram.shape, F32)

        def body(k, carry):
            values = part(k)[1]
            gram[:GROUPED, :GROUPED] += dot_nt(values, values)
            return carry

        lax.fori_loop(0, parts, body, 0)

    @pl.when(is_in | is_row)
    def _():
        result, inverse = polynomial_of(gram[...])
        poly[...] = (result * (inverse * factor)).astype(BF16)

    for at, here in ins.items():

        @pl.when(here)
        def _(at=at):
            window[:, :, :1024] = jnp.zeros((OWNERS, ROWS, 1024), BF16)

            def body(two_at, carry):
                two, served = pl.ds(2 * two_at, 2), pl.ds(pl.multiple_of(2 * ROWS * two_at, 2 * ROWS), 2 * ROWS)
                for h in range(2):
                    low = (at + H * h) // 128 * 128
                    step = dot_nt(halves[h, served], poly[...])
                    if (at + H * h) % 128:
                        step = pltpu.roll(step, (at + H * h) % 128, 1)
                    lanes = slice(low, low + 512)
                    window[two, :, lanes] = add_low(window[two, :, lanes], step.reshape(2, ROWS, 512))
                return carry

            lax.fori_loop(low_half, high_half, body, 0)

    @pl.when(is_row)
    def _():
        def body(k, carry):
            lanes, values = part(k)

            def half(two_at, carry):
                two, served = pl.ds(2 * two_at, 2), pl.ds(pl.multiple_of(2 * ROWS * two_at, 2 * ROWS), 2 * ROWS)
                step = dot(poly[served, :GROUPED], values)
                window[two, :, lanes] = step.astype(BF16).reshape(2, ROWS, 512)
                return carry

            lax.fori_loop(low_half, high_half, half, 0)
            return carry

        lax.fori_loop(0, parts, body, 0)


def norm_forward(src, width, gain, shift, act, unit, slope, spread, chunk=256):
    def body(k, carry):
        rows = pl.ds(pl.multiple_of(k * chunk, chunk), chunk)
        x = src[rows, :width].astype(F32)
        center = x - jnp.mean(x, axis=1, keepdims=True)
        scale = lax.rsqrt(jnp.mean(center * center, axis=1, keepdims=True) + EPSILON)
        xhat = center * scale
        a = xhat * gain + shift
        square = a * a
        half = 0.5 + 0.5 * jnp.tanh(a * (GELU_K + (GELU_K * GELU_C) * square))
        act[rows, :width] = (a * half).astype(BF16)
        unit[rows, :width] = xhat.astype(BF16)
        inner = GELU_K + (3.0 * GELU_K * GELU_C) * square
        slope[rows, :width] = (half + (2.0 * a * inner) * (half * (1.0 - half))).astype(BF16)
        spread[rows, :] = jnp.broadcast_to(scale, (chunk, 128))
        return carry

    lax.fori_loop(0, TOK // chunk, body, 0)


def fold_rows(values):
    total = values[0:8]
    for k in range(1, values.shape[0] // 8):
        total = total + values[8 * k : 8 * k + 8]
    return total


def norm_backward(grad, width, gain, unit, slope, spread, finish, chunk=256):
    def body(k, sums):
        rows = pl.ds(pl.multiple_of(k * chunk, chunk), chunk)
        da = grad[rows, :width] * slope[rows, :width].astype(F32)
        xhat = unit[rows, :width].astype(F32)
        product = da * xhat
        dxhat = da * gain
        mean_one = jnp.mean(dxhat, axis=1, keepdims=True)
        mean_two = jnp.mean(dxhat * xhat, axis=1, keepdims=True)
        dx = spread[rows, 0:1] * (dxhat - mean_one - xhat * mean_two)
        finish(rows, dx)
        return (sums[0] + fold_rows(product), sums[1] + fold_rows(da), sums[2] + fold_rows(dx))

    zero = jnp.zeros((8, width), F32)
    sums = lax.fori_loop(0, TOK // chunk, body, (zero, zero, zero))
    return tuple(jnp.sum(s, axis=0, keepdims=True) for s in sums)


def step_kernel(
    extra,
    dilation, lengths, tokens_hbm, cotangent_hbm,
    conv_hbm, in_hbm, out_hbm, wide_hbm, narrow_hbm,
    mom_conv_hbm, mom_in_hbm, mom_out_hbm, mom_wide_hbm, mom_narrow_hbm,
    *refs,
):
    results = refs[:12]
    refs = refs[12:]
    out, grad_tokens, moments, updates = refs[0], refs[1], refs[2:7], refs[7:12]
    refs = refs[2:]
    send, recv, own_send, own_recv, back_send, back_recv, local = refs[10:17]
    full, grads, parts = refs[17:22], refs[22:27], refs[27:32]
    rooms = refs[32:72]
    (
        window,
        tokens, cotangent, conv, in_shard, out_shard, wide_shard, narrow_shard,
        far, perm_h, vec_w, vec_n, w_in, x_one, wide_grad, tall,
        masks, act_d, act_h, act_g, act_t, e_all,
        unit_d, slope_d, spread_d, unit_h, slope_h, spread_h,
        gram, poly, halves,
    ) = refs[72:]
    place = Place(send, recv, extra)
    own = place.own
    owners = [Owner(place, k, owner) for k, matrix in enumerate(MATRICES) for owner in matrix["owners"]]
    conv_in, spare = gram.at[:TOK], gram.at[TOK:]
    hid = spare

    results = [
        pltpu.make_async_copy(source, target, local.at[12 + k])
        for k, (source, target) in enumerate(zip((out, grad_tokens) + moments + updates, results))
    ]

    sources = (conv_hbm, in_hbm, out_hbm, wide_hbm, narrow_hbm, tokens_hbm, cotangent_hbm)
    shard = (conv, in_shard, out_shard, wide_shard, narrow_shard)
    targets = shard + (tokens, cotangent)
    fetches = [pltpu.make_async_copy(s, t, local.at[k]) for k, (s, t) in enumerate(zip(sources, targets))]
    for fetch in fetches:
        fetch.start()
    barrier = pltpu.get_barrier_semaphore()
    for device in [place.core, place.near_x, place.near_y] + place.column + place.far:
        pl.semaphore_signal(barrier, inc=1, device_id=device, device_id_type=MESH)

    def pack(unit):
        full[unit][0] = jnp.zeros(full[unit].shape[1:], BF16)

        def put(low, rows, values, add):
            store(full[unit], unit, low, values.astype(BF16), lead=(0,), rows=rows, add=add)

        lay_out(unit, *shard, put)

    in_unit = WeightGather(place, full[IN0], 0, 128)
    conv_unit = WeightGather(place, full[CONV0], 0, 256)
    out_unit = WeightGather(place, full[OUT0], 0, 128)
    mid_unit = WeightGather(place, full[MID1], 0, 256)
    last_unit = WeightGather(place, full[OUT1], 0, 128)

    for k in (1, 3, 4):
        fetches[k].wait()
    pack(IN0)
    pl.semaphore_wait(barrier, 6 + len(extra))
    in_unit.cross()
    fetches[0].wait()
    pack(CONV0)
    conv_unit.cross()
    fetches[2].wait()
    for unit in (OUT0, MID1, OUT1):
        pack(unit)
    sources = (mom_conv_hbm, mom_in_hbm, mom_out_hbm, mom_wide_hbm, mom_narrow_hbm)
    moment_fetches = [pltpu.make_async_copy(s, t, local.at[7 + k]) for k, (s, t) in enumerate(zip(sources, shard))]
    for fetch in moment_fetches:
        fetch.start()

    row, col = iota((TOK, TOK), 0), iota((TOK, TOK), 1)
    seg_row, seg_col = jnp.zeros((TOK, TOK), jnp.int32), jnp.zeros((TOK, TOK), jnp.int32)
    end = jnp.int32(0)
    for k in range(8):
        end = end + lengths[0, k]
        seg_row = seg_row + jnp.where(row >= end, 1, 0)
        seg_col = seg_col + jnp.where(col >= end, 1, 0)
    far[...] = jnp.where(seg_row == seg_col, col - row, 4 * TOK)

    enc_shifts = [(j - K_ENC // 2) * dilation[0] for j in range(K_ENC)]
    dec_shifts = [j * dilation[1] for j in range(1 - K_DEC, K_DEC)]
    for k, shift in enumerate(enc_shifts + dec_shifts):
        masks[k] = one_hot(far[...] == shift)
    tap_masks = (
        [(j, K_ENC - 1 - j) for j in range(K_ENC)],
        [(K_ENC + K_DEC - 1 - j, K_ENC + K_DEC - 1 + j) for j in range(K_DEC)],
    )

    for fetch in moment_fetches:
        fetch.wait()
    for unit in UNITS:
        moments[unit][...] = jnp.zeros(moments[unit].shape, BF16)

        def put_moment(low, rows, values, add, unit=unit):
            store(moments[unit], unit, low, (MOMENT_DECAY * values).astype(BF16), rows=rows, add=add)

        lay_out(unit, *shard, put_moment)
        parts[unit][...] = jnp.zeros(parts[unit].shape, BF16)

    in_unit.first(out_unit)
    conv_unit.first(mid_unit)
    row, col = iota((H, GROUPED), 0), iota((H, GROUPED), 1)
    used = jnp.zeros((H, GROUPED), jnp.int32)
    for s in range(OWNERS):
        r = col - ROWS * s
        inside = (r >= 0) & (r < SHARD) & (row == r + SHARD * other_owner(own, s))
        used = used + jnp.where(inside, 1, 0)
    perm_h[...] = used.astype(F32).astype(BF16)
    in_unit.second()
    out_unit.first(last_unit)
    fetches[5].wait()
    x_one[...] = tokens[...].astype(F32).T
    conv_unit.second()
    in_unit.third()
    fetches[6].wait()
    wide_grad[...] = cotangent[...].astype(F32).T
    mid_unit.first()
    out_unit.second()
    conv_unit.third()
    in_unit.last()

    row_n, col_n = iota((128, H), 0), iota((128, H), 1)
    row_w, col_w = iota((128, D), 0), iota((128, D), 1)

    def put_narrow(s):
        return one_hot((col_n == row_n + SHARD * other_owner(own, s)) & (row_n < SHARD))

    def put_wide(s, h):
        return one_hot((col_w == row_w + SHARD * (2 * other_owner(own, s) + h)) & (row_w < SHARD))

    total_n, total_w = jnp.zeros((16, H), F32), jnp.zeros((16, D), F32)
    for s in range(OWNERS):
        vectors = load(full[IN0], IN0, VEC_AT, VEC_AT + 128, lead=(s,))
        total_n = total_n + dot(vectors[0:16], put_narrow(s))
        for h in range(2):
            total_w = total_w + dot(vectors[16 + 16 * h : 32 + 16 * h], put_wide(s, h))
    vec_n[...] = total_n
    vec_w[...] = total_w

    def narrow(b, k):
        return vec_n[6 * b + k : 6 * b + k + 1, :]

    def wide(b, k):
        return vec_w[3 * b + k : 3 * b + k + 1, :]

    def weights(unit, low, high):
        return load(full[unit], unit, low, high, lead=(slice(None),)).reshape(GROUPED, high - low)

    def weight_out(b):
        return weights(OUT_AT[b][0], 0, 896)[:, :D]

    def place_in(b):
        unit, at = IN_AT[b]
        for i in range(OWNERS):
            slot = other_owner(own, i)
            for h in range(2):
                low, high = lane_window(at + H * h, H)
                values = load(full[unit], unit, low, high, lead=(slot,)).astype(F32)[:SHARD]
                row_at = SHARD * (2 * i + h)
                tall[row_at : row_at + SHARD, :] = unshifted(values, at + H * h, H)
        w_in[b] = tall[...].astype(BF16)

    def taps(b):
        return [(H * j, forward, backward) for j, (forward, backward) in enumerate(tap_masks[b])]

    def forward_in(b):
        norm_forward(x_one, D, wide(b, 0), wide(b, 1), act_d.at[b], unit_d.at[b], slope_d.at[b], spread_d.at[b])
        place_in(b)
        hid[:, :H] = dot(act_d[b], w_in[b]) + narrow(b, 0)
        norm_forward(
            hid, H, narrow(b, 1), narrow(b, 2), act_h.at[0], unit_h.at[b, 0], slope_h.at[b, 0], spread_h.at[b, 0]
        )
        act_g[b, 0] = dot(act_h[0], perm_h[...]).astype(BF16)

    def forward_conv(b):
        for j, (at, mask, unused) in enumerate(taps(b)):
            moved = dot(masks[mask], act_g[b, 0]).astype(BF16)
            low = at - at % 128
            product = dot(moved, weights(CONV_AT[b][0], low, low + 512))
            if at % 128:
                product = pltpu.roll(product, 512 - at % 128, 1)
            if j == 0:
                conv_in[...] = product
            else:
                conv_in[...] += product
        conv_in[:, :H] += narrow(b, 3)

    def forward_out(b):
        norm_forward(
            conv_in, H, narrow(b, 4), narrow(b, 5), act_h.at[1], unit_h.at[b, 1], slope_h.at[b, 1], spread_h.at[b, 1]
        )
        act_g[b, 1] = dot(act_h[1], perm_h[...]).astype(BF16)
        return (x_one[...] + dot(act_g[b, 1], weight_out(b))) + wide(b, 2)

    forward_in(0)
    last_unit.first()
    mid_unit.second()
    out_unit.third()
    conv_unit.last()
    forward_conv(0)
    last_unit.second()
    mid_unit.third()
    out_unit.last()
    x_one[...] = forward_out(0)
    last_unit.third()

    mid_unit.last()
    forward_in(1)
    forward_conv(1)
    last_unit.last()
    out[...] = forward_out(1).T.astype(BF16)
    results[0].start()
    place.sent()
    gathers_used = place.used

    reduces = [Reduce(place, grads[k], moments[k], rooms[8 * k : 8 * k + 8]) for k in UNITS]
    grouped = (slice(None),)

    def put_grads(unit, low, values, add=False):
        store(grads[unit], unit, low, values.reshape(OWNERS, ROWS, values.shape[-1]), lead=grouped, add=add)

    rows_w, rows_n = [None] * 6, [None] * 12

    def keep_low(rows, dx):
        act_h[0, rows, :] = dx.astype(BF16)

    def backward_weight_out(b):
        rows_w[3 * b + 2] = jnp.sum(wide_grad[...], axis=0, keepdims=True)
        product = dot_tn(act_g[b, 1], wide_grad[...].astype(BF16)).astype(BF16)
        put_grads(OUT_AT[b][0], 0, jnp.concatenate([product, jnp.zeros((GROUPED, 1024 - D), BF16)], axis=1))

    def backward_out(b):
        back = dot_nt(wide_grad[...].astype(BF16), weight_out(b)).astype(BF16)
        spare[:, :H] = dot_nt(back, perm_h[...])
        sums = norm_backward(
            spare, H, narrow(b, 4), unit_h.at[b, 1], slope_h.at[b, 1], spread_h.at[b, 1], keep_low
        )
        rows_n[6 * b + 4], rows_n[6 * b + 5], rows_n[6 * b + 3] = sums

    def backward_conv(b):
        span = CONV_SPAN[b]
        e_all[:, :span] = jnp.zeros((TOK, span), BF16)
        for at, unused, mask in taps(b):
            moved = dot(masks[mask], act_h[0])
            moved = jnp.concatenate([moved, jnp.zeros((TOK, 512 - H), F32)], axis=1)
            if at % 128:
                moved = pltpu.roll(moved, at % 128, 1)
            low = at - at % 128
            e_all[:, low : low + 512] += moved.astype(BF16)
        act_t[...] = act_g[b, 0].T
        for low in range(0, span, 512):
            high = min(low + 512, span)
            put_grads(CONV_AT[b][0], low, dot(act_t[...], e_all[:, low:high]).astype(BF16))

    def backward_hidden(b):
        span = CONV_SPAN[b]
        back = None
        for low in range(0, span, 512):
            high = min(low + 512, span)
            part = dot_nt(e_all[:, low:high], weights(CONV_AT[b][0], low, high))
            back = part if back is None else back + part
        spare[:, :H] = dot_nt(back.astype(BF16), perm_h[...])
        sums = norm_backward(
            spare, H, narrow(b, 1), unit_h.at[b, 0], slope_h.at[b, 0], spread_h.at[b, 0], keep_low
        )
        rows_n[6 * b + 1], rows_n[6 * b + 2], rows_n[6 * b + 0] = sums

    def backward_weight_in(b):
        unit, at = IN_AT[b]
        tall[...] = dot_tn(act_d[b], act_h[0])
        low, high = lane_window(at, 2 * H)
        spare_rows = slice(SHARD, ROWS)
        if at % 128:
            rest = jnp.zeros((OWNERS, ROWS - SHARD, high - low - 128), BF16)
            store(grads[unit], unit, low + 128, rest, lead=grouped, rows=spare_rows)
        else:
            rest = jnp.zeros((OWNERS, ROWS - SHARD, high - low), BF16)
            store(grads[unit], unit, low, rest, lead=grouped, rows=spare_rows)
        for i in range(OWNERS):
            slot = other_owner(own, i)
            first = tall[2 * SHARD * i : 2 * SHARD * i + SHARD, :]
            second = tall[2 * SHARD * i + SHARD : 2 * SHARD * (i + 1), :]
            whole = shifted(first, at, low, high) + shifted(second, at + H, low, high)
            where = dict(lead=(slot,), rows=slice(0, SHARD))
            if at % 128:
                store(grads[unit], unit, low, whole[:, :128], add=True, **where)
                store(grads[unit], unit, low + 128, whole[:, 128:].astype(BF16), **where)
            else:
                store(grads[unit], unit, low, whole.astype(BF16), **where)

    def backward_in(b):
        x_one[...] = dot_nt(act_h[0], w_in[b])

        def add_up(rows, dx):
            wide_grad[rows, :] += dx

        sums = norm_backward(
            x_one, D, wide(b, 0), unit_d.at[b], slope_d.at[b], spread_d.at[b], add_up
        )
        rows_w[3 * b + 0], rows_w[3 * b + 1] = sums[0], sums[1]

    spread_moments = []

    def to_owners(unit):
        reduces[unit].finish()
        for k, owner in enumerate(owners):
            if owner.matrix["unit"] == unit:
                owner.gather(moments[unit], window, own_send, own_recv, k)
        spread_moments.append(Direct(place, moments[unit]))

    backward_weight_out(1)
    reduces[OUT1].core()
    backward_out(1)
    reduces[OUT1].plane()
    backward_conv(1)
    backward_hidden(1)
    reduces[OUT1].turn()
    backward_weight_in(1)
    reduces[MID1].core()
    backward_in(1)
    reduces[OUT1].cross()
    backward_weight_out(0)
    reduces[OUT0].core()
    reduces[MID1].plane()
    backward_out(0)
    backward_conv(0)
    reduces[CONV0].core()
    backward_hidden(0)
    reduces[MID1].turn()
    reduces[CONV0].plane()
    backward_weight_in(0)
    backward_in(0)
    reduces[OUT0].plane()
    for m in range(12):
        vec_n[m : m + 1, :] = rows_n[m]
    for m in range(6):
        vec_w[m : m + 1, :] = rows_w[m]
    low_n, low_w = vec_n[...].astype(BF16), vec_w[...].astype(BF16)
    for s in range(OWNERS):
        three = [dot_nt(low_n, put_narrow(s))] + [dot_nt(low_w, put_wide(s, h)) for h in range(2)]
        three.append(jnp.zeros((ROWS - 48, 128), F32))
        store(grads[IN0], IN0, VEC_AT, jnp.concatenate(three, axis=0).astype(BF16), lead=(s,))
    reduces[IN0].core()
    to_owners(OUT1)
    reduces[MID1].cross()
    reduces[CONV0].turn()
    reduces[IN0].plane()
    grad_tokens[...] = wide_grad[...].T
    results[1].start()
    to_owners(MID1)
    reduces[CONV0].cross()
    reduces[OUT0].turn()
    reduces[IN0].turn()
    reduces[OUT0].cross()
    to_owners(CONV0)
    reduces[IN0].cross()
    to_owners(OUT0)
    to_owners(IN0)
    for k, owner in enumerate(owners):
        owner.gather_sent(moments[owner.matrix["unit"]], window, own_send, own_recv, k)
    reduces_used, place.used = place.used, 0
    for gather in spread_moments:
        gather.first()
    for owner in owners:

        @pl.when(owner.here)
        def _(owner=owner):
            owner.gathered(window, own_recv)

    orthogonalize(owners, window, gram, poly, halves)
    for k, owner in enumerate(owners):

        @pl.when(owner.here)
        def _(owner=owner, k=k):
            owner.spread(window, parts[owner.matrix["unit"]], back_send, back_recv, owner.k)

    for gather in spread_moments:
        gather.second()
    spread_updates = []

    def take_updates(unit):
        for k, owner in enumerate(owners):
            if owner.matrix["unit"] == unit:
                owner.arrived(window, parts[unit], back_send, back_recv, owner.k)
        total = parts[unit][0]
        if unit == MID1:
            total = total + parts[unit][1]
        updates[unit][place.y, place.x, place.c] = total
        spread_updates.append(Direct(place, updates[unit]))
        spread_updates[-1].first()

    for unit in (OUT1, OUT0, IN0, MID1, CONV0):
        take_updates(unit)
    for gather in spread_moments:
        gather.last()
    for copy in results[2:7]:
        copy.start()
    for gather in spread_updates:
        gather.second()
    for k, unit in enumerate((OUT1, OUT0, IN0, MID1, CONV0)):
        spread_updates[k].last()
        results[7 + unit].start()
    assert place.used <= gathers_used
    place.sent()
    for copy in results:
        copy.wait()


def run_step(extra, dilation, lengths, params, tokens, cotangent, moments):
    in_smem = pl.BlockSpec(memory_space=pltpu.SMEM)
    anywhere = pl.BlockSpec(memory_space=pltpu.HBM)

    def dma(n):
        return pltpu.SemaphoreType.DMA((n,))

    def pieces(chunk, lead, dtype=BF16):
        return vmem(lead + (2, 2, 2, ROWS, WIDTH[chunk]), dtype)

    shared = [jax.ShapeDtypeStruct((2, 2, 2, ROWS, w), BF16) for w in WIDTH]
    results = [jax.ShapeDtypeStruct((D, TOK), BF16), jax.ShapeDtypeStruct((D, TOK), F32)] + shared + shared
    count = 8 * len(WIDTH) + (10 + len(extra)) * len(WIDTH)
    scratch = [vmem(a.shape, a.dtype) for a in results]
    scratch += [dma(count), dma(count), dma(2 * len(MATRICES)), dma(1), dma(1), dma(len(MATRICES)), dma(24)]
    scratch += [pieces(k, (OWNERS,)) for k in UNITS] * 2
    scratch += [vmem((2 if k == MID1 else 1, ROWS, w), BF16) for k, w in enumerate(WIDTH)]
    for unit in UNITS:
        scratch += reduce_room(unit, extra)
    scratch += [vmem((OWNERS, ROWS, WINDOW), BF16)]
    scratch += [vmem(a.shape, a.dtype) for a in (tokens, cotangent) + tuple(params)]
    scratch += [
        vmem((TOK, TOK), jnp.int32),
        vmem((H, GROUPED), BF16),
        vmem((16, D), F32),
        vmem((16, H), F32),
        vmem((2, D, H), BF16),
        vmem((TOK, D), F32),
        vmem((TOK, D), F32),
        vmem((D, H), F32),
        vmem((K_ENC + 2 * K_DEC - 1, TOK, TOK), BF16),
        vmem((2, TOK, D), BF16),
        vmem((2, TOK, H), BF16),
        vmem((2, 2, TOK, GROUPED), BF16),
        vmem((GROUPED, TOK), BF16),
        vmem((TOK, 2048), BF16),
        vmem((2, TOK, D), BF16),
        vmem((2, TOK, D), BF16),
        vmem((2, TOK, 128), F32),
        vmem((2, 2, TOK, H), BF16),
        vmem((2, 2, TOK, H), BF16),
        vmem((2, 2, TOK, 128), F32),
        vmem((512, 512), F32),
        vmem((512, 512), BF16),
        vmem((2, GROUPED, 512), BF16),
    ]
    return pl.pallas_call(
        functools.partial(step_kernel, extra),
        out_shape=tuple(results),
        in_specs=[in_smem] * 2 + [anywhere] * 12,
        out_specs=(anywhere,) * 12,
        scratch_shapes=scratch,
        compiler_params=pltpu.CompilerParams(
            collective_id=0, has_side_effects=True, vmem_limit_bytes=62 << 20
        ),
        name="step",
    )(dilation, lengths, tokens, cotangent, *params, *moments)


def finish_kernel(
    vector_step, *refs,
):
    in_hbm, out_to_hbm, ins, outs = refs[:17], refs[17:32], refs[32:49], refs[49:62]
    in_sems, out_sems = refs[62:]
    moments, updates = ins[2:7], ins[7:12]
    conv, w_in, w_out, wide, narrow = ins[12:]
    (
        mom_in, mom_conv, mom_out, mom_wide, mom_narrow,
        new_in, new_conv, new_out, new_wide, new_narrow, low_in, low_conv, low_out,
    ) = outs
    arrivals = [pltpu.make_async_copy(s, t, in_sems.at[k]) for k, (s, t) in enumerate(zip(in_hbm, ins))]
    sources = outs + ins[:2]
    targets = out_to_hbm[2:] + out_to_hbm[:2]
    departures = [pltpu.make_async_copy(s, t, out_sems.at[k]) for k, (s, t) in enumerate(zip(sources, targets))]
    arrivals = arrivals[2:] + arrivals[:2]
    for copy in arrivals:
        copy.start()
    rows = slice(0, SHARD)

    def conv_parts(refs):
        enc = load(refs[CONV0], CONV0, 0, 2048, rows=rows).astype(F32)
        dec = load(refs[MID1], MID1, 0, 1280, rows=rows).astype(F32)
        dec = pltpu.roll(dec, SPLIT % 128, 1)
        middle = jnp.where(iota((SHARD, 128), 1) < SPLIT % 128, enc[:, 1920:], dec[:, :128])
        return ((0, enc[:, :1920]), (1920, middle), (2048, dec[:, 128:]))

    def out_lanes(refs, b):
        return load(refs[OUT_AT[b][0]], OUT_AT[b][0], 0, 896, rows=rows).astype(F32)[:, :D]

    def in_lanes(refs, b, h):
        unit, at = IN_AT[b]
        low, high = lane_window(at + H * h, H)
        return unshifted(load(refs[unit], unit, low, high, rows=rows).astype(F32), at + H * h, H)

    for copy in arrivals[:5]:
        copy.wait()
    for low, values in conv_parts(moments):
        mom_conv[:, low : low + values.shape[1]] = values
    departures[1].start()
    for b in range(2):
        mom_out[:, b, :] = out_lanes(moments, b)
        for h in range(2):
            mom_in[b, h * SHARD : (h + 1) * SHARD, :] = in_lanes(moments, b, h)
    departures[0].start()
    departures[2].start()
    for copy in arrivals[15:]:
        copy.wait()
    for copy in departures[13:]:
        copy.start()
    for copy in arrivals[5:15]:
        copy.wait()
    for low, values in conv_parts(updates):
        lanes = slice(low, low + values.shape[1])
        value = conv[:, lanes] - values
        new_conv[:, lanes] = value
        low_conv[:, lanes] = value.astype(BF16)
    departures[6].start()
    departures[11].start()
    for b in range(2):
        value = w_out[:, b, :] - out_lanes(updates, b)
        new_out[:, b, :] = value
        for h in range(2):
            here = slice(h * SHARD, (h + 1) * SHARD)
            value = w_in[b, here, :] - in_lanes(updates, b, h)
            new_in[b, here, :] = value
            low_in[b, here, :] = value.astype(BF16)
    low_out[...] = new_out[...].astype(BF16)
    for k in (5, 7, 10, 12):
        departures[k].start()
    vectors = load(moments[IN0], IN0, VEC_AT, VEC_AT + 128).astype(F32)
    for b in range(2):
        for k in range(6):
            m = 6 * b + k
            value = vectors[m : m + 1, :SHARD]
            mom_narrow[k, b : b + 1, :] = value
            new_narrow[k, b : b + 1, :] = narrow[k, b : b + 1, :] - vector_step * value
        for k in range(3):
            for h in range(2):
                m = 16 + 16 * h + 3 * b + k
                lanes = slice(h * SHARD, (h + 1) * SHARD)
                value = vectors[m : m + 1, :SHARD]
                mom_wide[k, b : b + 1, lanes] = value
                new_wide[k, b : b + 1, lanes] = wide[k, b : b + 1, lanes] - vector_step * value
    for k in (3, 4, 8, 9):
        departures[k].start()
    for copy in departures:
        copy.wait()


def finish(vector_step, shared, params):
    in_hbm = pl.BlockSpec(memory_space=pltpu.HBM)
    conv, w_in, w_out, wide, narrow = params
    shapes = [w_in.shape, conv.shape, w_out.shape, wide.shape, narrow.shape]
    outs = [jax.ShapeDtypeStruct(a.shape, a.dtype) for a in shared[:2]]
    outs += [jax.ShapeDtypeStruct(s, F32) for s in shapes + shapes]
    outs += [jax.ShapeDtypeStruct(s, BF16) for s in shapes[:3]]
    ins = tuple(shared) + tuple(params)
    return pl.pallas_call(
        functools.partial(finish_kernel, vector_step),
        out_shape=tuple(outs),
        in_specs=[in_hbm] * len(ins),
        out_specs=(in_hbm,) * len(outs),
        scratch_shapes=[vmem(a.shape, a.dtype) for a in ins + tuple(outs[2:])]
        + [pltpu.SemaphoreType.DMA((17,)), pltpu.SemaphoreType.DMA((15,))],
        compiler_params=pltpu.CompilerParams(vmem_limit_bytes=62 << 20),
        name="finish",
    )(*ins)


def swap(array):
    return jnp.transpose(array, (1, 0, 2))


def shards(
    extra, vector_step, tokens, cotangent, lengths, dilation, proj_in, conv_weight, proj_out, vec_wide, vec_narrow,
    mom_in, mom_conv, mom_out, mom_wide, mom_narrow,
):
    params = (conv_weight, proj_in, swap(proj_out), swap(vec_wide), swap(vec_narrow))
    moments = (mom_conv, mom_in, swap(mom_out), swap(mom_wide), swap(mom_narrow))
    shared = run_step(extra, dilation, lengths, params, tokens.T, cotangent.T, moments)
    outs = list(finish(vector_step, shared, params))
    for k in (0, 1):
        outs[k] = outs[k].T
    for k in (4, 5, 6, 9, 10, 11, 14):
        outs[k] = swap(outs[k])
    return tuple(outs)


def solution(mesh):
    groups, owners = mesh.shape["dp"], mesh.shape["fsdp"]
    assert owners == OWNERS and groups % PIECES == 0
    extra, bit = [], PIECES
    while bit < groups:
        extra.append(bit)
        bit *= 2
    assert bit == groups
    vector_step = VECTOR_RATE / math.sqrt(TOK * groups * owners)
    tok, rep = P(("dp", "fsdp"), None), P()
    mid, first, final = P(None, "fsdp", None), P("fsdp", None), P(None, None, "fsdp")
    params = (mid, first, mid, final, final)
    return jax.shard_map(
        functools.partial(shards, tuple(extra), vector_step),
        mesh=mesh,
        in_specs=(tok, tok, tok, rep) + params + params,
        out_specs=(tok, tok) + params + params + (mid, first, mid),
        check_vma=False,
    )
```
